32 devices in a mesh: dp: 8 (over z, y), tower: 4 (over x, core).
Axes of the slice: x: 2, y: 2, z: 4, core: 2. Of those that a mesh axis runs over, the one named last changes fastest.
Arguments:
- layer_input: bfloat16 [4, 16, 512, 768], P('tower', 'dp'), may hold values from -6 to 6
- seg_lengths: int32 [4, 16, 16], P('tower', 'dp'), may hold values from 0 to 512, as said below
- positives: int32 [2, 16, 16], P(None, 'dp'), may hold values from 0 to 511, as said below
- query_weight: bfloat16 [768, 768], replicated, may hold values from -0.3125 to 0.3125
- key_weight: bfloat16 [768, 768], replicated, may hold values from -0.3125 to 0.3125
- value_weight: bfloat16 [768, 768], replicated, may hold values from -0.21875 to 0.21875
- out_weight: bfloat16 [768, 768], replicated, may hold values from -0.4375 to 0.4375
- up_weight: bfloat16 [768, 3072], replicated, may hold values from -0.21875 to 0.21875
- down_weight: bfloat16 [3072, 768], replicated, may hold values from -0.109375 to 0.109375
- query_bias: bfloat16 [768], replicated, may hold values from -1 to 1
- value_offset_bias: bfloat16 [768], replicated, may hold values from -1 to 1
- out_bias: bfloat16 [768], replicated, may hold values from -1 to 1
- up_bias: bfloat16 [3072], replicated, may hold values from -1 to 1
- down_bias: bfloat16 [768], replicated, may hold values from -1 to 1
- first_gain: bfloat16 [768], replicated, may hold values from 0.5 to 1.5
- first_shift: bfloat16 [768], replicated, may hold values from -0.5 to 0.5
- second_gain: bfloat16 [768], replicated, may hold values from 0.5 to 1.5
- latter_norm_translation: bfloat16 [768], replicated, may hold values from -0.25 to 0.25
Outputs:
- loss: float32 [], replicated
- grad_input: float32 [4, 16, 512, 768], P('tower', 'dp')
- grad_query_weight: float32 [768, 768], P('dp')
- grad_key_weight: float32 [768, 768], P('dp')
- grad_value_weight: float32 [768, 768], P('dp')
- grad_out_weight: float32 [768, 768], P('dp')
- grad_up_weight: float32 [768, 3072], P('dp')
- grad_down_weight: float32 [3072, 768], P('dp')
- grad_query_bias: float32 [768], P('dp')
- grad_value_bias: float32 [768], P('dp')
- grad_out_bias: float32 [768], P('dp')
- grad_up_bias: float32 [3072], P('dp')
- grad_down_bias: float32 [768], P('dp')
- grad_first_gain: float32 [768], P('dp')
- grad_first_shift: float32 [768], P('dp')
- grad_second_gain: float32 [768], P('dp')
- grad_second_shift: float32 [768], P('dp')
The draws below stay inside these ranges and needn't reach their ends.
Inputs may be any that keep to these rules, and one draw needn't show every extreme that they name: `seg_lengths`: in each row the first c slots hold the lengths of the row's c segments in order, each at least 1, summing to 512; the other slots are 0. c is at least 1 and at most 16; the first row of each tower index has c = 1 and the last row has c = 16. `positives`: each entry is a passage number as in the statement and names a live passage slot; entries of empty query slots are not read.
All inputs are finite; a program needn't handle non-finite values.
Results may differ from the reference program's by a relative error of at most 0.015.
Values may be sent and summed in bfloat16 or wider, within the bound.
No kernel may reach another device: no remote copies, remote signals or barrier semaphores. Data moves between devices by JAX's collectives and lax.ppermute only.
A program may use at most 192 MiB of HBM per device.

```python
import jax
import jax.numpy as jnp
from jax import lax

D = 768
H = 12
HD = 64
FF = 3072
LEN = 512
SEG_ROW = 16
ROWS = 16
N_TOWER = 4


def piece_tallies(key):
    floor_count = max(1, SEG_ROW // 8)
    places = jnp.arange(ROWS, dtype=jnp.int32)
    lowest = floor_count + (SEG_ROW - floor_count) * places // ROWS
    extra = jax.random.randint(jax.random.fold_in(key, 11), (N_TOWER, ROWS), 0, max(1, SEG_ROW // 4) + 1)
    counts = jnp.minimum(lowest[None, :] + extra, SEG_ROW)
    counts = jnp.where(places[None, :] == 0, 1, counts)
    counts = jnp.where(places[None, :] == ROWS - 1, SEG_ROW, counts)
    return counts.astype(jnp.int32)


def draw_seg_lengths(key, part):
    counts = piece_tallies(key)
    row_keys = jax.random.split(jax.random.fold_in(key, 23), N_TOWER * ROWS)
    cuts = jax.vmap(lambda row_key: jax.random.permutation(row_key, LEN - 1)[:SEG_ROW - 1] + 1)(row_keys)
    cuts = cuts.astype(jnp.int32).reshape(N_TOWER, ROWS, SEG_ROW - 1)
    slot_ids = jnp.arange(SEG_ROW - 1, dtype=jnp.int32)
    cuts = jnp.where(slot_ids[None, None, :] < counts[..., None] - 1, cuts, LEN)
    cuts = jnp.sort(cuts, axis=-1)
    starts = jnp.concatenate([jnp.zeros((N_TOWER, ROWS, 1), jnp.int32), cuts], axis=-1)
    ends = jnp.concatenate([cuts, jnp.full((N_TOWER, ROWS, 1), LEN, jnp.int32)], axis=-1)
    return (ends - starts).astype(jnp.int32)


def draw_positives(key, part):
    counts = piece_tallies(key)
    passage_counts = counts[N_TOWER // 2:].reshape(-1)
    pick_row = jax.random.randint(jax.random.fold_in(key, 37), (2, ROWS, SEG_ROW), 0, 2 * ROWS)
    chosen = passage_counts[pick_row]
    pick_slot = jax.random.randint(jax.random.fold_in(key, 41), (2, ROWS, SEG_ROW), 0, chosen)
    result = (pick_row * SEG_ROW + pick_slot).astype(jnp.int32)
    result = result.at[1, ROWS - 1, SEG_ROW - 1].set(2 * ROWS * SEG_ROW - 1)
    result = result.at[0, 0, 0].set(0)
    return result.astype(jnp.int32)


def shard_levels(own_key, shape, shards, least, largest):
    level, own = 1.0, jax.random.fold_in(own_key, 6)
    for axis_at, parts in shards:
        heights = jnp.exp(jax.random.uniform(jax.random.fold_in(own, axis_at), (parts,), jnp.float32, least / len(shards), largest / len(shards)))
        level = level * jnp.repeat(heights, shape[axis_at] // parts).reshape([-1 if axis == axis_at else 1 for axis in range(len(shape))])
    return level


def normal_values(rng, dims, scale, limit, cuts=(), kind=jnp.bfloat16):
    array = scale * jax.random.normal(rng, dims, jnp.float32)
    if cuts:
        array = array * shard_levels(rng, dims, cuts, -0.22, 0.18)
    return jnp.clip(array, -limit, limit).astype(kind)


def setup_inputs(seed: int = 0) -> dict:
    arg_keys = jax.random.split(jax.random.key(seed), 19)
    return {
        "layer_input": normal_values(arg_keys[0], (N_TOWER, ROWS, LEN, D), 1.0, 6.0, ((0, 4), (1, 8))),
        "seg_lengths": draw_seg_lengths(jax.random.fold_in(arg_keys[18], 71), 0),
        "positives": draw_positives(jax.random.fold_in(arg_keys[18], 71), 0),
        "query_weight": normal_values(arg_keys[3], (D, D), (D // 2) ** -0.5, 0.3125),
        "key_weight": normal_values(arg_keys[4], (D, D), (D // 2) ** -0.5, 0.3125),
        "value_weight": normal_values(arg_keys[5], (D, D), D ** -0.5, 0.21875),
        "out_weight": normal_values(arg_keys[6], (D, D), (D // 4) ** -0.5, 0.4375),
        "up_weight": normal_values(arg_keys[7], (D, FF), D ** -0.5, 0.21875),
        "down_weight": normal_values(arg_keys[8], (FF, D), FF ** -0.5, 0.109375),
        "query_bias": normal_values(arg_keys[9], (D,), 0.2, 1.0),
        "value_offset_bias": normal_values(arg_keys[10], (D,), 0.2, 1.0),
        "out_bias": normal_values(arg_keys[11], (D,), 0.2, 1.0),
        "up_bias": normal_values(arg_keys[12], (FF,), 0.2, 1.0),
        "down_bias": normal_values(arg_keys[13], (D,), 0.2, 1.0),
        "first_gain": jnp.clip(1.0 + 0.1 * jax.random.normal(arg_keys[14], (D,), jnp.float32), 0.5, 1.5).astype(jnp.bfloat16),
        "first_shift": normal_values(arg_keys[15], (D,), 0.1, 0.5),
        "second_gain": jnp.clip(1.0 + 0.1 * jax.random.normal(arg_keys[16], (D,), jnp.float32), 0.5, 1.5).astype(jnp.bfloat16),
        "latter_norm_translation": normal_values(arg_keys[17], (D,), 0.05, 0.25),
    }


finest_matmul_mode = lax.Precision.HIGHEST
contrastive_sharpness_divisor = 0.01
norm_eps = 1e-06
pool_eps = 1e-06
masked_score = -1e+30

@jax.custom_vjp
def low(v):
    return lax.optimization_barrier(v.astype(jnp.bfloat16)).astype(jnp.float32)

@jax.custom_vjp
def summed_gradient_pass(v):
    return v

def low_keep(v):
    return (low(v), None)

def low_pass(kept, grad):
    return (grad,)

def back_keep(v):
    return (v, None)

def back_low(kept, grad):
    return (low(grad),)
low.defvjp(low_keep, low_pass)
summed_gradient_pass.defvjp(back_keep, back_low)

def segment_ids(seg_rows, row_width):
    ends = jnp.cumsum(seg_rows, axis=-1).astype(jnp.int32)
    places = jnp.arange(row_width, dtype=jnp.int32)
    return lax.optimization_barrier(jnp.sum((places[:, None] >= ends[..., None, :]).astype(jnp.int32), axis=-1)).astype(jnp.int32)

def layer_norm(values, gain, shift):
    middle = lax.optimization_barrier(jnp.mean(values, axis=-1, keepdims=True))
    centered = values - middle
    token_variance = lax.optimization_barrier(jnp.mean(centered * centered, axis=-1, keepdims=True))
    return centered * lax.rsqrt(token_variance + norm_eps) * gain + shift

def encode_row(tokens, seg_row, params):
    query_weight, key_weight, value_weight, out_weight, up_weight, down_weight, query_bias, value_offset_bias, out_bias, up_bias, down_bias, first_gain, first_shift, second_gain, latter_norm_translation = params
    score_scale = HD ** (-0.5)
    queries = low(summed_gradient_pass(jnp.dot(tokens, query_weight, precision=finest_matmul_mode) + query_bias)).reshape(LEN, H, HD)
    key_rows = low(summed_gradient_pass(jnp.dot(tokens, key_weight, precision=finest_matmul_mode))).reshape(LEN, H, HD)
    values = low(summed_gradient_pass(jnp.dot(tokens, value_weight, precision=finest_matmul_mode) + value_offset_bias)).reshape(LEN, H, HD)
    scores = summed_gradient_pass(jnp.einsum('qhd,khd->hqk', queries, key_rows, precision=finest_matmul_mode) * score_scale)
    same_seg = seg_row[:, None] == seg_row[None, :]
    scores = jnp.where(same_seg[None], scores, masked_score)
    row_top = lax.optimization_barrier(jnp.max(scores, axis=-1, keepdims=True))
    shifted = jnp.exp(scores - row_top)
    probs = shifted / lax.optimization_barrier(jnp.sum(shifted, axis=-1, keepdims=True))
    mixed_out = jnp.einsum('hqk,khd->qhd', low(probs), values, precision=finest_matmul_mode).reshape(LEN, D)
    mixed_out = low(summed_gradient_pass(mixed_out))
    branch = summed_gradient_pass(jnp.dot(mixed_out, out_weight, precision=finest_matmul_mode) + out_bias)
    first_out = layer_norm(tokens + branch, first_gain, first_shift)
    hidden = summed_gradient_pass(jnp.dot(low(first_out), up_weight, precision=finest_matmul_mode) + up_bias)
    active = low(jax.nn.gelu(hidden, approximate=False))
    second = summed_gradient_pass(jnp.dot(active, down_weight, precision=finest_matmul_mode) + down_bias)
    return layer_norm(first_out + second, second_gain, latter_norm_translation)

def objective(inputs, params, seg_tokens, member, divisor, live_slot, targets):
    row_step = jax.checkpoint(encode_row)
    rows_all = inputs.reshape(N_TOWER * ROWS, LEN, D)
    encoded = lax.map(lambda row_pair: row_step(row_pair[0], row_pair[1], params), (rows_all, seg_tokens))
    pooled = jnp.einsum('rsl,rld->rsd', member, encoded, precision=finest_matmul_mode) / divisor[..., None]
    norm_sq = lax.optimization_barrier(jnp.sum(pooled * pooled, axis=-1, keepdims=True))
    unit_vec = low(pooled * lax.rsqrt(norm_sq + pool_eps)).reshape(N_TOWER, ROWS * SEG_ROW, D)
    half_tower = N_TOWER // 2
    question_vector = unit_vec[:half_tower].reshape(half_tower * ROWS * SEG_ROW, D)
    document_vector = unit_vec[half_tower:].reshape((N_TOWER - half_tower) * ROWS * SEG_ROW, D)
    query_live = live_slot[:half_tower].reshape(-1)
    passage_live = live_slot[half_tower:].reshape(-1)
    pairwise_match_scores = summed_gradient_pass(jnp.dot(question_vector, document_vector.T, precision=finest_matmul_mode) / contrastive_sharpness_divisor)
    pairwise_match_scores = jnp.where(passage_live[None, :], pairwise_match_scores, masked_score)
    row_top = lax.optimization_barrier(jnp.max(pairwise_match_scores, axis=-1, keepdims=True))
    log_sum = (row_top + jnp.log(lax.optimization_barrier(jnp.sum(jnp.exp(pairwise_match_scores - row_top), axis=-1, keepdims=True))))[:, 0]
    picked = jnp.take_along_axis(pairwise_match_scores, targets.reshape(-1, 1), axis=1)[:, 0]
    query_count = jnp.sum(query_live.astype(jnp.float32))
    return jnp.sum(jnp.where(query_live, log_sum - picked, 0.0)) / query_count

def reference(layer_input, seg_lengths, positives, query_weight, key_weight, value_weight, out_weight, up_weight, down_weight, query_bias, value_offset_bias, out_bias, up_bias, down_bias, first_gain, first_shift, second_gain, latter_norm_translation):
    params = tuple((item.astype(jnp.float32) for item in (query_weight, key_weight, value_weight, out_weight, up_weight, down_weight, query_bias, value_offset_bias, out_bias, up_bias, down_bias, first_gain, first_shift, second_gain, latter_norm_translation)))
    inputs = layer_input.astype(jnp.float32)
    seg_rows = seg_lengths.reshape(N_TOWER * ROWS, SEG_ROW)
    seg_tokens = segment_ids(seg_rows, LEN)
    slot_ids = jnp.arange(SEG_ROW, dtype=jnp.int32)
    member = (seg_tokens[:, None, :] == slot_ids[None, :, None]).astype(jnp.float32)
    divisor = jnp.maximum(seg_rows, 1).astype(jnp.float32)
    live_slot = (seg_lengths > 0).reshape(N_TOWER, ROWS * SEG_ROW)
    targets = positives.reshape(-1).astype(jnp.int32)

    def loss_of(inputs_in, params_in):
        return objective(inputs_in, params_in, seg_tokens, member, divisor, live_slot, targets)
    loss, pullback = jax.vjp(loss_of, inputs, params)
    grad_input, grad_params = pullback(jnp.ones((), jnp.float32))
    return (loss, grad_input, grad_params[0], grad_params[1], grad_params[2], grad_params[3], grad_params[4], grad_params[5], grad_params[6], grad_params[7], grad_params[8], grad_params[9], grad_params[10], grad_params[11], grad_params[12], grad_params[13], grad_params[14])
```

```python
from functools import partial

import jax
import jax.numpy as jnp
from jax import lax
from jax.sharding import PartitionSpec as P

H = 12


finest_matmul_mode = lax.Precision.HIGHEST
inverse_temp = 100.0
norm_eps = 1e-06
pool_eps = 1e-06
masked_score = -1e30


def segment_ids(seg_rows, row_width):
    ends = jnp.cumsum(seg_rows, axis=-1)
    places = jnp.arange(row_width, dtype=jnp.int32)
    return jnp.sum((places[:, None] >= ends[..., None, :]).astype(jnp.int32), axis=-1)


def exact_gelu(values):
    return jax.nn.gelu(values, approximate=False)


def layer_stats(values):
    middle = jnp.mean(values, axis=-1, keepdims=True)
    centered = values - middle
    token_variance = jnp.mean(centered * centered, axis=-1, keepdims=True)
    inverse = lax.rsqrt(token_variance + norm_eps)
    return (centered * inverse, inverse)


def layer_back(grad_out, scaled, inverse, gain):
    grad_norm = grad_out * gain
    grad_in = inverse * (
        grad_norm
        - jnp.mean(grad_norm, axis=-1, keepdims=True)
        - scaled * jnp.mean(grad_norm * scaled, axis=-1, keepdims=True)
    )
    return (grad_in, jnp.sum(grad_out * scaled, axis=0), jnp.sum(grad_out, axis=0))


def score_block(score_scale, query_row, key_row, seg_row):
    scores = (
        jnp.einsum("qhd,khd->hqk", query_row, key_row, preferred_element_type=jnp.float32)
        * score_scale
    )
    same_seg = seg_row[:, None] == seg_row[None, :]
    return (jnp.where(same_seg[None], scores, masked_score), same_seg)


def attend_row(score_scale, row_args):
    query_row, key_row, value_row, seg_row = row_args
    scores, same_seg = score_block(score_scale, query_row, key_row, seg_row)
    row_top = jnp.max(scores, axis=-1, keepdims=True)
    shifted = jnp.exp(scores - row_top)
    row_total = jnp.sum(shifted, axis=-1, keepdims=True)
    prob_low = (shifted / row_total).astype(jnp.bfloat16)
    mixed_out = jnp.einsum("hqk,khd->qhd", prob_low, value_row, preferred_element_type=jnp.float32)
    return (mixed_out, (row_top + jnp.log(row_total))[..., 0])


def attend_back(score_scale, row_args):
    query_row, key_row, value_row, seg_row, log_total, grad_mixed = row_args
    scores, same_seg = score_block(score_scale, query_row, key_row, seg_row)
    probs = jnp.where(same_seg[None], jnp.exp(scores - log_total[..., None]), 0.0)
    grad_values = jnp.einsum(
        "hqk,qhd->khd", probs.astype(jnp.bfloat16), grad_mixed, preferred_element_type=jnp.float32
    )
    grad_prob = jnp.einsum(
        "qhd,khd->hqk", grad_mixed, value_row, preferred_element_type=jnp.float32
    )
    inner = jnp.sum(grad_prob * probs, axis=-1, keepdims=True)
    grad_scores = (probs * (grad_prob - inner)).astype(jnp.bfloat16)
    grad_queries = (
        jnp.einsum("hqk,khd->qhd", grad_scores, key_row, preferred_element_type=jnp.float32)
        * score_scale
    )
    grad_keys = (
        jnp.einsum("hqk,qhd->khd", grad_scores, query_row, preferred_element_type=jnp.float32)
        * score_scale
    )
    return (
        grad_queries.astype(jnp.bfloat16),
        grad_keys.astype(jnp.bfloat16),
        grad_values.astype(jnp.bfloat16),
    )


def swap(value, axis, bits):
    count = lax.axis_size(axis)
    return lax.ppermute(value, axis, [(place, place ^ bits) for place in range(count)])


def swap_both(value, tower_bits, dp_bits):
    if not tower_bits:
        return swap(value, "dp", dp_bits)
    if not dp_bits:
        return swap(value, "tower", tower_bits)
    towers = lax.axis_size("tower")
    total = towers * lax.axis_size("dp")
    moves = [(place, place ^ (dp_bits * towers + tower_bits)) for place in range(total)]
    return lax.ppermute(value, ("dp", "tower"), moves)


def outer_bits():
    outer = lax.axis_size("dp") // 2
    return [1 << k for k in range(outer.bit_length() - 1)]


def gather_all(block):
    outer = lax.axis_size("dp") // 2
    if outer <= 4:
        blocks = jnp.stack([block] + [swap(block, "dp", 2 * k) for k in range(1, outer)])
    else:
        blocks = block[None]
        for bit in outer_bits():
            blocks = jnp.concatenate([blocks, swap(blocks, "dp", 2 * bit)])
    sides = [swap_both(blocks, 2 * x, y) if x or y else blocks for x in range(2) for y in range(2)]
    blocks = jnp.stack(sides).reshape((2, 2) + blocks.shape)
    return jnp.stack([blocks, swap(blocks, "tower", 1)], axis=1)


def slot_numbers(slot_total):
    outer = lax.axis_size("dp") // 2
    tower_index = lax.axis_index("tower")
    dp_index = lax.axis_index("dp")
    cores = jnp.arange(2)[:, None, None, None]
    sides = jnp.arange(2)[None, :, None, None]
    outers = jnp.arange(outer)[None, None, :, None]
    slots = jnp.arange(slot_total)[None, None, None, :]
    tower = (tower_index & 1) ^ cores
    place = dp_index ^ (outers * 2 + sides)
    numbers = (tower * lax.axis_size("dp") + place) * slot_total + slots
    return jnp.broadcast_to(numbers.reshape(1, -1), (2, numbers.size))


def pick(value, index):
    return lax.dynamic_index_in_dim(value, index, 0, keepdims=False)


def add_up(parts):
    total = parts[0].astype(jnp.float32)
    for part in parts[1:]:
        total = total + part.astype(jnp.float32)
    return total


def sum_group(blocks):
    outer = lax.axis_size("dp") // 2
    tower_index = lax.axis_index("tower")
    dp_index = lax.axis_index("dp")
    core, far = tower_index & 1, tower_index >> 1
    side, place = dp_index & 1, dp_index >> 1
    got = swap(pick(blocks, 1 - core), "tower", 1)
    blocks = add_up([pick(blocks, core), got]).astype(jnp.bfloat16)
    blocks = blocks.reshape((4,) + blocks.shape[2:])
    own = far * 2 + side
    parts = [pick(blocks, own)]
    for rel in range(1, 4):
        parts.append(swap_both(pick(blocks, own ^ rel), 2 * (rel >> 1), rel & 1))
    blocks = add_up(parts).astype(jnp.bfloat16)
    if outer <= 4:
        parts = [pick(blocks, place)]
        for rel in range(1, outer):
            parts.append(swap(pick(blocks, place ^ rel), "dp", 2 * rel))
        total = add_up(parts)
    else:
        for bit in reversed(outer_bits()):
            halves = blocks.reshape((2, bit) + blocks.shape[1:])
            mine = jnp.where(place & bit, 1, 0)
            got = swap(pick(halves, 1 - mine), "dp", 2 * bit)
            total = add_up([pick(halves, mine), got])
            blocks = total.astype(jnp.bfloat16)
        total = total[0]
    low = total.astype(jnp.bfloat16)
    got = swap(low, "tower", 2)
    pair = jnp.where(far == 0, jnp.stack([low, got]), jnp.stack([got, low]))
    got = swap(pair, "tower", 1)
    every = jnp.where(core == 0, jnp.stack([pair, got]), jnp.stack([got, pair]))
    return every.astype(jnp.float32)


def shards(
    layer_input,
    seg_lengths,
    positives,
    query_weight,
    key_weight,
    value_weight,
    out_weight,
    up_weight,
    down_weight,
    query_bias,
    value_offset_bias,
    out_bias,
    up_bias,
    down_bias,
    first_gain,
    first_shift,
    second_gain,
    latter_norm_translation,
):
    row_count = layer_input.shape[1]
    row_len = layer_input.shape[2]
    model_width = layer_input.shape[3]
    head_size = model_width // H
    slot_count = seg_lengths.shape[2]
    token_count = row_count * row_len
    slot_total = row_count * slot_count
    score_scale = head_size ** (-0.5)
    heads_shape = (row_count, row_len, H, head_size)
    flat_in = layer_input.reshape(token_count, model_width)
    seg_rows = seg_lengths.reshape(row_count, slot_count)
    seg_tokens = segment_ids(seg_rows, row_len)
    queries = jnp.dot(
        flat_in, query_weight, preferred_element_type=jnp.float32
    ) + query_bias.astype(jnp.float32)
    key_out = jnp.dot(flat_in, key_weight, preferred_element_type=jnp.float32)
    value_out = jnp.dot(
        flat_in, value_weight, preferred_element_type=jnp.float32
    ) + value_offset_bias.astype(jnp.float32)
    query_low = queries.astype(jnp.bfloat16).reshape(heads_shape)
    key_low = key_out.astype(jnp.bfloat16).reshape(heads_shape)
    value_low = value_out.astype(jnp.bfloat16).reshape(heads_shape)
    mixed_out, log_total = lax.map(
        partial(attend_row, score_scale), (query_low, key_low, value_low, seg_tokens)
    )
    mixed_low = mixed_out.reshape(token_count, model_width).astype(jnp.bfloat16)
    branch = jnp.dot(mixed_low, out_weight, preferred_element_type=jnp.float32) + out_bias.astype(
        jnp.float32
    )
    first_scaled, first_inverse = layer_stats(flat_in.astype(jnp.float32) + branch)
    gain_first = first_gain.astype(jnp.float32)
    first_out = first_scaled * gain_first + first_shift.astype(jnp.float32)
    first_low = first_out.astype(jnp.bfloat16)
    hidden = jnp.dot(first_low, up_weight, preferred_element_type=jnp.float32) + up_bias.astype(
        jnp.float32
    )
    active, gelu_back = jax.vjp(exact_gelu, hidden)
    active_low = active.astype(jnp.bfloat16)
    second = jnp.dot(
        active_low, down_weight, preferred_element_type=jnp.float32
    ) + down_bias.astype(jnp.float32)
    second_scaled, second_inverse = layer_stats(first_out + second)
    gain_second = second_gain.astype(jnp.float32)
    final_out = second_scaled * gain_second + latter_norm_translation.astype(jnp.float32)
    slot_ids = jnp.arange(slot_count, dtype=jnp.int32)
    member = (seg_tokens[:, None, :] == slot_ids[None, :, None]).astype(jnp.float32)
    divisor = jnp.maximum(seg_rows, 1).astype(jnp.float32)
    pooled = (
        jnp.einsum(
            "rsl,rld->rsd",
            member,
            final_out.reshape(row_count, row_len, model_width),
            precision=finest_matmul_mode,
        )
        / divisor[..., None]
    )
    norm_sq = jnp.sum(pooled * pooled, axis=-1, keepdims=True)
    inverse = lax.rsqrt(norm_sq + pool_eps)
    unit_low = (pooled * inverse).reshape(slot_total, model_width).astype(jnp.bfloat16)
    tower_index = lax.axis_index("tower")
    half_tower = lax.axis_size("tower") // 2
    is_query = tower_index < half_tower
    live_slot = (seg_rows > 0).reshape(slot_total)
    own_targets = lax.dynamic_index_in_dim(
        positives, jnp.minimum(tower_index, half_tower - 1), 0, keepdims=False
    ).reshape(slot_total)
    marks = jnp.stack(
        [live_slot.astype(jnp.int32), own_targets // 64, own_targets % 64], axis=-1
    ).astype(jnp.bfloat16)
    marks = jnp.pad(marks, ((0, 0), (0, 125)))
    rows = gather_all(jnp.concatenate([unit_low, marks], axis=-1))
    rows = rows.reshape(2, -1, model_width + 128)
    query_side = jnp.where(is_query, rows[0], rows[1])
    passage_side = jnp.where(is_query, rows[1], rows[0])
    numbers = slot_numbers(slot_total)
    passage_numbers = jnp.where(is_query, numbers[1], numbers[0])
    question_vector = query_side[:, :model_width]
    document_vector = passage_side[:, :model_width]
    query_live = query_side[:, model_width] > 0
    passage_live = passage_side[:, model_width] > 0
    query_targets = query_side[:, model_width + 1].astype(jnp.int32) * 64 + query_side[
        :, model_width + 2
    ].astype(jnp.int32)
    query_count = jnp.sum(query_live.astype(jnp.float32))
    scores = (
        jnp.einsum("qd,pd->qp", question_vector, document_vector, preferred_element_type=jnp.float32)
        * inverse_temp
    )
    scores = jnp.where(passage_live[None, :], scores, masked_score)
    row_top = jnp.max(scores, axis=-1, keepdims=True)
    log_sum = row_top + jnp.log(jnp.sum(jnp.exp(scores - row_top), axis=-1, keepdims=True))
    is_target = passage_numbers[None, :] == query_targets[:, None]
    picked = jnp.sum(jnp.where(is_target, scores, 0.0), axis=-1)
    loss = jnp.sum(jnp.where(query_live, log_sum[:, 0] - picked, 0.0)) / query_count
    chances = jnp.where(passage_live[None, :], jnp.exp(scores - log_sum), 0.0)
    grad_logits = jnp.where(
        query_live[:, None], (chances - is_target.astype(jnp.float32)) / query_count, 0.0
    ).astype(jnp.bfloat16)
    query_grad = jnp.einsum(
        "sp,pd->sd", grad_logits[:slot_total], document_vector, preferred_element_type=jnp.float32
    )
    passage_grad = jnp.einsum(
        "qs,qd->sd", grad_logits[:, :slot_total], question_vector, preferred_element_type=jnp.float32
    )
    grad_unit = jnp.where(is_query, query_grad, passage_grad) * inverse_temp
    grad_unit_rows = grad_unit.reshape(row_count, slot_count, model_width)
    grad_pooled = inverse * grad_unit_rows - pooled * (inverse * inverse * inverse) * jnp.sum(
        grad_unit_rows * pooled, axis=-1, keepdims=True
    )
    grad_final = jnp.einsum(
        "rsl,rsd->rld", member, grad_pooled / divisor[..., None], precision=finest_matmul_mode
    ).reshape(token_count, model_width)
    grad_sum2, grad_second_gain, grad_second_shift = layer_back(
        grad_final, second_scaled, second_inverse, gain_second
    )
    grad_second_low = grad_sum2.astype(jnp.bfloat16)
    grad_down_weight = jnp.einsum(
        "tf,td->fd", active_low, grad_second_low, preferred_element_type=jnp.float32
    )
    grad_down_bias = jnp.sum(grad_second_low.astype(jnp.float32), axis=0)
    grad_active = jnp.einsum(
        "td,fd->tf", grad_second_low, down_weight, preferred_element_type=jnp.float32
    )
    grad_hidden_low = gelu_back(grad_active)[0].astype(jnp.bfloat16)
    grad_up_weight = jnp.einsum(
        "td,tf->df", first_low, grad_hidden_low, preferred_element_type=jnp.float32
    )
    grad_up_bias = jnp.sum(grad_hidden_low.astype(jnp.float32), axis=0)
    grad_first = (
        jnp.einsum("tf,df->td", grad_hidden_low, up_weight, preferred_element_type=jnp.float32)
        + grad_sum2
    )
    grad_sum1, grad_first_gain, grad_first_shift = layer_back(
        grad_first, first_scaled, first_inverse, gain_first
    )
    grad_branch_low = grad_sum1.astype(jnp.bfloat16)
    grad_out_weight = jnp.einsum(
        "td,te->de", mixed_low, grad_branch_low, preferred_element_type=jnp.float32
    )
    grad_out_bias = jnp.sum(grad_branch_low.astype(jnp.float32), axis=0)
    grad_mixed_low = (
        jnp.einsum("te,de->td", grad_branch_low, out_weight, preferred_element_type=jnp.float32)
        .astype(jnp.bfloat16)
        .reshape(heads_shape)
    )
    grad_queries, grad_keys, grad_values = lax.map(
        partial(attend_back, score_scale),
        (query_low, key_low, value_low, seg_tokens, log_total, grad_mixed_low),
    )
    grad_queries = grad_queries.reshape(token_count, model_width)
    grad_keys = grad_keys.reshape(token_count, model_width)
    grad_values = grad_values.reshape(token_count, model_width)
    grad_query_weight = jnp.einsum(
        "td,te->de", flat_in, grad_queries, preferred_element_type=jnp.float32
    )
    grad_key_weight = jnp.einsum(
        "td,te->de", flat_in, grad_keys, preferred_element_type=jnp.float32
    )
    grad_value_weight = jnp.einsum(
        "td,te->de", flat_in, grad_values, preferred_element_type=jnp.float32
    )
    grad_query_bias = jnp.sum(grad_queries.astype(jnp.float32), axis=0)
    grad_value_bias = jnp.sum(grad_values.astype(jnp.float32), axis=0)
    grad_input = (
        grad_sum1
        + jnp.einsum("te,de->td", grad_queries, query_weight, preferred_element_type=jnp.float32)
        + jnp.einsum("te,de->td", grad_keys, key_weight, preferred_element_type=jnp.float32)
        + jnp.einsum("te,de->td", grad_values, value_weight, preferred_element_type=jnp.float32)
    )
    grad_input = grad_input.reshape(layer_input.shape)
    dp_count = lax.axis_size("dp")
    outer = dp_count // 2
    share = model_width // dp_count
    wide = 4 * share

    def by_rows(grad):
        return grad.astype(jnp.bfloat16).reshape(outer, 2, share, 2, 2, model_width).transpose(
            3, 4, 1, 0, 2, 5
        )

    square = jnp.stack([grad_query_weight, grad_key_weight, grad_value_weight, grad_out_weight], axis=1)
    vectors = jnp.concatenate(
        [
            vec.reshape(dp_count, -1)
            for vec in (
                grad_query_bias,
                grad_value_bias,
                grad_out_bias,
                grad_down_bias,
                grad_first_gain,
                grad_first_shift,
                grad_second_gain,
                grad_second_shift,
                grad_up_bias,
            )
        ],
        axis=1,
    )
    vectors = vectors.astype(jnp.bfloat16).reshape(outer, 2, 2, 2, -1).transpose(2, 3, 1, 0, 4)
    vectors = jnp.pad(vectors, ((0, 0),) * 4 + ((0, model_width - vectors.shape[-1]),))
    down = (
        grad_down_weight.astype(jnp.bfloat16)
        .reshape(outer, 2, 2, 2, share, model_width)
        .transpose(2, 3, 1, 0, 4, 5)
    )
    total_down = sum_group(down).reshape(wide, model_width)
    total_up = sum_group(by_rows(grad_up_weight)).reshape(4, share, model_width)
    total_up = total_up.transpose(1, 0, 2).reshape(share, wide // share * model_width)
    last = jnp.concatenate([by_rows(square), vectors[:, :, :, :, None]], axis=4)
    last = sum_group(last).reshape(4, share + 1, model_width)
    total_query, total_key, total_value, total_out = [last[i, :share] for i in range(4)]
    short = last[:, share, : share * 12 // 4].reshape(-1)
    (
        total_query_bias,
        total_value_bias,
        total_out_bias,
        total_down_bias,
        total_first_gain,
        total_first_shift,
        total_second_gain,
        total_second_shift,
    ) = [short[i * share : (i + 1) * share] for i in range(8)]
    total_up_bias = short[8 * share :]
    return (
        loss,
        grad_input,
        total_query,
        total_key,
        total_value,
        total_out,
        total_up,
        total_down,
        total_query_bias,
        total_value_bias,
        total_out_bias,
        total_up_bias,
        total_down_bias,
        total_first_gain,
        total_first_shift,
        total_second_gain,
        total_second_shift,
    )


def solution(mesh):
    in_specs = (
        P("tower", "dp", None, None),
        P("tower", "dp", None),
        P(None, "dp", None),
        P(),
        P(),
        P(),
        P(),
        P(),
        P(),
        P(),
        P(),
        P(),
        P(),
        P(),
        P(),
        P(),
        P(),
        P(),
    )
    out_specs = (
        P(),
        P("tower", "dp", None, None),
        P("dp", None),
        P("dp", None),
        P("dp", None),
        P("dp", None),
        P("dp", None),
        P("dp", None),
        P("dp"),
        P("dp"),
        P("dp"),
        P("dp"),
        P("dp"),
        P("dp"),
        P("dp"),
        P("dp"),
        P("dp"),
    )
    return jax.shard_map(shards, mesh=mesh, in_specs=in_specs, out_specs=out_specs, check_vma=False)
```

```python
from functools import partial

import jax
import jax.numpy as jnp
from jax import lax
from jax.experimental import pallas as pl
from jax.experimental.pallas import tpu as pltpu
from jax.sharding import PartitionSpec as P

H = 12

inverse_temp = 100.0
norm_eps = 1e-06
pool_eps = 1e-06
masked_score = -1e30
f32 = jnp.float32
bf16 = jnp.bfloat16


def swap(value, axis, bits):
    count = lax.axis_size(axis)
    return lax.ppermute(value, axis, [(place, place ^ bits) for place in range(count)])


def swap_both(value, tower_bits, dp_bits):
    if not tower_bits:
        return swap(value, "dp", dp_bits)
    if not dp_bits:
        return swap(value, "tower", tower_bits)
    towers = lax.axis_size("tower")
    total = towers * lax.axis_size("dp")
    moves = [(place, place ^ (dp_bits * towers + tower_bits)) for place in range(total)]
    return lax.ppermute(value, ("dp", "tower"), moves)


def outer_bits():
    outer = lax.axis_size("dp") // 2
    return [1 << k for k in range(outer.bit_length() - 1)]


def gather_all(block):
    outer = lax.axis_size("dp") // 2
    if outer <= 4:
        blocks = jnp.stack([block] + [swap(block, "dp", 2 * k) for k in range(1, outer)])
    else:
        blocks = block[None]
        for bit in outer_bits():
            blocks = jnp.concatenate([blocks, swap(blocks, "dp", 2 * bit)])
    sides = [swap_both(blocks, 2 * x, y) if x or y else blocks for x in range(2) for y in range(2)]
    blocks = jnp.stack(sides).reshape((2, 2) + blocks.shape)
    return jnp.stack([blocks, swap(blocks, "tower", 1)], axis=1)


def pick(value, index):
    return lax.dynamic_index_in_dim(value, index, 0, keepdims=False)


def add_up(parts):
    total = parts[0].astype(f32)
    for part in parts[1:]:
        total = total + part.astype(f32)
    return total


def sum_group(blocks):
    tower_index = lax.axis_index("tower")
    dp_index = lax.axis_index("dp")
    core, far = tower_index & 1, tower_index >> 1
    side, place = dp_index & 1, dp_index >> 1
    got = swap(pick(blocks, 1 - core), "tower", 1)
    blocks = add_up([pick(blocks, core), got]).astype(bf16)
    blocks = blocks.reshape((4,) + blocks.shape[2:])
    own = far * 2 + side
    parts = [pick(blocks, own)]
    for rel in range(1, 4):
        parts.append(swap_both(pick(blocks, own ^ rel), 2 * (rel >> 1), rel & 1))
    blocks = add_up(parts).astype(bf16)
    for bit in reversed(outer_bits()):
        halves = blocks.reshape((2, bit) + blocks.shape[1:])
        mine = jnp.where(place & bit, 1, 0)
        got = swap(pick(halves, 1 - mine), "dp", 2 * bit)
        blocks = add_up([pick(halves, mine), got]).astype(bf16)
    low = blocks[0]
    got = swap(low, "tower", 2)
    pair = jnp.where(far == 0, jnp.stack([low, got]), jnp.stack([got, low]))
    got = swap(pair, "tower", 1)
    every = jnp.where(core == 0, jnp.stack([pair, got]), jnp.stack([got, pair]))
    return every.astype(f32)


def dot(left, right):
    return jnp.dot(left, right, preferred_element_type=f32)


def dot_rows(left, right):
    return lax.dot_general(left, right, (((1,), (1,)), ((), ())), preferred_element_type=f32)


def dot_cols(left, right):
    return lax.dot_general(left, right, (((0,), (0,)), ((), ())), preferred_element_type=f32)


def split_low(value):
    high = value.astype(bf16)
    return high, (value - high.astype(f32)).astype(bf16)


def segment_of(lens_ref, row, places):
    total = jnp.int32(0)
    seg = jnp.zeros(places.shape, jnp.int32)
    for slot in range(lens_ref.shape[1]):
        total = total + lens_ref[row, slot]
        seg = seg + (places >= total).astype(jnp.int32)
    return seg


def fill_mask(lens_ref, mask_ref):
    rows, length, _ = mask_ref.shape
    for row in range(rows):
        across = segment_of(lens_ref, row, lax.broadcasted_iota(jnp.int32, (1, length), 1))
        down = segment_of(lens_ref, row, lax.broadcasted_iota(jnp.int32, (length, 1), 0))
        mask_ref[row] = jnp.where(down == across, 0.0, masked_score)


def line(ref):
    return ref[...].reshape(1, -1).astype(f32)


def whole(shape):
    return pl.BlockSpec(shape, lambda *_: (0,) * len(shape))


def smem():
    return pl.BlockSpec(memory_space=pltpu.SMEM)


def shaped(shape, kind):
    return jax.ShapeDtypeStruct(shape, kind)


def params(limit):
    return pltpu.CompilerParams(vmem_limit_bytes=limit)


def cost(flops, moved):
    return pl.CostEstimate(flops=int(flops), bytes_accessed=int(moved), transcendentals=0)


def norm_stats(value):
    middle = jnp.mean(value, axis=-1, keepdims=True)
    centered = value - middle
    inverse = lax.rsqrt(jnp.mean(centered * centered, axis=-1, keepdims=True) + norm_eps)
    return centered * inverse, inverse


def norm_back(grad, scaled, inverse, gain):
    grad = grad * gain
    return inverse * (
        grad
        - jnp.mean(grad, axis=-1, keepdims=True)
        - scaled * jnp.mean(grad * scaled, axis=-1, keepdims=True)
    )


def attend_kernel(
    lens_ref, x_ref, wq, wk, wv, wo, bq, bv, bo, gain, shift,
    q_out, k_out, v_out, mixed_out, lse_out, first_out, low_out, xhat_out, inv_out,
    mask_ref, acc_ref,
):
    step = pl.program_id(0)
    steps = pl.num_programs(0)
    rows, length, _ = mask_ref.shape

    @pl.when(step == 0)
    def _():
        fill_mask(lens_ref, mask_ref)
        acc_ref[...] = x_ref[...].astype(f32) + line(bo)

    x = x_ref[...]
    q_out[...] = (dot(x, wq[...]) + line(bq)).astype(bf16)
    k_out[...] = dot(x, wk[...]).astype(bf16)
    v_out[...] = (dot(x, wv[...]) + line(bv)).astype(bf16)
    lane = lax.broadcasted_iota(jnp.int32, (1, 128), 1)
    first_half = lane < 64
    pairs = q_out.shape[1] // 128
    scale = bf16(64 ** (-0.5))
    for row in range(rows):
        for pair in range(pairs):
            tokens = slice(row * length, (row + 1) * length)
            lanes = slice(pair * 128, (pair + 1) * 128)
            q = q_out[tokens, lanes] * scale
            k = k_out[tokens, lanes]
            v = v_out[tokens, lanes]
            outs, logs = [], []
            for head in range(2):
                mine = first_half == (head == 0)
                scores = dot_rows(jnp.where(mine, q, bf16(0)), k) + mask_ref[row]
                top = jnp.max(scores, axis=-1, keepdims=True)
                shifted = jnp.exp(scores - top).astype(bf16)
                out = dot(shifted, jnp.where(mine, v, bf16(1)))
                total = pltpu.roll(out, 64, 1)
                outs.append(out / total)
                logs.append(top + jnp.log(jnp.where(mine, total, out)))
            mixed_out[tokens, lanes] = jnp.where(first_half, outs[0], outs[1]).astype(bf16)
            logs = jnp.transpose(jnp.where(first_half, logs[0], logs[1]))
            at = (step * pairs + pair) * 2
            lse_out[row, pl.ds(at, 1), :] = logs[0:1]
            lse_out[row, pl.ds(at + 1, 1), :] = logs[64:65]
    part = dot(mixed_out[...], wo[...])

    @pl.when(step < steps - 1)
    def _():
        acc_ref[...] += part

    @pl.when(step == steps - 1)
    def _():
        scaled, inverse = norm_stats(acc_ref[...] + part)
        first = scaled * line(gain) + line(shift)
        first_out[...] = first
        low_out[...] = first.astype(bf16)
        xhat_out[...] = scaled.astype(bf16)
        inv_out[...] = inverse


def attend(lens, x, wq, wk, wv, wo, bq, bv, bo, gain, shift):
    tokens, width = x.shape
    rows = lens.shape[0]
    length = tokens // rows
    group = 256
    cols = pl.BlockSpec((width, group), lambda j: (0, j))
    vec = whole((width,))
    act = pl.BlockSpec((tokens, group), lambda j: (0, j))
    full = whole((tokens, width))
    return pl.pallas_call(
        attend_kernel,
        grid=(width // group,),
        in_specs=[
            smem(), full, cols, cols, cols, pl.BlockSpec((group, width), lambda j: (j, 0)),
            pl.BlockSpec((group,), lambda j: (j,)), pl.BlockSpec((group,), lambda j: (j,)),
            vec, vec, vec,
        ],
        out_specs=[act] * 4 + [whole((rows, H, length)), full, full, full, whole((tokens, 1))],
        out_shape=[shaped((tokens, width), bf16)] * 4
        + [
            shaped((rows, H, length), f32),
            shaped((tokens, width), f32),
            shaped((tokens, width), bf16),
            shaped((tokens, width), bf16),
            shaped((tokens, 1), f32),
        ],
        scratch_shapes=[pltpu.VMEM((rows, length, length), f32), pltpu.VMEM((tokens, width), f32)],
        compiler_params=params(60 << 20),
        cost_estimate=cost(8 * tokens * width * width * 3, 20 << 20),
        name="attend",
    )(lens, x, wq, wk, wv, wo, bq, bv, bo, gain, shift)


def feed_kernel(
    lens_ref, low_ref, first_ref, wu, bu, wd, bd, gain, shift, marks,
    act_out, slope_out, xhat_out, inv_out, pool_out, unit_out, acc_ref,
):
    step = pl.program_id(0)
    steps = pl.num_programs(0)
    tokens, width = low_ref.shape
    rows, slots = lens_ref.shape
    length = tokens // rows

    @pl.when(step == 0)
    def _():
        acc_ref[...] = first_ref[...] + line(bd)

    for row in range(rows):
        at = slice(row * length, (row + 1) * length)
        hidden = dot(low_ref[at, :], wu[...]) + line(bu)
        share = 0.5 + 0.5 * lax.erf(hidden * 0.7071067811865476)
        bell = jnp.exp(hidden * hidden * -0.5) * 0.3989422804014327
        active = (hidden * share).astype(bf16)
        act_out[at, :] = active
        slope_out[at, :] = (share + hidden * bell).astype(bf16)
        acc_ref[at, :] += dot(active, wd[...])

    @pl.when(step == steps - 1)
    def _():
        for row in range(rows):
            at = slice(row * length, (row + 1) * length)
            own = slice(row * slots, (row + 1) * slots)
            scaled, inverse = norm_stats(acc_ref[at, :])
            xhat_out[at, :] = scaled.astype(bf16)
            inv_out[at, :] = inverse
            final = scaled * line(gain) + line(shift)
            high, low = split_low(final)
            seg = segment_of(lens_ref, row, lax.broadcasted_iota(jnp.int32, (slots, length), 1))
            member = (seg == lax.broadcasted_iota(jnp.int32, (slots, length), 0)).astype(f32)
            count = jnp.maximum(jnp.sum(member, axis=-1, keepdims=True), 1.0)
            member = member.astype(bf16)
            pooled = (dot(member, high) + dot(member, low)) / count
            pool_out[own, :] = pooled
            norm_sq = jnp.sum(pooled * pooled, axis=-1, keepdims=True)
            unit_out[own, :width] = (pooled * lax.rsqrt(norm_sq + pool_eps)).astype(bf16)
        unit_out[:, width:] = marks[...]


def feed(lens, low, first, wu, bu, wd, bd, gain, shift, marks):
    tokens, width = low.shape
    hidden = wu.shape[1]
    slots = lens.size
    chunk = 512
    vec = whole((width,))
    full = whole((tokens, width))
    act = pl.BlockSpec((tokens, chunk), lambda j: (0, j))
    return pl.pallas_call(
        feed_kernel,
        grid=(hidden // chunk,),
        in_specs=[
            smem(), full, full, pl.BlockSpec((width, chunk), lambda j: (0, j)),
            pl.BlockSpec((chunk,), lambda j: (j,)),
            pl.BlockSpec((chunk, width), lambda j: (j, 0)), vec, vec, vec, whole((slots, 128)),
        ],
        out_specs=[act, act, full, whole((tokens, 1)), whole((slots, width)), whole((slots, width + 128))],
        out_shape=[
            shaped((tokens, hidden), bf16),
            shaped((tokens, hidden), bf16),
            shaped((tokens, width), bf16),
            shaped((tokens, 1), f32),
            shaped((slots, width), f32),
            shaped((slots, width + 128), bf16),
        ],
        scratch_shapes=[pltpu.VMEM((tokens, width), f32)],
        compiler_params=params(60 << 20),
        cost_estimate=cost(4 * tokens * width * hidden, 30 << 20),
        name="feed",
    )(lens, low, first, wu, bu, wd, bd, gain, shift, marks)


def match_kernel(
    place_ref, lens_ref, rows_ref, pool_ref, xhat_ref, inv_ref, gain, active_hbm,
    loss_out, grad_out, vec_out, send_out, active_ref, sem,
):
    copy = pltpu.make_async_copy(active_hbm, active_ref, sem)
    copy.start()
    width = pool_ref.shape[1]
    slots = pool_ref.shape[0]
    rows, row_slots = lens_ref.shape
    length = xhat_ref.shape[0] // rows
    total = rows_ref.shape[1]
    outer = total // 4 // slots
    spot = lax.broadcasted_iota(jnp.int32, (1, total), 1)
    group = spot // slots
    cores, sides, outers = group // (2 * outer), group // outer % 2, group % outer
    device = (place_ref[4] ^ outers) * 2 + (place_ref[3] ^ sides)
    numbers = ((place_ref[1] ^ cores) * (2 * outer) + device) * slots + spot % slots
    passage_side = place_ref[0]
    query_side = 1 - passage_side
    chunk = min(512, total)
    lane = lax.broadcasted_iota(jnp.int32, (8, 128), 1)
    passage_marks = rows_ref[passage_side, :, width:]
    passage_live = dot_rows((lane == 0).astype(bf16), passage_marks)[:1] > 0
    query_count = jnp.sum(rows_ref[query_side, :, width:][:, :1].astype(f32))
    per_query = 1.0 / query_count

    def part(i, carry):
        loss, as_query, as_passage = carry
        at = pl.ds(pl.multiple_of(i * chunk, chunk), chunk)
        marks = rows_ref[query_side, at, width:].astype(f32)
        live = marks[:, 0:1] > 0
        target = marks[:, 1:2].astype(jnp.int32) * 64 + marks[:, 2:3].astype(jnp.int32)
        queries = rows_ref[query_side, at, :width]
        passages = rows_ref[passage_side, :, :width]
        scores = dot_rows(queries, passages) * inverse_temp
        scores = jnp.where(passage_live, scores, masked_score)
        top = jnp.max(scores, axis=-1, keepdims=True)
        log_sum = top + jnp.log(jnp.sum(jnp.exp(scores - top), axis=-1, keepdims=True))
        is_target = numbers == target
        picked = jnp.sum(jnp.where(is_target, scores, 0.0), axis=-1, keepdims=True)
        loss = loss + jnp.sum(jnp.where(live, log_sum - picked, 0.0))
        chances = jnp.where(passage_live, jnp.exp(scores - log_sum), 0.0)
        grad = jnp.where(live, (chances - is_target.astype(f32)) * per_query, 0.0).astype(bf16)
        as_passage = as_passage + dot_cols(grad[:, :128], queries)[:slots]
        own = dot(grad[:slots], passages)
        as_query = jnp.where(i == 0, own, as_query)
        return loss, as_query, as_passage

    zeros = jnp.zeros((slots, width), f32)
    carry = (jnp.float32(0), zeros, zeros)
    if total == chunk:
        carry = part(0, carry)
    else:
        carry = lax.fori_loop(0, total // chunk, part, carry)
    loss, as_query, as_passage = carry
    loss_out[0, 0] = loss * per_query
    grad_unit = jnp.where(passage_side == 1, as_query, as_passage) * inverse_temp
    pooled = pool_ref[...]
    inverse = lax.rsqrt(jnp.sum(pooled * pooled, axis=-1, keepdims=True) + pool_eps)
    along = jnp.sum(grad_unit * pooled, axis=-1, keepdims=True)
    grad_pooled = inverse * grad_unit - pooled * (inverse * inverse * inverse) * along
    gain = line(gain)
    sums = []
    for row in range(rows):
        at = slice(row * length, (row + 1) * length)
        own = slice(row * row_slots, (row + 1) * row_slots)
        seg = segment_of(lens_ref, row, lax.broadcasted_iota(jnp.int32, (row_slots, length), 1))
        member = (seg == lax.broadcasted_iota(jnp.int32, (row_slots, length), 0)).astype(f32)
        count = jnp.maximum(jnp.sum(member, axis=-1, keepdims=True), 1.0)
        member = member.astype(bf16)
        high, low = split_low(grad_pooled[own] / count)
        grad_final = dot_cols(member, high) + dot_cols(member, low)
        scaled = xhat_ref[at, :].astype(f32)
        grad_sum = norm_back(grad_final, scaled, inv_ref[at, :], gain)
        grad_low = grad_sum.astype(bf16)
        grad_out[at, :] = grad_low
        sums.append(
            (
                jnp.sum(grad_final * scaled, axis=0, keepdims=True),
                jnp.sum(grad_final, axis=0, keepdims=True),
                jnp.sum(grad_low.astype(f32), axis=0, keepdims=True),
            )
        )
    for i in range(3):
        vec_out[i : i + 1, :] = sum(each[i] for each in sums)
    copy.wait()
    parts, sides, half, share = send_out.shape
    other = grad_out[:, pl.ds(pl.multiple_of(place_ref[5] * half, half), half)]
    for z in range(parts):
        for y in range(sides):
            at = slice((z * sides + y) * share, (z * sides + y + 1) * share)
            send_out[z, y] = dot_cols(other, active_ref[:, at]).astype(bf16)


def match(place, lens, rows, pooled, xhat, inverse, gain, active):
    tokens, width = xhat.shape
    slots = pooled.shape[0]
    vmem = pl.BlockSpec(memory_space=pltpu.VMEM)
    return pl.pallas_call(
        match_kernel,
        in_specs=[smem(), smem()] + [vmem] * 4 + [vmem, pl.BlockSpec(memory_space=pl.ANY)],
        out_specs=[smem()] + [vmem] * 3,
        out_shape=[
            shaped((1, 1), f32),
            shaped((tokens, width), bf16),
            shaped((8, width), f32),
            shaped((4, 2, width // 2, active.shape[1] // 8), bf16),
        ],
        scratch_shapes=[
            pltpu.VMEM(active.shape, bf16),
            pltpu.SemaphoreType.DMA,
        ],
        compiler_params=params(60 << 20),
        cost_estimate=cost(2e9, 10 << 20),
        name="match",
    )(place, lens, rows, pooled, xhat, inverse, gain, active)


def hidden_kernel(grad_ref, slope_ref, wd, hidden_out, bias_out):
    grad = dot_rows(grad_ref[...], wd[...]) * slope_ref[...].astype(f32)
    grad_low = grad.astype(bf16)
    hidden_out[...] = grad_low
    bias_out[...] = jnp.sum(grad_low.astype(f32), axis=0, keepdims=True)


def hidden_grad(grad, slope, wd):
    tokens, width = grad.shape
    hidden = wd.shape[0]
    chunk = 768
    act = pl.BlockSpec((tokens, chunk), lambda j: (0, j))
    return pl.pallas_call(
        hidden_kernel,
        grid=(hidden // chunk,),
        in_specs=[whole((tokens, width)), act, pl.BlockSpec((chunk, width), lambda j: (j, 0))],
        out_specs=[act, pl.BlockSpec((1, chunk), lambda j: (0, j))],
        out_shape=[shaped((tokens, hidden), bf16), shaped((1, hidden), f32)],
        compiler_params=params(28 << 20),
        cost_estimate=cost(2 * tokens * width * hidden, 18 << 20),
        name="hidden_grad",
    )(grad, slope, wd)


def feed_back_kernel(
    place_ref, grad_ref, hidden_ref, wu, wo, xhat_ref, inv_ref, gain, low_ref, mixed_ref,
    branch_out, mixed_out, vec_out, send_out, acc_ref,
):
    step = pl.program_id(0)
    steps = pl.num_programs(0)
    tokens, width = grad_ref.shape
    half = tokens // 2
    chunk = hidden_ref.shape[1]
    per = steps // 2

    @pl.when(step == 0)
    def _():
        acc_ref[...] = grad_ref[...].astype(f32)

    for part in range(2):
        at = slice(part * half, (part + 1) * half)
        acc_ref[at, :] += dot_rows(hidden_ref[at, :], wu[...])

    @pl.when(step // per == place_ref[5])
    def _():
        at = pl.ds(pl.multiple_of(step % per * chunk, chunk), chunk)
        send_out[:, at] = dot_cols(low_ref[...], hidden_ref[...]).astype(bf16)

    @pl.when(step == steps - 1)
    def _():
        tallies = []
        for part in range(2):
            at = slice(part * half, (part + 1) * half)
            grad = acc_ref[at, :]
            scaled = xhat_ref[at, :].astype(f32)
            grad_low = norm_back(grad, scaled, inv_ref[at, :], line(gain)).astype(bf16)
            branch_out[at, :] = grad_low
            mixed_out[at, :] = dot_rows(grad_low, wo[...]).astype(bf16)
            tallies.append(
                (
                    jnp.sum(grad * scaled, axis=0, keepdims=True),
                    jnp.sum(grad, axis=0, keepdims=True),
                    jnp.sum(grad_low.astype(f32), axis=0, keepdims=True),
                )
            )
        for i in range(3):
            vec_out[i : i + 1, :] = tallies[0][i] + tallies[1][i]
        narrow = width // 2
        other = branch_out[:, pl.ds(pl.multiple_of(place_ref[5] * narrow, narrow), narrow)]
        send_out[:, send_out.shape[1] - narrow :] = dot_cols(mixed_ref[...], other).astype(bf16)


def feed_back(place, grad, grad_hidden, wu, wo, xhat, inverse, gain, low, mixed):
    tokens, width = grad.shape
    hidden = wu.shape[1]
    chunk = 768
    full = whole((tokens, width))
    total = hidden // 2 + width // 2
    return pl.pallas_call(
        feed_back_kernel,
        grid=(hidden // chunk,),
        in_specs=[
            smem(), full, pl.BlockSpec((tokens, chunk), lambda j: (0, j)),
            pl.BlockSpec((width, chunk), lambda j: (0, j)), whole((width, width)), full,
            whole((tokens, 1)), whole((width,)), full, full,
        ],
        out_specs=[full, full, whole((8, width)), whole((width, total))],
        out_shape=[
            shaped((tokens, width), bf16),
            shaped((tokens, width), bf16),
            shaped((8, width), f32),
            shaped((width, total), bf16),
        ],
        scratch_shapes=[pltpu.VMEM((tokens, width), f32)],
        compiler_params=params(40 << 20),
        cost_estimate=cost(4 * tokens * width * hidden, 25 << 20),
        name="feed_back",
    )(place, grad, grad_hidden, wu, wo, xhat, inverse, gain, low, mixed)


def attend_back_kernel(
    place_ref, lens_ref, q_ref, k_ref, v_ref, lse_ref, mixed_ref, grad_ref, x_ref,
    out, vec_out, send_out, mask_ref,
):
    step = pl.program_id(0)
    rows, length, _ = mask_ref.shape

    @pl.when(step == 0)
    def _():
        fill_mask(lens_ref, mask_ref)

    lane = lax.broadcasted_iota(jnp.int32, (1, 128), 1)
    scale = 64 ** (-0.5)
    pairs = q_ref.shape[1] // 128
    for pair in range(pairs):
        lanes = slice(pair * 128, (pair + 1) * 128)
        query_sums, value_sums = [], []
        for row in range(rows):
            tokens = slice(row * length, (row + 1) * length)
            q = q_ref[tokens, lanes] * bf16(scale)
            k = k_ref[tokens, lanes]
            v = v_ref[tokens, lanes]
            grad = grad_ref[tokens, lanes]
            high, low = split_low(grad.astype(f32) * mixed_ref[tokens, lanes].astype(f32))
            grad_v = grad_k = grad_q = 0.0
            for head in range(2):
                mine = (lane < 64) == (head == 0)
                ones = jnp.broadcast_to(jnp.where(mine, 1.0, 0.0), (8, 128)).astype(bf16)
                inner = (dot_rows(ones, high) + dot_rows(ones, low))[:1]
                log_total = lse_ref[row, pl.ds((step * pairs + pair) * 2 + head, 1), :]
                own_q = jnp.where(mine, q, bf16(0))
                own_grad = jnp.where(mine, grad, bf16(0))
                scores = dot_rows(k, own_q) + mask_ref[row]
                probs = jnp.exp(scores - log_total)
                grad_scores = (probs * (dot_rows(v, own_grad) - inner)).astype(bf16)
                grad_v = grad_v + dot(probs.astype(bf16), own_grad)
                grad_k = grad_k + dot(grad_scores, own_q)
                grad_q = grad_q + dot_cols(jnp.where(mine, k, bf16(0)), grad_scores)
            grad_q = (jnp.transpose(grad_q) * scale).astype(bf16)
            grad_v = grad_v.astype(bf16)
            out[0, tokens, lanes] = grad_q
            out[1, tokens, lanes] = grad_k.astype(bf16)
            out[2, tokens, lanes] = grad_v
            query_sums.append(jnp.sum(grad_q.astype(f32), axis=0, keepdims=True))
            value_sums.append(jnp.sum(grad_v.astype(f32), axis=0, keepdims=True))
        vec_out[0:1, lanes] = sum(query_sums)
        vec_out[1:2, lanes] = sum(value_sums)
    other = pl.ds(pl.multiple_of(place_ref[5] * 128, 128), 128)
    grads = jnp.concatenate([out[i, :, other] for i in range(3)], axis=1)
    send_out[...] = dot_cols(x_ref[...], grads).astype(bf16)


def attend_back(place, lens, q, k, v, lse, mixed, grad, x):
    tokens, width = q.shape
    rows = lens.shape[0]
    length = tokens // rows
    group = 256
    act = pl.BlockSpec((tokens, group), lambda j: (0, j))
    return pl.pallas_call(
        attend_back_kernel,
        grid=(width // group,),
        in_specs=[smem(), smem(), act, act, act, whole(lse.shape), act, act, whole(x.shape)],
        out_specs=[
            pl.BlockSpec((3, tokens, group), lambda j: (0, 0, j)),
            pl.BlockSpec((8, group), lambda j: (0, j)),
            pl.BlockSpec((width, 384), lambda j: (0, j)),
        ],
        out_shape=[
            shaped((3, tokens, width), bf16),
            shaped((8, width), f32),
            shaped((width, width // group * 384), bf16),
        ],
        scratch_shapes=[pltpu.VMEM((rows, length, length), f32)],
        compiler_params=params(40 << 20),
        cost_estimate=cost(20 * tokens * length * width, 15 << 20),
        name="attend_back",
    )(place, lens, q, k, v, lse, mixed, grad, x)


def input_kernel(branch_ref, grads_ref, wq, wk, wv, out):
    out[...] = (
        branch_ref[...].astype(f32)
        + dot_rows(grads_ref[0], wq[...])
        + dot_rows(grads_ref[1], wk[...])
        + dot_rows(grads_ref[2], wv[...])
    )


def input_grad(branch, grads, wq, wk, wv):
    tokens, width = branch.shape
    part = tokens // 4
    weight = whole((width, width))
    rows = pl.BlockSpec((part, width), lambda j: (j, 0))
    return pl.pallas_call(
        input_kernel,
        grid=(4,),
        in_specs=[rows, pl.BlockSpec((3, part, width), lambda j: (0, j, 0)), weight, weight, weight],
        out_specs=rows,
        out_shape=shaped((tokens, width), f32),
        compiler_params=params(20 << 20),
        cost_estimate=cost(6 * tokens * width * width, 13 << 20),
        name="input_grad",
    )(branch, grads, wq, wk, wv)


def down_kernel(place_ref, left_ref, right_ref, got_ref, *refs):
    outs, acc_ref = refs[:-1], refs[-1]
    share = right_ref.shape[1] // 2
    half = left_ref.shape[1] // 2
    for y in range(2):
        lanes = slice(y * share, (y + 1) * share)
        acc_ref[...] = dot_cols(left_ref[...], right_ref[:, lanes]) + got_ref[0, y].astype(f32)
        for rel, out in enumerate(outs):
            at = pl.multiple_of((place_ref[2] ^ (rel >> 1)) * half, half)

            @pl.when(place_ref[3] == y ^ (rel & 1))
            def _():
                out[0] = acc_ref[pl.ds(at, half), :].astype(bf16)


def down_grad(place, grad, active, got):
    tokens, width = grad.shape
    hidden = active.shape[1]
    half, parts = width // 2, 4
    share = hidden // parts // 2
    piece = pl.BlockSpec((1, half // 2, share), lambda z, s: (z, 0, 0))
    piece_shape = shaped((parts, half // 2, share), bf16)
    return pl.pallas_call(
        down_kernel,
        grid_spec=pltpu.PrefetchScalarGridSpec(
            num_scalar_prefetch=1,
            grid=(parts,),
            in_specs=[
                pl.BlockSpec((tokens, half), lambda z, s: (0, s[1])),
                pl.BlockSpec((tokens, 2 * share), lambda z, s: (0, z)),
                pl.BlockSpec((1, 2, half, share), lambda z, s: (z, 0, 0, 0)),
            ],
            out_specs=[piece] * 4,
            scratch_shapes=[pltpu.VMEM((half, share), f32)],
        ),
        out_shape=[piece_shape] * 4,
        compiler_params=params(20 << 20),
        cost_estimate=cost(2 * half * tokens * hidden, 12 << 20),
        name="down_keep",
    )(place, grad, active, got)


def cut_rows(place_ref, acc_ref, sends, at, size, mode):
    outer = acc_ref.shape[0] // 4 // size
    for rel, out in enumerate(sends):
        for z in range(outer):
            if mode == "y":
                for x in range(2):
                    row = ((z * 2 + (place_ref[3] ^ rel)) * 2 + x) * size
                    row = pl.multiple_of(row, size)
                    out[x, z, :, at] = acc_ref[pl.ds(row, size), :].astype(bf16)
            else:
                row = ((z * 2 + (place_ref[3] ^ (rel & 1))) * 2 + (place_ref[2] ^ (rel >> 1))) * size
                row = pl.multiple_of(row, size)
                out[z, :, at] = acc_ref[pl.ds(row, size), :].astype(bf16)


def up_kernel(
    place_ref, low_ref, mixed_ref, hidden_ref, branch_ref, got_ref, *refs
):
    outs, acc_ref = refs[:-1], refs[-1]
    step = pl.program_id(0)
    steps = pl.num_programs(0)
    wide = hidden_ref.shape[1]
    narrow = branch_ref.shape[1]
    size = outs[0].shape[1]

    def done(result, at, span):
        acc_ref[:, :span] = result + got_ref[:, at].astype(f32)
        cut_rows(place_ref, acc_ref.at[:, :span], outs, at, size, "xy")

    @pl.when(step < steps - 1)
    def _():
        at = pl.ds(pl.multiple_of(step * wide, wide), wide)
        done(dot_cols(low_ref[...], hidden_ref[...]), at, wide)

    @pl.when(step == steps - 1)
    def _():
        last = outs[0].shape[-1] - narrow
        done(dot_cols(mixed_ref[...], branch_ref[...]), pl.ds(last, narrow), narrow)


def up_grad(place, low, mixed, hidden, branch, got):
    tokens, width = low.shape
    half = hidden.shape[1] // 2
    narrow = width // 2
    wide = half // 2
    total = half + narrow
    size = width // 16
    piece_shape = (4, size, total)
    full = whole((tokens, width))
    return pl.pallas_call(
        up_kernel,
        grid_spec=pltpu.PrefetchScalarGridSpec(
            num_scalar_prefetch=1,
            grid=(3,),
            in_specs=[
                full, full,
                pl.BlockSpec((tokens, wide), lambda j, s: (0, s[1] * 2 + jnp.minimum(j, 1))),
                pl.BlockSpec((tokens, narrow), lambda j, s: (0, s[1])),
                whole((width, total)),
            ],
            out_specs=[whole(piece_shape)] * 4,
            scratch_shapes=[pltpu.VMEM((width, wide), f32)],
        ),
        out_shape=[shaped(piece_shape, bf16)] * 4,
        compiler_params=params(28 << 20),
        cost_estimate=cost(2 * width * tokens * total, 12 << 20),
        name="up_keep",
    )(place, low, mixed, hidden, branch, got)


def head_kernel(place_ref, x_ref, grads_ref, vec_ref, got_vec_ref, got_ref, *refs):
    outs, acc_ref = refs[:-1], refs[-1]
    step = pl.program_id(0)
    steps = pl.num_programs(0)
    span = got_ref.shape[1]
    size = outs[0].shape[1]
    grads = jnp.concatenate([grads_ref[i] for i in range(3)], axis=1)
    acc_ref[...] = dot_cols(x_ref[...], grads) + got_ref[...].astype(f32)
    at = pl.ds(pl.multiple_of(step * span, span), span)
    cut_rows(place_ref, acc_ref, outs, at, size, "xy")

    @pl.when(step == steps - 1)
    def _():
        acc_ref[:, :128] = vec_ref[0].astype(f32) + got_vec_ref[...].astype(f32)
        tail = pl.ds(outs[0].shape[2] - 128, 128)
        cut_rows(place_ref, acc_ref.at[:, :128], outs, tail, size, "xy")


def head_grad(place, x, grads, vectors, got_vectors, got):
    tokens, width = x.shape
    groups = width // 256
    total = groups * 384 + 128
    size = width // 16
    piece_shape = (4, size, total)
    return pl.pallas_call(
        head_kernel,
        grid_spec=pltpu.PrefetchScalarGridSpec(
            num_scalar_prefetch=1,
            grid=(groups,),
            in_specs=[
                whole((tokens, width)),
                pl.BlockSpec((3, tokens, 128), lambda j, s: (0, 0, 2 * j + s[1])),
                pl.BlockSpec((1, width, 128), lambda j, s: (s[1], 0, 0)),
                whole((width, 128)),
                pl.BlockSpec((width, 384), lambda j, s: (0, j)),
            ],
            out_specs=[whole(piece_shape)] * 4,
            scratch_shapes=[pltpu.VMEM((width, 384), f32)],
        ),
        out_shape=[shaped(piece_shape, bf16)] * 4,
        compiler_params=params(24 << 20),
        cost_estimate=cost(2 * width * tokens * total, 9 << 20),
        name="head_keep",
    )(place, x, grads, vectors, got_vectors, got)


def mix_kernel(which, parts, place_ref, *refs):
    ins, outs = refs[:-parts], refs[-parts:]
    for rel, out in enumerate(outs):
        at = place_ref[which] ^ rel if parts > 1 else 0
        total = ins[0][at].astype(f32)
        for ref in ins[1:]:
            total = total + ref[at].astype(f32)
        out[...] = total.astype(bf16)


def mix(place, which, arrays):
    parts = arrays[0].shape[0]
    return pl.pallas_call(
        partial(mix_kernel, which, parts),
        in_specs=[smem()] + [pl.BlockSpec(memory_space=pltpu.VMEM)] * len(arrays),
        out_specs=[pl.BlockSpec(memory_space=pltpu.VMEM)] * parts,
        out_shape=[shaped(arrays[0].shape[1:], bf16)] * parts,
        compiler_params=params(12 << 20),
        cost_estimate=cost(0, 2 * arrays[0].size * (len(arrays) + 1)),
        name="mix",
    )(place, *arrays)


def exchange(parts):
    return [parts[0]] + [swap_both(parts[rel], 2 * (rel >> 1), rel & 1) for rel in range(1, 4)]


def cut_outer(place, arrays):
    return mix(place, 4, arrays)


def exchange_outer(parts):
    return [parts[0]] + [swap(part, "dp", 2 * rel) for rel, part in enumerate(parts) if rel]


def join_outer(place, parts):
    return mix(place, 4, [part[None] for part in parts])[0]


def spread_kernel(kind, place_ref, *refs):
    blocks, outs = refs[:4], refs[4:]
    core, far = place_ref[1], place_ref[2]
    for i, block in enumerate(blocks):
        c, x = core ^ (i >> 1), far ^ (i & 1)
        value = block[...].astype(f32)
        size = value.shape[0]
        rows = pl.ds(pl.multiple_of(x * size, size), size)
        if kind == "down":
            at = pl.multiple_of((c * 2 + x) * size, size)
            outs[0][pl.ds(at, size), :] = value
            continue
        half = outs[1].shape[1] // 2
        if kind == "up":
            total = outs[0].shape[1] // 2
            wide = pl.ds(pl.multiple_of(c * total, total), total)
            narrow = pl.ds(pl.multiple_of(c * half, half), half)
            outs[0][rows, wide] = value[:, :total]
            outs[1][rows, narrow] = value[:, total:]
        else:
            groups = half // 128
            for j in range(groups):
                lanes = pl.ds(pl.multiple_of(j * 256 + c * 128, 128), 128)
                for m in range(3):
                    outs[m][rows, lanes] = value[:, (j * 3 + m) * 128 : (j * 3 + m + 1) * 128]
            outs[3][c * 2 + x] = value[:16, 3 * half :]


def spread(place, kind, block, shapes):
    far = swap(block, "tower", 2)
    blocks = [block, far, swap(block, "tower", 1), swap(far, "tower", 1)]
    return pl.pallas_call(
        partial(spread_kernel, kind),
        in_specs=[smem()] + [pl.BlockSpec(memory_space=pltpu.VMEM)] * 4,
        out_specs=[pl.BlockSpec(memory_space=pltpu.VMEM)] * len(shapes),
        out_shape=[shaped(shape, f32) for shape in shapes],
        compiler_params=params(12 << 20),
        cost_estimate=cost(0, 2 << 20),
        name="spread_" + kind,
    )(place, *blocks)


def shards(
    layer_input,
    seg_lengths,
    positives,
    query_weight,
    key_weight,
    value_weight,
    out_weight,
    up_weight,
    down_weight,
    query_bias,
    value_offset_bias,
    out_bias,
    up_bias,
    down_bias,
    first_gain,
    first_shift,
    second_gain,
    latter_norm_translation,
):
    row_count = layer_input.shape[1]
    row_len = layer_input.shape[2]
    width = layer_input.shape[3]
    slot_count = seg_lengths.shape[2]
    token_count = row_count * row_len
    slot_total = row_count * slot_count
    tower_index = lax.axis_index("tower")
    dp_index = lax.axis_index("dp")
    dp_count = lax.axis_size("dp")
    core, far = tower_index & 1, tower_index >> 1
    place = jnp.stack([1 - far, core, far, dp_index & 1, dp_index >> 1, 1 - core]).astype(jnp.int32)
    flat_in = layer_input.reshape(token_count, width)
    lens = seg_lengths.reshape(row_count, slot_count)

    own_targets = lax.dynamic_index_in_dim(positives, core, 0, keepdims=False).reshape(slot_total)
    live_slot = (lens > 0).reshape(slot_total).astype(jnp.int32)
    marks = jnp.stack([live_slot, own_targets // 64, own_targets % 64], axis=-1).astype(bf16)
    marks = jnp.pad(marks, ((0, 0), (0, 125)))

    q, k, v, mixed, lse, first, low, first_scaled, first_inverse = attend(
        lens, flat_in, query_weight, key_weight, value_weight, out_weight,
        query_bias, value_offset_bias, out_bias, first_gain, first_shift,
    )
    active, slope, second_scaled, second_inverse, pooled, unit = feed(
        lens, low, first, up_weight, up_bias, down_weight, down_bias,
        second_gain, latter_norm_translation, marks,
    )
    rows = gather_all(unit).reshape(2, -1, width + 128)
    loss, grad_second, second_sums, down_half = match(
        place, lens, rows, pooled, second_scaled, second_inverse, second_gain, active
    )
    loss = loss.reshape(())
    share = width // dp_count
    fast = dp_count == 8 and lax.axis_size("tower") == 4
    grad_hidden, up_sums = hidden_grad(grad_second, slope, down_weight)
    if fast:
        got = swap(down_half, "tower", 1)
        got, grad_hidden = lax.optimization_barrier((got, grad_hidden))
        down_parts = down_grad(place, grad_second, active, got)
        *down_parts, grad_hidden = lax.optimization_barrier((*down_parts, grad_hidden))
        down_parts = exchange(down_parts)
    grad_branch, grad_mixed, first_sums, up_half = feed_back(
        place, grad_second, grad_hidden, up_weight, out_weight, first_scaled, first_inverse,
        first_gain, low, mixed,
    )
    if fast:
        *down_parts, up_half = lax.optimization_barrier((*down_parts, up_half))
        down_parts = cut_outer(place, down_parts)
        got = swap(up_half, "tower", 1)
        *down_parts, got = lax.optimization_barrier((*down_parts, got))
        down_parts = exchange_outer(down_parts)
        up_parts = up_grad(place, low, mixed, grad_hidden, grad_branch, got)
        *up_parts, grad_mixed = lax.optimization_barrier((*up_parts, grad_mixed))
        up_parts = exchange(up_parts)
        *down_parts, grad_mixed = lax.optimization_barrier((*down_parts, grad_mixed))
        down_part = join_outer(place, down_parts)
    grads, head_sums, head_half = attend_back(
        place, lens, q, k, v, lse, mixed, grad_mixed, flat_in
    )
    if fast:
        *up_parts, grads, head_half, head_sums = lax.optimization_barrier(
            (*up_parts, grads, head_half, head_sums)
        )
    vectors = jnp.concatenate(
        [
            vec.reshape(dp_count, -1)
            for vec in (
                head_sums[0],
                head_sums[1],
                first_sums[2],
                second_sums[2],
                first_sums[0],
                first_sums[1],
                second_sums[0],
                second_sums[1],
                up_sums,
            )
        ],
        axis=1,
    ).astype(bf16)
    if fast:
        vectors = vectors.reshape(dp_count, 2, 2, -1).transpose(1, 0, 2, 3)
        vectors = jnp.pad(vectors, ((0, 0),) * 3 + ((0, width // 16 * 128 - vectors.shape[-1]),))
        vectors = vectors.reshape(2, width, 128)
        got = swap(head_half, "tower", 1)
        got_vectors = swap(pick(vectors, 1 - core), "tower", 1)
        up_parts = cut_outer(place, up_parts)
        *up_parts, got = lax.optimization_barrier((*up_parts, got))
        up_parts = exchange_outer(up_parts)
        parts = head_grad(place, flat_in, grads, vectors, got_vectors, got)
        *parts, grad_branch = lax.optimization_barrier((*parts, grad_branch))
        parts = exchange(parts)
        up_part = join_outer(place, up_parts)
        head_part = join_outer(place, exchange_outer(cut_outer(place, parts)))
        (down_turned,) = spread(place, "down", down_part, [(width, 4 * share)])
        total_down = down_turned.T
        total_up, total_out = spread(
            place, "up", up_part, [(share, up_weight.shape[1]), (share, width)]
        )
        total_query, total_key, total_value, short = spread(
            place, "head", head_part, [(share, width)] * 3 + [(4, 16, 128)]
        )
        short = short.reshape(4, -1)[:, : share * 3].reshape(-1)
    else:
        outer = dp_count // 2

        def by_rows(grad):
            return grad.astype(bf16).reshape(outer, 2, share, 2, 2, width).transpose(3, 4, 1, 0, 2, 5)

        square = jnp.stack(
            [dot_cols(flat_in, grads[i]) for i in range(3)] + [dot_cols(mixed, grad_branch)], axis=1
        )
        vectors = vectors.reshape(outer, 2, 2, 2, -1).transpose(2, 3, 1, 0, 4)
        vectors = jnp.pad(vectors, ((0, 0),) * 4 + ((0, width - vectors.shape[-1]),))
        down = dot_cols(active, grad_second).astype(bf16)
        down = down.reshape(outer, 2, 2, 2, share, width).transpose(2, 3, 1, 0, 4, 5)
        total_down = sum_group(down).reshape(4 * share, width)
        total_up = sum_group(by_rows(dot_cols(low, grad_hidden))).reshape(4, share, width)
        total_up = total_up.transpose(1, 0, 2).reshape(share, 4 * width)
        last = jnp.concatenate([by_rows(square), vectors[:, :, :, :, None]], axis=4)
        last = sum_group(last).reshape(4, share + 1, width)
        total_query, total_key, total_value, total_out = [last[i, :share] for i in range(4)]
        short = last[:, share, : share * 3].reshape(-1)
    grad_input = input_grad(grad_branch, grads, query_weight, key_weight, value_weight)
    grad_input = grad_input.reshape(layer_input.shape)
    (
        total_query_bias,
        total_value_bias,
        total_out_bias,
        total_down_bias,
        total_first_gain,
        total_first_shift,
        total_second_gain,
        total_second_shift,
    ) = [short[i * share : (i + 1) * share] for i in range(8)]
    total_up_bias = short[8 * share :]
    return (
        loss,
        grad_input,
        total_query,
        total_key,
        total_value,
        total_out,
        total_up,
        total_down,
        total_query_bias,
        total_value_bias,
        total_out_bias,
        total_up_bias,
        total_down_bias,
        total_first_gain,
        total_first_shift,
        total_second_gain,
        total_second_shift,
    )


def solution(mesh):
    in_specs = (P("tower", "dp", None, None), P("tower", "dp", None), P(None, "dp", None)) + (P(),) * 15
    out_specs = (P(), P("tower", "dp", None, None)) + (P("dp", None),) * 6 + (P("dp"),) * 9
    return jax.shard_map(shards, mesh=mesh, in_specs=in_specs, out_specs=out_specs, check_vma=False)
```

```python
from functools import partial

import jax
import jax.numpy as jnp
from jax import lax
from jax.experimental import pallas as pl
from jax.experimental.pallas import tpu as pltpu
from jax.sharding import PartitionSpec as P

H = 12

inverse_temp = 100.0
norm_eps = 1e-06
pool_eps = 1e-06
masked_score = -1e30
f32 = jnp.float32
bf16 = jnp.bfloat16


def swap(value, axis, bits):
    count = lax.axis_size(axis)
    return lax.ppermute(value, axis, [(place, place ^ bits) for place in range(count)])


def swap_both(value, tower_bits, dp_bits):
    if not tower_bits:
        return swap(value, "dp", dp_bits)
    if not dp_bits:
        return swap(value, "tower", tower_bits)
    towers = lax.axis_size("tower")
    total = towers * lax.axis_size("dp")
    moves = [(place, place ^ (dp_bits * towers + tower_bits)) for place in range(total)]
    return lax.ppermute(value, ("dp", "tower"), moves)


def outer_bits():
    outer = lax.axis_size("dp") // 2
    return [1 << k for k in range(outer.bit_length() - 1)]


def gather_all(block):
    outer = lax.axis_size("dp") // 2
    if outer <= 4:
        blocks = jnp.stack([block] + [swap(block, "dp", 2 * k) for k in range(1, outer)])
    else:
        blocks = block[None]
        for bit in outer_bits():
            blocks = jnp.concatenate([blocks, swap(blocks, "dp", 2 * bit)])
    sides = [swap_both(blocks, 2 * x, y) if x or y else blocks for x in range(2) for y in range(2)]
    blocks = jnp.stack(sides).reshape((2, 2) + blocks.shape)
    return jnp.stack([blocks, swap(blocks, "tower", 1)], axis=1)


def pick(value, index):
    return lax.dynamic_index_in_dim(value, index, 0, keepdims=False)


def add_up(parts):
    total = parts[0].astype(f32)
    for part in parts[1:]:
        total = total + part.astype(f32)
    return total


def sum_group(blocks):
    tower_index = lax.axis_index("tower")
    dp_index = lax.axis_index("dp")
    core, far = tower_index & 1, tower_index >> 1
    side, place = dp_index & 1, dp_index >> 1
    got = swap(pick(blocks, 1 - core), "tower", 1)
    blocks = add_up([pick(blocks, core), got]).astype(bf16)
    blocks = blocks.reshape((4,) + blocks.shape[2:])
    own = far * 2 + side
    parts = [pick(blocks, own)]
    for rel in range(1, 4):
        parts.append(swap_both(pick(blocks, own ^ rel), 2 * (rel >> 1), rel & 1))
    blocks = add_up(parts).astype(bf16)
    for bit in reversed(outer_bits()):
        halves = blocks.reshape((2, bit) + blocks.shape[1:])
        mine = jnp.where(place & bit, 1, 0)
        got = swap(pick(halves, 1 - mine), "dp", 2 * bit)
        blocks = add_up([pick(halves, mine), got]).astype(bf16)
    low = blocks[0]
    got = swap(low, "tower", 2)
    pair = jnp.where(far == 0, jnp.stack([low, got]), jnp.stack([got, low]))
    got = swap(pair, "tower", 1)
    every = jnp.where(core == 0, jnp.stack([pair, got]), jnp.stack([got, pair]))
    return every.astype(f32)


def dot(left, right):
    return jnp.dot(left, right, preferred_element_type=f32)


def dot_rows(left, right):
    return lax.dot_general(left, right, (((1,), (1,)), ((), ())), preferred_element_type=f32)


def dot_cols(left, right):
    return lax.dot_general(left, right, (((0,), (0,)), ((), ())), preferred_element_type=f32)


def split_low(value):
    high = value.astype(bf16)
    return high, (value - high.astype(f32)).astype(bf16)


def segment_of(lens_ref, row, places):
    total = jnp.int32(0)
    seg = jnp.zeros(places.shape, jnp.int32)
    for slot in range(lens_ref.shape[1]):
        total = total + lens_ref[row, slot]
        seg = seg + (places >= total).astype(jnp.int32)
    return seg


def fill_mask(lens_ref, mask_ref):
    rows, length, _ = mask_ref.shape
    for row in range(rows):
        across = segment_of(lens_ref, row, lax.broadcasted_iota(jnp.int32, (1, length), 1))
        down = segment_of(lens_ref, row, lax.broadcasted_iota(jnp.int32, (length, 1), 0))
        mask_ref[row] = jnp.where(down == across, 0.0, masked_score)


def line(ref):
    return ref[...].reshape(1, -1).astype(f32)


def whole(shape):
    return pl.BlockSpec(shape, lambda *_: (0,) * len(shape))


def smem():
    return pl.BlockSpec(memory_space=pltpu.SMEM)


def shaped(shape, kind):
    return jax.ShapeDtypeStruct(shape, kind)


def params(limit):
    return pltpu.CompilerParams(vmem_limit_bytes=limit)


def cost(flops, moved):
    return pl.CostEstimate(flops=int(flops), bytes_accessed=int(moved), transcendentals=0)


def norm_stats(value):
    middle = jnp.mean(value, axis=-1, keepdims=True)
    centered = value - middle
    inverse = lax.rsqrt(jnp.mean(centered * centered, axis=-1, keepdims=True) + norm_eps)
    return centered * inverse, inverse


def norm_back(grad, scaled, inverse, gain):
    grad = grad * gain
    return inverse * (
        grad
        - jnp.mean(grad, axis=-1, keepdims=True)
        - scaled * jnp.mean(grad * scaled, axis=-1, keepdims=True)
    )


def attend_kernel(
    lens_ref, x_ref, wq, wk, wv, wo, bq, bv, bo, gain, shift,
    q_out, k_out, v_out, mixed_out, lse_out, first_out, low_out, xhat_out, inv_out,
    mask_ref, acc_ref,
):
    step = pl.program_id(0)
    steps = pl.num_programs(0)
    rows, length, _ = mask_ref.shape

    @pl.when(step == 0)
    def _():
        fill_mask(lens_ref, mask_ref)
        acc_ref[...] = x_ref[...].astype(f32) + line(bo)

    x = x_ref[...]
    q_out[...] = (dot(x, wq[...]) + line(bq)).astype(bf16)
    k_out[...] = dot(x, wk[...]).astype(bf16)
    v_out[...] = (dot(x, wv[...]) + line(bv)).astype(bf16)
    lane = lax.broadcasted_iota(jnp.int32, (1, 128), 1)
    first_half = lane < 64
    pairs = q_out.shape[1] // 128
    scale = bf16(64 ** (-0.5))
    for row in range(rows):
        for pair in range(pairs):
            tokens = slice(row * length, (row + 1) * length)
            lanes = slice(pair * 128, (pair + 1) * 128)
            q = q_out[tokens, lanes] * scale
            k = k_out[tokens, lanes]
            v = v_out[tokens, lanes]
            outs, logs = [], []
            for head in range(2):
                mine = first_half == (head == 0)
                scores = dot_rows(jnp.where(mine, q, bf16(0)), k) + mask_ref[row]
                top = jnp.max(scores, axis=-1, keepdims=True)
                shifted = jnp.exp(scores - top).astype(bf16)
                out = dot(shifted, jnp.where(mine, v, bf16(1)))
                total = pltpu.roll(out, 64, 1)
                outs.append(out / total)
                logs.append(top + jnp.log(jnp.where(mine, total, out)))
            mixed_out[tokens, lanes] = jnp.where(first_half, outs[0], outs[1]).astype(bf16)
            logs = jnp.transpose(jnp.where(first_half, logs[0], logs[1]))
            at = (step * pairs + pair) * 2
            lse_out[row, pl.ds(at, 1), :] = logs[0:1]
            lse_out[row, pl.ds(at + 1, 1), :] = logs[64:65]
    part = dot(mixed_out[...], wo[...])

    @pl.when(step < steps - 1)
    def _():
        acc_ref[...] += part

    @pl.when(step == steps - 1)
    def _():
        scaled, inverse = norm_stats(acc_ref[...] + part)
        first = scaled * line(gain) + line(shift)
        first_out[...] = first
        low_out[...] = first.astype(bf16)
        xhat_out[...] = scaled.astype(bf16)
        inv_out[...] = inverse


def attend(lens, x, wq, wk, wv, wo, bq, bv, bo, gain, shift):
    tokens, width = x.shape
    rows = lens.shape[0]
    length = tokens // rows
    group = 256
    cols = pl.BlockSpec((width, group), lambda j: (0, j))
    vec = whole((width,))
    act = pl.BlockSpec((tokens, group), lambda j: (0, j))
    full = whole((tokens, width))
    return pl.pallas_call(
        attend_kernel,
        grid=(width // group,),
        in_specs=[
            smem(), full, cols, cols, cols, pl.BlockSpec((group, width), lambda j: (j, 0)),
            pl.BlockSpec((group,), lambda j: (j,)), pl.BlockSpec((group,), lambda j: (j,)),
            vec, vec, vec,
        ],
        out_specs=[act] * 4 + [whole((rows, H, length)), full, full, full, whole((tokens, 1))],
        out_shape=[shaped((tokens, width), bf16)] * 4
        + [
            shaped((rows, H, length), f32),
            shaped((tokens, width), f32),
            shaped((tokens, width), bf16),
            shaped((tokens, width), bf16),
            shaped((tokens, 1), f32),
        ],
        scratch_shapes=[pltpu.VMEM((rows, length, length), f32), pltpu.VMEM((tokens, width), f32)],
        compiler_params=params(60 << 20),
        cost_estimate=cost(8 * tokens * width * width * 3, 20 << 20),
        name="attend",
    )(lens, x, wq, wk, wv, wo, bq, bv, bo, gain, shift)


def feed_kernel(
    place_ref, lens_ref, targets_ref, low_ref, first_ref, wu, bu, wd, bd, gain, shift,
    act_out, slope_out, xhat_out, inv_out, pool_out, unit_out, acc_ref,
):
    step = pl.program_id(0)
    steps = pl.num_programs(0)
    tokens, width = low_ref.shape
    rows, slots = lens_ref.shape
    length = tokens // rows

    @pl.when(step == 0)
    def _():
        acc_ref[...] = first_ref[...] + line(bd)

    for row in range(rows):
        at = slice(row * length, (row + 1) * length)
        hidden = dot(low_ref[at, :], wu[...]) + line(bu)
        share = 0.5 + 0.5 * lax.erf(hidden * 0.7071067811865476)
        bell = jnp.exp(hidden * hidden * -0.5) * 0.3989422804014327
        active = (hidden * share).astype(bf16)
        act_out[at, :] = active
        slope_out[at, :] = (share + hidden * bell).astype(bf16)
        acc_ref[at, :] += dot(active, wd[...])

    @pl.when(step == steps - 1)
    def _():
        for row in range(rows):
            at = slice(row * length, (row + 1) * length)
            own = slice(row * slots, (row + 1) * slots)
            scaled, inverse = norm_stats(acc_ref[at, :])
            xhat_out[at, :] = scaled.astype(bf16)
            inv_out[at, :] = inverse
            final = scaled * line(gain) + line(shift)
            high, low = split_low(final)
            seg = segment_of(lens_ref, row, lax.broadcasted_iota(jnp.int32, (slots, length), 1))
            member = (seg == lax.broadcasted_iota(jnp.int32, (slots, length), 0)).astype(f32)
            count = jnp.maximum(jnp.sum(member, axis=-1, keepdims=True), 1.0)
            member = member.astype(bf16)
            pooled = (dot(member, high) + dot(member, low)) / count
            pool_out[own, :] = pooled
            norm_sq = jnp.sum(pooled * pooled, axis=-1, keepdims=True)
            unit_out[own, :width] = (pooled * lax.rsqrt(norm_sq + pool_eps)).astype(bf16)
        spot = lax.broadcasted_iota(jnp.int32, (rows * slots, 128), 0)
        lane = lax.broadcasted_iota(jnp.int32, (rows * slots, 128), 1)
        marks = jnp.zeros((rows * slots, 128), jnp.int32)
        for row in range(rows):
            for slot in range(slots):
                live = (lens_ref[row, slot] > 0).astype(jnp.int32)
                target = targets_ref[place_ref[1], row, slot]
                mark = jnp.where(lane == 0, live, jnp.where(lane == 1, target >> 6, target & 63))
                marks = jnp.where((spot == row * slots + slot) & (lane < 3), mark, marks)
        unit_out[:, width:] = marks.astype(f32).astype(bf16)


def feed(place, lens, targets, low, first, wu, bu, wd, bd, gain, shift):
    tokens, width = low.shape
    hidden = wu.shape[1]
    slots = lens.size
    chunk = 512
    vec = whole((width,))
    full = whole((tokens, width))
    act = pl.BlockSpec((tokens, chunk), lambda j: (0, j))
    return pl.pallas_call(
        feed_kernel,
        grid=(hidden // chunk,),
        in_specs=[
            smem(), smem(), smem(), full, full, pl.BlockSpec((width, chunk), lambda j: (0, j)),
            pl.BlockSpec((chunk,), lambda j: (j,)),
            pl.BlockSpec((chunk, width), lambda j: (j, 0)), vec, vec, vec,
        ],
        out_specs=[act, act, full, whole((tokens, 1)), whole((slots, width)), whole((slots, width + 128))],
        out_shape=[
            shaped((tokens, hidden), bf16),
            shaped((tokens, hidden), bf16),
            shaped((tokens, width), bf16),
            shaped((tokens, 1), f32),
            shaped((slots, width), f32),
            shaped((slots, width + 128), bf16),
        ],
        scratch_shapes=[pltpu.VMEM((tokens, width), f32)],
        compiler_params=params(60 << 20),
        cost_estimate=cost(4 * tokens * width * hidden, 30 << 20),
        name="feed",
    )(place, lens, targets, low, first, wu, bu, wd, bd, gain, shift)


def match_kernel(
    place_ref, lens_ref, rows_ref, pool_ref, xhat_ref, inv_ref, gain, active_hbm,
    loss_out, grad_out, vec_out, send_out, active_ref, sem,
):
    copy = pltpu.make_async_copy(active_hbm, active_ref, sem)
    copy.start()
    width = pool_ref.shape[1]
    slots = pool_ref.shape[0]
    rows, row_slots = lens_ref.shape
    length = xhat_ref.shape[0] // rows
    total = rows_ref.shape[1]
    outer = total // 4 // slots
    spot = lax.broadcasted_iota(jnp.int32, (1, total), 1)
    group = spot // slots
    cores, sides, outers = group // (2 * outer), group // outer % 2, group % outer
    device = (place_ref[4] ^ outers) * 2 + (place_ref[3] ^ sides)
    numbers = ((place_ref[1] ^ cores) * (2 * outer) + device) * slots + spot % slots
    passage_side = place_ref[0]
    query_side = 1 - passage_side
    chunk = min(512, total)
    lane = lax.broadcasted_iota(jnp.int32, (8, 128), 1)
    passage_marks = rows_ref[passage_side, :, width:]
    passage_live = dot_rows((lane == 0).astype(bf16), passage_marks)[:1] > 0
    query_count = jnp.sum(rows_ref[query_side, :, width:][:, :1].astype(f32))
    per_query = 1.0 / query_count

    def part(i, carry):
        loss, as_query, as_passage = carry
        at = pl.ds(pl.multiple_of(i * chunk, chunk), chunk)
        marks = rows_ref[query_side, at, width:].astype(f32)
        live = marks[:, 0:1] > 0
        target = marks[:, 1:2].astype(jnp.int32) * 64 + marks[:, 2:3].astype(jnp.int32)
        queries = rows_ref[query_side, at, :width]
        passages = rows_ref[passage_side, :, :width]
        scores = dot_rows(queries, passages) * inverse_temp
        scores = jnp.where(passage_live, scores, masked_score)
        top = jnp.max(scores, axis=-1, keepdims=True)
        log_sum = top + jnp.log(jnp.sum(jnp.exp(scores - top), axis=-1, keepdims=True))
        is_target = numbers == target
        picked = jnp.sum(jnp.where(is_target, scores, 0.0), axis=-1, keepdims=True)
        loss = loss + jnp.sum(jnp.where(live, log_sum - picked, 0.0))
        chances = jnp.where(passage_live, jnp.exp(scores - log_sum), 0.0)
        grad = jnp.where(live, (chances - is_target.astype(f32)) * per_query, 0.0).astype(bf16)
        as_passage = as_passage + dot_cols(grad[:, :128], queries)[:slots]
        own = dot(grad[:slots], passages)
        as_query = jnp.where(i == 0, own, as_query)
        return loss, as_query, as_passage

    zeros = jnp.zeros((slots, width), f32)
    carry = (jnp.float32(0), zeros, zeros)
    if total == chunk:
        carry = part(0, carry)
    else:
        carry = lax.fori_loop(0, total // chunk, part, carry)
    loss, as_query, as_passage = carry
    loss_out[0, 0] = loss * per_query
    grad_unit = jnp.where(passage_side == 1, as_query, as_passage) * inverse_temp
    pooled = pool_ref[...]
    inverse = lax.rsqrt(jnp.sum(pooled * pooled, axis=-1, keepdims=True) + pool_eps)
    along = jnp.sum(grad_unit * pooled, axis=-1, keepdims=True)
    grad_pooled = inverse * grad_unit - pooled * (inverse * inverse * inverse) * along
    gain = line(gain)
    sums = []
    for row in range(rows):
        at = slice(row * length, (row + 1) * length)
        own = slice(row * row_slots, (row + 1) * row_slots)
        seg = segment_of(lens_ref, row, lax.broadcasted_iota(jnp.int32, (row_slots, length), 1))
        member = (seg == lax.broadcasted_iota(jnp.int32, (row_slots, length), 0)).astype(f32)
        count = jnp.maximum(jnp.sum(member, axis=-1, keepdims=True), 1.0)
        member = member.astype(bf16)
        high, low = split_low(grad_pooled[own] / count)
        grad_final = dot_cols(member, high) + dot_cols(member, low)
        scaled = xhat_ref[at, :].astype(f32)
        grad_sum = norm_back(grad_final, scaled, inv_ref[at, :], gain)
        grad_low = grad_sum.astype(bf16)
        grad_out[at, :] = grad_low
        sums.append(
            (
                jnp.sum(grad_final * scaled, axis=0, keepdims=True),
                jnp.sum(grad_final, axis=0, keepdims=True),
                jnp.sum(grad_low.astype(f32), axis=0, keepdims=True),
            )
        )
    for i in range(3):
        vec_out[i : i + 1, :] = sum(each[i] for each in sums)
    copy.wait()
    parts, sides, half, share = send_out.shape
    other = grad_out[:, pl.ds(pl.multiple_of(place_ref[5] * half, half), half)]
    for z in range(parts):
        for y in range(sides):
            at = slice((z * sides + y) * share, (z * sides + y + 1) * share)
            send_out[z, y] = dot_cols(other, active_ref[:, at]).astype(bf16)


def match(place, lens, rows, pooled, xhat, inverse, gain, active):
    tokens, width = xhat.shape
    slots = pooled.shape[0]
    vmem = pl.BlockSpec(memory_space=pltpu.VMEM)
    return pl.pallas_call(
        match_kernel,
        in_specs=[smem(), smem()] + [vmem] * 4 + [vmem, pl.BlockSpec(memory_space=pl.ANY)],
        out_specs=[smem()] + [vmem] * 3,
        out_shape=[
            shaped((1, 1), f32),
            shaped((tokens, width), bf16),
            shaped((8, width), f32),
            shaped((4, 2, width // 2, active.shape[1] // 8), bf16),
        ],
        scratch_shapes=[
            pltpu.VMEM(active.shape, bf16),
            pltpu.SemaphoreType.DMA,
        ],
        compiler_params=params((16 << 20) + 5 * rows.size),
        cost_estimate=cost(2e9, 10 << 20),
        name="match",
    )(place, lens, rows, pooled, xhat, inverse, gain, active)


def hidden_kernel(place_ref, grad_ref, slope_ref, wd, low_ref, hidden_out, bias_out, send_out):
    step = pl.program_id(0)
    per = pl.num_programs(0) // 2
    grad = dot_rows(grad_ref[...], wd[...]) * slope_ref[...].astype(f32)
    grad_low = grad.astype(bf16)
    hidden_out[...] = grad_low
    bias_out[...] = jnp.sum(grad_low.astype(f32), axis=0, keepdims=True)

    @pl.when(step // per == place_ref[5])
    def _():
        send_out[step % per] = dot_cols(low_ref[...], hidden_out[...]).astype(bf16)


def hidden_grad(place, grad, slope, wd, low):
    tokens, width = grad.shape
    hidden = wd.shape[0]
    chunk = hidden // 4
    act = pl.BlockSpec((tokens, chunk), lambda j: (0, j))
    full = whole((tokens, width))
    return pl.pallas_call(
        hidden_kernel,
        grid=(hidden // chunk,),
        in_specs=[smem(), full, act, pl.BlockSpec((chunk, width), lambda j: (j, 0)), full],
        out_specs=[act, pl.BlockSpec((1, chunk), lambda j: (0, j)), whole((2, width, chunk))],
        out_shape=[
            shaped((tokens, hidden), bf16),
            shaped((1, hidden), f32),
            shaped((2, width, chunk), bf16),
        ],
        compiler_params=params(12 << 20),
        cost_estimate=cost(3 * tokens * width * hidden, 22 << 20),
        name="hidden_grad",
    )(place, grad, slope, wd, low)


def feed_back_kernel(
    place_ref, grad_ref, hidden_ref, wu, wo, xhat_ref, inv_ref, gain, low_ref, mixed_ref, got_ref,
    branch_out, mixed_out, vec_out, send_out, keep_out, *refs,
):
    outs, acc_ref, part_ref = refs[:-2], refs[-2], refs[-1]
    step = pl.program_id(0)
    steps = pl.num_programs(0)
    tokens, width = grad_ref.shape
    half = tokens // 2
    chunk = hidden_ref.shape[1]
    per = steps // 2

    @pl.when(step == 0)
    def _():
        acc_ref[...] = grad_ref[...].astype(f32)

    for part in range(2):
        at = slice(part * half, (part + 1) * half)
        acc_ref[at, :] += dot_rows(hidden_ref[at, :], wu[...])

    if outs:

        size = outs[0].shape[2]
        narrow = width // 2
        first = outs[0].shape[3] - chunk

        @pl.when(step // per == place_ref[1])
        def _():
            part_ref[...] = dot_cols(low_ref[...], hidden_ref[...]) + got_ref[step % per].astype(f32)

            @pl.when(step % per == 0)
            def _():
                cut_rows(place_ref, part_ref, outs[:2], slice(0, chunk), False, size)

            @pl.when(step % per == 1)
            def _():
                at = slice(chunk, chunk + first)
                cut_rows(place_ref, part_ref.at[:, :first], outs[:2], at, False, size)
                at = slice(narrow, narrow + chunk - first)
                cut_rows(place_ref, part_ref.at[:, first:], outs[2:], at, True, size)

    @pl.when(step == steps - 1)
    def _():
        tallies = []
        for part in range(2):
            at = slice(part * half, (part + 1) * half)
            grad = acc_ref[at, :]
            scaled = xhat_ref[at, :].astype(f32)
            grad_low = norm_back(grad, scaled, inv_ref[at, :], line(gain)).astype(bf16)
            branch_out[at, :] = grad_low
            mixed_out[at, :] = dot_rows(grad_low, wo[...]).astype(bf16)
            tallies.append(
                (
                    jnp.sum(grad * scaled, axis=0, keepdims=True),
                    jnp.sum(grad, axis=0, keepdims=True),
                    jnp.sum(grad_low.astype(f32), axis=0, keepdims=True),
                )
            )
        for i in range(3):
            vec_out[i : i + 1, :] = tallies[0][i] + tallies[1][i]
        narrow = width // 2
        for i, out in enumerate((keep_out, send_out)):
            at = pl.ds(pl.multiple_of(place_ref[1 + 4 * i] * narrow, narrow), narrow)
            out[...] = dot_cols(mixed_ref[...], branch_out[:, at]).astype(bf16)


def feed_back(place, grad, grad_hidden, wu, wo, xhat, inverse, gain, low, mixed, got, fast):
    tokens, width = grad.shape
    hidden = wu.shape[1]
    chunk = hidden // 4
    narrow = width // 2
    full = whole((tokens, width))
    strip = whole((width, narrow))
    first = chunk + width // 3
    pieces = [(2, 4, width // 16, first)] * 2 + [(2, 4, width // 16, 2 * chunk - first + narrow)] * 2
    pieces = pieces if fast else []
    return pl.pallas_call(
        feed_back_kernel,
        grid=(hidden // chunk,),
        in_specs=[
            smem(), full, pl.BlockSpec((tokens, chunk), lambda j: (0, j)),
            pl.BlockSpec((width, chunk), lambda j: (0, j)), whole((width, width)), full,
            whole((tokens, 1)), whole((width,)), full, full, whole((2, width, chunk)),
        ],
        out_specs=[full, full, whole((8, width)), strip, strip] + [whole(each) for each in pieces],
        out_shape=[
            shaped((tokens, width), bf16),
            shaped((tokens, width), bf16),
            shaped((8, width), f32),
            shaped((width, narrow), bf16),
            shaped((width, narrow), bf16),
        ]
        + [shaped(each, bf16) for each in pieces],
        scratch_shapes=[pltpu.VMEM((tokens, width), f32), pltpu.VMEM((width, chunk), f32)],
        compiler_params=params(24 << 20),
        cost_estimate=cost(4 * tokens * width * hidden, 30 << 20),
        name="feed_back",
    )(place, grad, grad_hidden, wu, wo, xhat, inverse, gain, low, mixed, got)


def join_kernel(place_ref, keep_ref, got_ref, *refs):
    outs, acc_ref = refs[2:4], refs[4]
    acc_ref[...] = keep_ref[...].astype(f32) + got_ref[...].astype(f32)
    cut_rows(place_ref, acc_ref, outs, slice(None), True, outs[0].shape[2])


def join_out(place, keep, got, pieces):
    width, narrow = keep.shape
    piece = pl.BlockSpec((2, 4, width // 16, narrow), lambda j: (0, 0, 0, 0))
    return pl.pallas_call(
        join_kernel,
        grid=(1,),
        in_specs=[smem(), whole(keep.shape), whole(got.shape)]
        + [pl.BlockSpec(memory_space=pl.ANY)] * 2,
        out_specs=[piece] * 2,
        out_shape=[shaped(each.shape, bf16) for each in pieces],
        input_output_aliases={3 + i: i for i in range(2)},
        scratch_shapes=[pltpu.VMEM((width, narrow), f32)],
        compiler_params=params(8 << 20),
        cost_estimate=cost(0, 3 << 20),
        name="join_out",
    )(place, keep, got, *pieces)


def attend_back_kernel(
    place_ref, lens_ref, q_ref, k_ref, v_ref, lse_ref, mixed_ref, grad_ref, x_ref,
    first_sums, second_sums, up_sums, out, vec_out, send_out, own_out, other_out, mask_ref, sums_ref, pack_ref,
):
    step = pl.program_id(0)
    rows, length, _ = mask_ref.shape

    @pl.when(step == 0)
    def _():
        fill_mask(lens_ref, mask_ref)

    lane = lax.broadcasted_iota(jnp.int32, (1, 128), 1)
    scale = 64 ** (-0.5)
    pairs = q_ref.shape[1] // 128
    for pair in range(pairs):
        lanes = slice(pair * 128, (pair + 1) * 128)
        query_sums, value_sums = [], []
        for row in range(rows):
            tokens = slice(row * length, (row + 1) * length)
            q = q_ref[tokens, lanes] * bf16(scale)
            k = k_ref[tokens, lanes]
            v = v_ref[tokens, lanes]
            grad = grad_ref[tokens, lanes]
            high, low = split_low(grad.astype(f32) * mixed_ref[tokens, lanes].astype(f32))
            grad_v = grad_k = grad_q = 0.0
            for head in range(2):
                mine = (lane < 64) == (head == 0)
                ones = jnp.broadcast_to(jnp.where(mine, 1.0, 0.0), (8, 128)).astype(bf16)
                inner = (dot_rows(ones, high) + dot_rows(ones, low))[:1]
                log_total = lse_ref[row, pl.ds((step * pairs + pair) * 2 + head, 1), :]
                own_q = jnp.where(mine, q, bf16(0))
                own_grad = jnp.where(mine, grad, bf16(0))
                scores = dot_rows(k, own_q) + mask_ref[row]
                probs = jnp.exp(scores - log_total)
                grad_scores = (probs * (dot_rows(v, own_grad) - inner)).astype(bf16)
                grad_v = grad_v + dot(probs.astype(bf16), own_grad)
                grad_k = grad_k + dot(grad_scores, own_q)
                grad_q = grad_q + dot_cols(jnp.where(mine, k, bf16(0)), grad_scores)
            grad_q = (jnp.transpose(grad_q) * scale).astype(bf16)
            grad_v = grad_v.astype(bf16)
            out[0, tokens, lanes] = grad_q
            out[1, tokens, lanes] = grad_k.astype(bf16)
            out[2, tokens, lanes] = grad_v
            query_sums.append(jnp.sum(grad_q.astype(f32), axis=0, keepdims=True))
            value_sums.append(jnp.sum(grad_v.astype(f32), axis=0, keepdims=True))
        vec_out[0:1, lanes] = sum(query_sums)
        vec_out[1:2, lanes] = sum(value_sums)
        at = pl.ds(pl.multiple_of((step * pairs + pair) * 128, 128), 128)
        sums_ref[0:1, at] = sum(query_sums)
        sums_ref[1:2, at] = sum(value_sums)
    other = pl.ds(pl.multiple_of(place_ref[5] * 128, 128), 128)
    grads = jnp.concatenate([out[i, :, other] for i in range(3)], axis=1)
    send_out[...] = dot_cols(x_ref[...], grads).astype(bf16)

    @pl.when(step == pl.num_programs(0) - 1)
    def _():
        sums = [sums_ref[i : i + 1, :] for i in range(2)]
        sums += [first_sums[2:3, :], second_sums[2:3, :], first_sums[0:1, :], first_sums[1:2, :]]
        sums += [second_sums[0:1, :], second_sums[1:2, :]]
        width = x_ref.shape[1]
        share = width // 8
        pack_ref[...] = jnp.zeros(pack_ref.shape, f32)
        for n in range(12):
            for d in range(8):
                if n < 8:
                    piece = sums[n][:, d * share : (d + 1) * share]
                else:
                    piece = up_sums[:, (d * 4 + n - 8) * share : (d * 4 + n - 7) * share]
                row = (d * 2 + n // 3 % 2) * (width // 16) + n % 3
                pack_ref[n // 6, row : row + 1, :share] = piece
        own_out[...] = pack_ref[place_ref[1]].astype(bf16)
        other_out[...] = pack_ref[place_ref[5]].astype(bf16)


def attend_back(place, lens, q, k, v, lse, mixed, grad, x, first_sums, second_sums, up_sums):
    tokens, width = q.shape
    rows = lens.shape[0]
    length = tokens // rows
    group = 256
    act = pl.BlockSpec((tokens, group), lambda j: (0, j))
    return pl.pallas_call(
        attend_back_kernel,
        grid=(width // group,),
        in_specs=[smem(), smem(), act, act, act, whole(lse.shape), act, act, whole(x.shape)]
        + [whole(each.shape) for each in (first_sums, second_sums, up_sums)],
        out_specs=[
            pl.BlockSpec((3, tokens, group), lambda j: (0, 0, j)),
            pl.BlockSpec((8, group), lambda j: (0, j)),
            pl.BlockSpec((width, 384), lambda j: (0, j)),
            whole((width, 128)),
            whole((width, 128)),
        ],
        out_shape=[
            shaped((3, tokens, width), bf16),
            shaped((8, width), f32),
            shaped((width, width // group * 384), bf16),
            shaped((width, 128), bf16),
            shaped((width, 128), bf16),
        ],
        scratch_shapes=[
            pltpu.VMEM((rows, length, length), f32),
            pltpu.VMEM((8, width), f32),
            pltpu.VMEM((2, width, 128), f32),
        ],
        compiler_params=params(60 << 20),
        cost_estimate=cost(20 * tokens * length * width, 15 << 20),
        name="attend_back",
    )(place, lens, q, k, v, lse, mixed, grad, x, first_sums, second_sums, up_sums)


def input_kernel(branch_ref, grads_ref, wq, wk, wv, out):
    out[...] = (
        branch_ref[...].astype(f32)
        + dot_rows(grads_ref[0], wq[...])
        + dot_rows(grads_ref[1], wk[...])
        + dot_rows(grads_ref[2], wv[...])
    )


def input_grad(branch, grads, wq, wk, wv):
    tokens, width = branch.shape
    part = tokens // 4
    weight = whole((width, width))
    rows = pl.BlockSpec((part, width), lambda j: (j, 0))
    return pl.pallas_call(
        input_kernel,
        grid=(4,),
        in_specs=[rows, pl.BlockSpec((3, part, width), lambda j: (0, j, 0)), weight, weight, weight],
        out_specs=rows,
        out_shape=shaped((tokens, width), f32),
        compiler_params=params(60 << 20),
        cost_estimate=cost(6 * tokens * width * width, 13 << 20),
        name="input_grad",
    )(branch, grads, wq, wk, wv)


def down_kernel(place_ref, left_ref, right_ref, got_ref, *refs):
    outs, acc_ref = refs[:-1], refs[-1]
    share = right_ref.shape[1] // 2
    half = left_ref.shape[1] // 2
    strip = half // 2
    for y in range(2):
        lanes = slice(y * share, (y + 1) * share)
        acc_ref[...] = dot_cols(left_ref[...], right_ref[:, lanes]) + got_ref[0, y].astype(f32)
        for rel in range(2):
            at = pl.multiple_of((place_ref[2] ^ rel) * half, half)
            outs[rel][y, 0] = acc_ref[pl.ds(at, strip), :].astype(bf16)

            @pl.when(place_ref[3] == y ^ rel)
            def _():
                for x in range(2):
                    rows = slice(x * half + strip, (x + 1) * half)
                    outs[2 + rel][x, 0] = acc_ref[rows, :].astype(bf16)


def down_grad(place, grad, active, got):
    tokens, width = grad.shape
    hidden = active.shape[1]
    half, parts = width // 2, 4
    share = hidden // parts // 2
    piece = pl.BlockSpec((2, 1, half // 4, share), lambda z, s: (0, z, 0, 0))
    piece_shape = shaped((2, parts, half // 4, share), bf16)
    return pl.pallas_call(
        down_kernel,
        grid_spec=pltpu.PrefetchScalarGridSpec(
            num_scalar_prefetch=1,
            grid=(parts,),
            in_specs=[
                pl.BlockSpec((tokens, half), lambda z, s: (0, s[1])),
                pl.BlockSpec((tokens, 2 * share), lambda z, s: (0, z)),
                pl.BlockSpec((1, 2, half, share), lambda z, s: (z, 0, 0, 0)),
            ],
            out_specs=[piece] * 4,
            scratch_shapes=[pltpu.VMEM((half, share), f32)],
        ),
        out_shape=[piece_shape] * 4,
        compiler_params=params(10 << 20),
        cost_estimate=cost(2 * half * tokens * hidden, 12 << 20),
        name="down_keep",
    )(place, grad, active, got)


def cut_rows(place_ref, acc_ref, outs, at, by_y, size):
    outer = acc_ref.shape[0] // 4 // size
    for rel, out in enumerate(outs):
        for z in range(outer):
            for i in range(2):
                y, x = (place_ref[3] ^ rel, i) if by_y else (i, place_ref[2] ^ rel)
                row = pl.multiple_of(((z * 2 + y) * 2 + x) * size, size)
                out[i, z, :, at] = acc_ref[pl.ds(row, size), :].astype(bf16)


def head_kernel(place_ref, x_ref, grads_ref, vec_ref, got_vec_ref, got_ref, *refs):
    outs, acc_ref = refs[:-1], refs[-1]
    step = pl.program_id(0)
    steps = pl.num_programs(0)
    span = got_ref.shape[1]
    grads = jnp.concatenate([grads_ref[i] for i in range(3)], axis=1)
    acc_ref[...] = dot_cols(x_ref[...], grads) + got_ref[...].astype(f32)
    half = outs[0].shape[3]
    size = outs[0].shape[2]

    def cut_lanes(start, stop, source):
        for low, high, by_y in ((0, half, False), (half, 2 * half, True)):
            begin, end = max(start, low), min(stop, high)
            if begin < end:
                part = source.at[:, begin - start : end - start]
                at = slice(begin - low, end - low)
                cut_rows(place_ref, part, outs[2 * by_y : 2 * by_y + 2], at, by_y, size)

    for j in range(2 * half // span):

        @pl.when(step == j)
        def _():
            cut_lanes(j * span, (j + 1) * span, acc_ref)

    @pl.when(step == steps - 1)
    def _():
        acc_ref[:, :128] = vec_ref[...].astype(f32) + got_vec_ref[...].astype(f32)
        cut_lanes(2 * half - 128, 2 * half, acc_ref.at[:, :128])


def head_grad(place, x, grads, vectors, got_vectors, got):
    tokens, width = x.shape
    groups = width // 256
    total = groups * 384 + 128
    piece_shape = (2, 4, width // 16, total // 2)
    return pl.pallas_call(
        head_kernel,
        grid_spec=pltpu.PrefetchScalarGridSpec(
            num_scalar_prefetch=1,
            grid=(groups,),
            in_specs=[
                whole((tokens, width)),
                pl.BlockSpec((3, tokens, 128), lambda j, s: (0, 0, 2 * j + s[1])),
                whole((width, 128)),
                whole((width, 128)),
                pl.BlockSpec((width, 384), lambda j, s: (0, j)),
            ],
            out_specs=[whole(piece_shape)] * 4,
            scratch_shapes=[pltpu.VMEM((width, 384), f32)],
        ),
        out_shape=[shaped(piece_shape, bf16)] * 4,
        compiler_params=params(10 << 20),
        cost_estimate=cost(2 * width * tokens * total, 9 << 20),
        name="head_keep",
    )(place, x, grads, vectors, got_vectors, got)


def mix_kernel(which, parts, place_ref, *refs):
    ins, outs = refs[:-parts], refs[-parts:]
    for rel, out in enumerate(outs):
        at = place_ref[which] ^ rel if parts > 1 else 0
        total = ins[0][at].astype(f32)
        for ref in ins[1:]:
            total = total + ref[at].astype(f32)
        out[...] = total.astype(bf16)


def mix(place, which, arrays):
    parts = arrays[0].shape[0]
    return pl.pallas_call(
        partial(mix_kernel, which, parts),
        in_specs=[smem()] + [pl.BlockSpec(memory_space=pltpu.VMEM)] * len(arrays),
        out_specs=[pl.BlockSpec(memory_space=pltpu.VMEM)] * parts,
        out_shape=[shaped(arrays[0].shape[1:], bf16)] * parts,
        compiler_params=params(8 << 20),
        cost_estimate=cost(0, 2 * arrays[0].size * (len(arrays) + 1)),
        name="mix",
    )(place, *arrays)


def first_exchange(parts):
    return [parts[0], swap(parts[1], "tower", 2), parts[2], swap(parts[3], "dp", 1)]


def second_exchange(parts):
    return [parts[0], swap(parts[1], "dp", 1), parts[2], swap(parts[3], "tower", 2)]


def cross_kernel(place_ref, *refs):
    ins, outs = refs[:4], refs[4:]
    for i in range(2):
        mine, got = ins[2 * i : 2 * i + 2]
        for rel in range(2):
            at = place_ref[3 - i] ^ rel
            outs[2 * i + rel][...] = (mine[at].astype(f32) + got[at].astype(f32)).astype(bf16)


def cross(place, parts):
    vmem = pl.BlockSpec(memory_space=pltpu.VMEM)
    return pl.pallas_call(
        cross_kernel,
        in_specs=[smem()] + [vmem] * 4,
        out_specs=[vmem] * 4,
        out_shape=[shaped(each.shape[1:], bf16) for each in parts],
        compiler_params=params(8 << 20),
        cost_estimate=cost(0, 6 << 20),
        name="cross",
    )(place, *parts)


def outer_kernel(axis, place_ref, *refs):
    ins, outs = refs[:4], refs[4:]
    for rel, out in enumerate(outs):
        at = place_ref[4] ^ rel
        sums = [ins[2 * i][at].astype(f32) + ins[2 * i + 1][at].astype(f32) for i in range(2)]
        out[...] = jnp.concatenate(sums, axis=axis).astype(bf16)


def cut_halves(place, axis, parts):
    vmem = pl.BlockSpec(memory_space=pltpu.VMEM)
    outer = parts[0].shape[0]
    shape = list(parts[0].shape[1:])
    shape[axis] += parts[2].shape[1 + axis]
    return pl.pallas_call(
        partial(outer_kernel, axis),
        in_specs=[smem()] + [vmem] * 4,
        out_specs=[vmem] * outer,
        out_shape=[shaped(tuple(shape), bf16)] * outer,
        compiler_params=params(8 << 20),
        cost_estimate=cost(0, 3 << 20),
        name="cut_halves",
    )(place, *parts)


def exchange_outer(parts):
    return [parts[0]] + [swap(part, "dp", 2 * rel) for rel, part in enumerate(parts) if rel]


def join_outer(place, parts):
    return mix(place, 4, [part[None] for part in parts])[0]


def spread_kernel(kind, place_ref, *refs):
    blocks, outs = refs[:4], refs[4:]
    core, far = place_ref[1], place_ref[2]
    share = outs[0].shape[0]
    for i, block in enumerate(blocks):
        c, x = core ^ (i >> 1), far ^ (i & 1)
        value = block[...].astype(f32)
        size = value.shape[0]
        rows = pl.ds(pl.multiple_of(x * size, size), size)
        if kind == "down":
            at = pl.multiple_of((c * 2 + x) * size, size)
            outs[0][pl.ds(at, size), :] = value
            continue
        half = outs[1].shape[1] // 2
        if kind == "up":
            total = outs[0].shape[1] // 2
            wide = pl.ds(pl.multiple_of(c * total, total), total)
            narrow = pl.ds(pl.multiple_of(c * half, half), half)
            first = total // 3 * 2
            outs[0][rows, wide] = jnp.concatenate([value[:, :first], value[:, first + half :]], axis=1)
            outs[1][rows, narrow] = value[:, first : first + half]
        else:
            groups = half // 128
            for j in range(groups):
                lanes = pl.ds(pl.multiple_of(j * 256 + c * 128, 128), 128)
                for m in range(3):
                    outs[m][rows, lanes] = value[:, (j * 3 + m) * 128 : (j * 3 + m + 1) * 128]
            refs[-1][c * 2 + x] = value[:16, 3 * half :]
    if kind == "head":
        for n in range(8):
            outs[3 + n][...] = refs[-1][n // 3, n % 3 : n % 3 + 1, :share].reshape(-1)
        last = [refs[-1][n // 3, n % 3 : n % 3 + 1, :share] for n in range(8, 12)]
        outs[11][...] = jnp.concatenate(last, axis=1).reshape(-1)


def spread(place, kind, block, far, shapes):
    blocks = [block, far, swap(block, "tower", 1), swap(far, "tower", 1)]
    return pl.pallas_call(
        partial(spread_kernel, kind),
        in_specs=[smem()] + [pl.BlockSpec(memory_space=pltpu.VMEM)] * 4,
        out_specs=[pl.BlockSpec(memory_space=pltpu.VMEM)] * len(shapes),
        out_shape=[shaped(shape, f32) for shape in shapes],
        scratch_shapes=[pltpu.VMEM((4, 16, 128), f32)] if kind == "head" else [],
        compiler_params=params(8 << 20),
        cost_estimate=cost(0, 2 << 20),
        name="spread_" + kind,
    )(place, *blocks)


def shards(
    layer_input,
    seg_lengths,
    positives,
    query_weight,
    key_weight,
    value_weight,
    out_weight,
    up_weight,
    down_weight,
    query_bias,
    value_offset_bias,
    out_bias,
    up_bias,
    down_bias,
    first_gain,
    first_shift,
    second_gain,
    latter_norm_translation,
):
    row_count = layer_input.shape[1]
    row_len = layer_input.shape[2]
    width = layer_input.shape[3]
    slot_count = seg_lengths.shape[2]
    token_count = row_count * row_len
    tower_index = lax.axis_index("tower")
    dp_index = lax.axis_index("dp")
    dp_count = lax.axis_size("dp")
    core, far = tower_index & 1, tower_index >> 1
    place = jnp.stack([1 - far, core, far, dp_index & 1, dp_index >> 1, 1 - core]).astype(jnp.int32)
    flat_in = layer_input.reshape(token_count, width)
    lens = seg_lengths.reshape(row_count, slot_count)

    q, k, v, mixed, lse, first, low, first_scaled, first_inverse = attend(
        lens, flat_in, query_weight, key_weight, value_weight, out_weight,
        query_bias, value_offset_bias, out_bias, first_gain, first_shift,
    )
    active, slope, second_scaled, second_inverse, pooled, unit = feed(
        place, lens, positives, low, first, up_weight, up_bias, down_weight, down_bias,
        second_gain, latter_norm_translation,
    )
    rows = gather_all(unit).reshape(2, -1, width + 128)
    loss, grad_second, second_sums, down_half = match(
        place, lens, rows, pooled, second_scaled, second_inverse, second_gain, active
    )
    loss = loss.reshape(())
    share = width // dp_count
    fast = dp_count == 8 and lax.axis_size("tower") == 4
    grad_hidden, up_sums, up_half = hidden_grad(place, grad_second, slope, down_weight, low)
    if fast:
        got = swap(down_half, "tower", 1)
        got, grad_hidden, up_half = lax.optimization_barrier((got, grad_hidden, up_half))
        down_parts = down_grad(place, grad_second, active, got)
        up_half = swap(up_half, "tower", 1)
        down_parts, grad_hidden, up_half = lax.optimization_barrier(
            (down_parts, grad_hidden, up_half)
        )
        down_parts = first_exchange(down_parts)
    grad_branch, grad_mixed, first_sums, out_half, out_keep, *up_parts = feed_back(
        place, grad_second, grad_hidden, up_weight, out_weight, first_scaled, first_inverse,
        first_gain, low, mixed, up_half, fast,
    )
    if fast:
        down_parts, out_half = lax.optimization_barrier((down_parts, out_half))
        out_half = swap(out_half, "tower", 1)
        down_parts = cross(place, down_parts)
        down_parts, out_half = lax.optimization_barrier((down_parts, out_half))
        up_parts[2:] = join_out(place, out_keep, out_half, up_parts[2:])
        up_parts, down_parts, grad_mixed = lax.optimization_barrier((up_parts, down_parts, grad_mixed))
        up_parts = first_exchange(up_parts)
        down_parts = second_exchange(down_parts)
    grads, head_sums, head_half, vectors, other_vectors = attend_back(
        place, lens, q, k, v, lse, mixed, grad_mixed, flat_in, first_sums, second_sums, up_sums
    )
    if fast:
        up_parts, down_parts, grads, head_half, other_vectors = lax.optimization_barrier(
            (up_parts, down_parts, grads, head_half, other_vectors)
        )
    if fast:
        got = swap(head_half, "tower", 1)
        got_vectors = swap(other_vectors, "tower", 1)
        down_parts = cut_halves(place, 0, down_parts)
        up_parts = cross(place, up_parts)
        up_parts, down_parts, got = lax.optimization_barrier((up_parts, down_parts, got))
        up_parts = second_exchange(up_parts)
        down_parts = exchange_outer(down_parts)
        parts = head_grad(place, flat_in, grads, vectors, got_vectors, got)
        up_parts, down_parts, parts, grads = lax.optimization_barrier(
            (up_parts, down_parts, parts, grads)
        )
        parts = first_exchange(parts)
        up_parts = exchange_outer(cut_halves(place, 1, up_parts))
        down_part = join_outer(place, down_parts)
        down_part, parts = lax.optimization_barrier((down_part, parts))
        parts = cross(place, parts)
        parts, grads = lax.optimization_barrier((parts, grads))
        parts = second_exchange(parts)
        grad_input = input_grad(grad_branch, grads, query_weight, key_weight, value_weight)
        up_parts, parts, grad_input = lax.optimization_barrier((up_parts, parts, grad_input))
        parts = exchange_outer(cut_halves(place, 1, parts))
        up_part = join_outer(place, up_parts)
        down_far, up_far = swap(down_part, "tower", 2), swap(up_part, "tower", 2)
        up_far, down_far, parts = lax.optimization_barrier((up_far, down_far, parts))
        head_part = join_outer(place, parts)
        head_far = swap(head_part, "tower", 2)
        (down_turned,) = spread(place, "down", down_part, down_far, [(width, 4 * share)])
        total_down = down_turned.T
        total_up, total_out = spread(
            place, "up", up_part, up_far, [(share, up_weight.shape[1]), (share, width)]
        )
        total_down, total_up, total_out, head_far = lax.optimization_barrier(
            (total_down, total_up, total_out, head_far)
        )
        total_query, total_key, total_value, *sums = spread(
            place, "head", head_part, head_far,
            [(share, width)] * 3 + [(share,)] * 8 + [(4 * share,)],
        )
    else:
        grad_input = input_grad(grad_branch, grads, query_weight, key_weight, value_weight)
        outer = dp_count // 2
        vectors = jnp.concatenate(
            [
                vec.reshape(dp_count, -1)
                for vec in (
                    head_sums[0],
                    head_sums[1],
                    first_sums[2],
                    second_sums[2],
                    first_sums[0],
                    first_sums[1],
                    second_sums[0],
                    second_sums[1],
                    up_sums,
                )
            ],
            axis=1,
        ).astype(bf16)

        def by_rows(grad):
            return grad.astype(bf16).reshape(outer, 2, share, 2, 2, width).transpose(3, 4, 1, 0, 2, 5)

        square = jnp.stack(
            [dot_cols(flat_in, grads[i]) for i in range(3)] + [dot_cols(mixed, grad_branch)], axis=1
        )
        vectors = vectors.reshape(outer, 2, 2, 2, -1).transpose(2, 3, 1, 0, 4)
        vectors = jnp.pad(vectors, ((0, 0),) * 4 + ((0, width - vectors.shape[-1]),))
        down = dot_cols(active, grad_second).astype(bf16)
        down = down.reshape(outer, 2, 2, 2, share, width).transpose(2, 3, 1, 0, 4, 5)
        total_down = sum_group(down).reshape(4 * share, width)
        total_up = sum_group(by_rows(dot_cols(low, grad_hidden))).reshape(4, share, width)
        total_up = total_up.transpose(1, 0, 2).reshape(share, 4 * width)
        last = jnp.concatenate([by_rows(square), vectors[:, :, :, :, None]], axis=4)
        last = sum_group(last).reshape(4, share + 1, width)
        total_query, total_key, total_value, total_out = [last[i, :share] for i in range(4)]
        short = last[:, share, : share * 3].reshape(-1)
        sums = [short[i * share : (i + 1) * share] for i in range(8)] + [short[8 * share :]]
    grad_input = grad_input.reshape(layer_input.shape)
    return (
        loss,
        grad_input,
        total_query,
        total_key,
        total_value,
        total_out,
        total_up,
        total_down,
        sums[0],
        sums[1],
        sums[2],
        sums[8],
        sums[3],
        *sums[4:8],
    )


def solution(mesh):
    in_specs = (P("tower", "dp", None, None), P("tower", "dp", None), P(None, "dp", None)) + (P(),) * 15
    out_specs = (P(), P("tower", "dp", None, None)) + (P("dp", None),) * 6 + (P("dp"),) * 9
    return jax.shard_map(shards, mesh=mesh, in_specs=in_specs, out_specs=out_specs, check_vma=False)
```

```python
from functools import partial

import jax
import jax.numpy as jnp
from jax import lax
from jax.experimental import pallas as pl
from jax.experimental.pallas import tpu as pltpu
from jax.sharding import PartitionSpec as P

H = 12

inverse_temp = 100.0
norm_eps = 1e-06
pool_eps = 1e-06
masked_score = -1e30
f32 = jnp.float32
bf16 = jnp.bfloat16


def swap(value, axis, bits):
    count = lax.axis_size(axis)
    return lax.ppermute(value, axis, [(place, place ^ bits) for place in range(count)])


def swap_both(value, tower_bits, dp_bits):
    if not tower_bits:
        return swap(value, "dp", dp_bits)
    if not dp_bits:
        return swap(value, "tower", tower_bits)
    towers = lax.axis_size("tower")
    total = towers * lax.axis_size("dp")
    moves = [(place, place ^ (dp_bits * towers + tower_bits)) for place in range(total)]
    return lax.ppermute(value, ("dp", "tower"), moves)


def outer_bits():
    outer = lax.axis_size("dp") // 2
    return [1 << k for k in range(outer.bit_length() - 1)]


def gather_all(block, early, late):
    outer = lax.axis_size("dp") // 2
    if outer <= 4:
        got = [swap(block, "dp", 2 * k) for k in range(1, outer)]
        got, beside = lax.optimization_barrier((got, early()))
        blocks = jnp.stack([block] + got)
    else:
        beside = early()
        blocks = block[None]
        for bit in outer_bits():
            blocks = jnp.concatenate([blocks, swap(blocks, "dp", 2 * bit)])
    sides = [swap_both(blocks, 2 * x, y) if x or y else blocks for x in range(2) for y in range(2)]
    sides, beside = lax.optimization_barrier((sides, late(beside)))
    pairs = [sides[:2], sides[2:]]
    return [each for pair in pairs for each in pair + [swap(side, "tower", 1) for side in pair]], beside


def pick(value, index):
    return lax.dynamic_index_in_dim(value, index, 0, keepdims=False)


def add_up(parts):
    total = parts[0].astype(f32)
    for part in parts[1:]:
        total = total + part.astype(f32)
    return total


def sum_group(blocks):
    tower_index = lax.axis_index("tower")
    dp_index = lax.axis_index("dp")
    core, far = tower_index & 1, tower_index >> 1
    side, place = dp_index & 1, dp_index >> 1
    got = swap(pick(blocks, 1 - core), "tower", 1)
    blocks = add_up([pick(blocks, core), got]).astype(bf16)
    blocks = blocks.reshape((4,) + blocks.shape[2:])
    own = far * 2 + side
    parts = [pick(blocks, own)]
    for rel in range(1, 4):
        parts.append(swap_both(pick(blocks, own ^ rel), 2 * (rel >> 1), rel & 1))
    blocks = add_up(parts).astype(bf16)
    for bit in reversed(outer_bits()):
        halves = blocks.reshape((2, bit) + blocks.shape[1:])
        mine = jnp.where(place & bit, 1, 0)
        got = swap(pick(halves, 1 - mine), "dp", 2 * bit)
        blocks = add_up([pick(halves, mine), got]).astype(bf16)
    low = blocks[0]
    got = swap(low, "tower", 2)
    pair = jnp.where(far == 0, jnp.stack([low, got]), jnp.stack([got, low]))
    got = swap(pair, "tower", 1)
    every = jnp.where(core == 0, jnp.stack([pair, got]), jnp.stack([got, pair]))
    return every.astype(f32)


def dot(left, right):
    return jnp.dot(left, right, preferred_element_type=f32)


def dot_rows(left, right):
    return lax.dot_general(left, right, (((1,), (1,)), ((), ())), preferred_element_type=f32)


def dot_cols(left, right):
    return lax.dot_general(left, right, (((0,), (0,)), ((), ())), preferred_element_type=f32)


def split_low(value):
    high = value.astype(bf16)
    return high, (value - high.astype(f32)).astype(bf16)


def segment_of(lens_ref, row, places):
    total = jnp.int32(0)
    seg = jnp.zeros(places.shape, jnp.int32)
    for slot in range(lens_ref.shape[1]):
        total = total + lens_ref[row, slot]
        seg = seg + (places >= total).astype(jnp.int32)
    return seg


def fill_mask(lens_ref, mask_ref):
    rows, length, _ = mask_ref.shape
    for row in range(rows):
        across = segment_of(lens_ref, row, lax.broadcasted_iota(jnp.int32, (1, length), 1))
        down = segment_of(lens_ref, row, lax.broadcasted_iota(jnp.int32, (length, 1), 0))
        mask_ref[row] = jnp.where(down == across, 0.0, masked_score)


def line(ref):
    return ref[...].reshape(1, -1).astype(f32)


class Place:
    def __getitem__(self, which):
        tower, dp = lax.axis_index("tower"), lax.axis_index("dp")
        core, x = tower & 1, tower >> 1
        return (1 - x, core, x, dp & 1, dp >> 1, 1 - core)[which]


class Copies:
    def __init__(self, sems):
        self.sems, self.made = sems, {}

    def start(self, name, source, target):
        self.made[name] = pltpu.make_async_copy(source, target, self.sems.at[len(self.made)])
        self.made[name].start()

    def wait(self, *names):
        for name in names:
            self.made[name].wait()


def hbm():
    return pl.BlockSpec(memory_space=pl.ANY)


def whole(shape):
    return pl.BlockSpec(shape, lambda *_: (0,) * len(shape))


def smem():
    return pl.BlockSpec(memory_space=pltpu.SMEM)


def shaped(shape, kind):
    return jax.ShapeDtypeStruct(shape, kind)


def params(limit):
    return pltpu.CompilerParams(vmem_limit_bytes=limit)


def cost(flops, moved):
    return pl.CostEstimate(flops=int(flops), bytes_accessed=int(moved), transcendentals=0)


def norm_stats(value):
    middle = jnp.mean(value, axis=-1, keepdims=True)
    centered = value - middle
    inverse = lax.rsqrt(jnp.mean(centered * centered, axis=-1, keepdims=True) + norm_eps)
    return centered * inverse, inverse


def norm_back(grad, scaled, inverse, gain):
    grad = grad * gain
    return inverse * (
        grad
        - jnp.mean(grad, axis=-1, keepdims=True)
        - scaled * jnp.mean(grad * scaled, axis=-1, keepdims=True)
    )


def forward_kernel(
    lens_ref, targets_ref, x_ref, wq, wk, wv, wo, bq, bv, bo, gain1, shift1,
    wu, bu, wd, bd, gain2, shift2,
    q_out, k_out, v_out, mixed_out, lse_out, low_hbm, xhat1_hbm, inv1_out,
    act_out, slope_out, xhat2_out, inv2_out, pool_out, unit_out,
    mask_ref, acc_ref, low_ref, xhat1_ref, sems,
):
    step = pl.program_id(0)
    steps = pl.num_programs(0)
    groups = x_ref.shape[1] // q_out.shape[1]
    rows, slots = lens_ref.shape
    tokens, width = x_ref.shape
    length = tokens // rows
    copies = [
        pltpu.make_async_copy(low_ref, low_hbm, sems.at[0]),
        pltpu.make_async_copy(xhat1_ref, xhat1_hbm, sems.at[1]),
    ]

    @pl.when(step == 0)
    def _():
        fill_mask(lens_ref, mask_ref)
        acc_ref[...] = x_ref[...].astype(f32) + line(bo)

    @pl.when(step < groups)
    def _():
        x = x_ref[...]
        q_out[...] = (dot(x, wq[...]) + line(bq)).astype(bf16)
        k_out[...] = dot(x, wk[...]).astype(bf16)
        v_out[...] = (dot(x, wv[...]) + line(bv)).astype(bf16)
        lane = lax.broadcasted_iota(jnp.int32, (1, 128), 1)
        first_half = lane < 64
        pairs = q_out.shape[1] // 128
        scale = bf16(64 ** (-0.5))
        for row in range(rows):
            for pair in range(pairs):
                at = slice(row * length, (row + 1) * length)
                lanes = slice(pair * 128, (pair + 1) * 128)
                q = q_out[at, lanes] * scale
                k = k_out[at, lanes]
                v = v_out[at, lanes]
                outs, logs = [], []
                for head in range(2):
                    mine = first_half == (head == 0)
                    scores = dot_rows(jnp.where(mine, q, bf16(0)), k) + mask_ref[row]
                    top = jnp.max(scores, axis=-1, keepdims=True)
                    shifted = jnp.exp(scores - top).astype(bf16)
                    out = dot(shifted, jnp.where(mine, v, bf16(1)))
                    total = pltpu.roll(out, 64, 1)
                    outs.append(out / total)
                    logs.append(top + jnp.log(jnp.where(mine, total, out)))
                mixed_out[at, lanes] = jnp.where(first_half, outs[0], outs[1]).astype(bf16)
                logs = jnp.transpose(jnp.where(first_half, logs[0], logs[1]))
                place = (step * pairs + pair) * 2
                lse_out[row, pl.ds(place, 1), :] = logs[0:1]
                lse_out[row, pl.ds(place + 1, 1), :] = logs[64:65]
        acc_ref[...] += dot(mixed_out[...], wo[...])

    @pl.when(step == groups - 1)
    def _():
        for row in range(rows):
            at = slice(row * length, (row + 1) * length)
            scaled, inverse = norm_stats(acc_ref[at, :])
            first = scaled * line(gain1) + line(shift1)
            acc_ref[at, :] = first + line(bd)
            low_ref[at, :] = first.astype(bf16)
            xhat1_ref[at, :] = scaled.astype(bf16)
            inv1_out[at, :] = inverse
        for copy in copies:
            copy.start()

    @pl.when(step >= groups)
    def _():
        chunk = wu.shape[1]
        part = min(chunk, 512)
        for row in range(rows):
            at = slice(row * length, (row + 1) * length)
            for low in range(0, chunk, part):
                lanes = slice(low, low + part)
                hidden = dot(low_ref[at, :], wu[:, lanes]) + line(bu)[:, lanes]
                share = 0.5 + 0.5 * lax.erf(hidden * 0.7071067811865476)
                bell = jnp.exp(hidden * hidden * -0.5) * 0.3989422804014327
                act_out[at, lanes] = (hidden * share).astype(bf16)
                slope_out[at, lanes] = (share + hidden * bell).astype(bf16)
            acc_ref[at, :] += dot(act_out[at, :], wd[...])

    @pl.when(step == steps - 1)
    def _():
        for row in range(rows):
            at = slice(row * length, (row + 1) * length)
            own = slice(row * slots, (row + 1) * slots)
            scaled, inverse = norm_stats(acc_ref[at, :])
            xhat2_out[at, :] = scaled.astype(bf16)
            inv2_out[at, :] = inverse
            final = scaled * line(gain2) + line(shift2)
            high, low = split_low(final)
            seg = segment_of(lens_ref, row, lax.broadcasted_iota(jnp.int32, (slots, length), 1))
            member = (seg == lax.broadcasted_iota(jnp.int32, (slots, length), 0)).astype(f32)
            count = jnp.maximum(jnp.sum(member, axis=-1, keepdims=True), 1.0)
            member = member.astype(bf16)
            pooled = (dot(member, high) + dot(member, low)) / count
            pool_out[own, :] = pooled
            norm_sq = jnp.sum(pooled * pooled, axis=-1, keepdims=True)
            unit_out[own, :width] = (pooled * lax.rsqrt(norm_sq + pool_eps)).astype(bf16)
        spot = lax.broadcasted_iota(jnp.int32, (rows * slots, 128), 0)
        lane = lax.broadcasted_iota(jnp.int32, (rows * slots, 128), 1)
        marks = jnp.zeros((rows * slots, 128), jnp.int32)
        for row in range(rows):
            for slot in range(slots):
                live = (lens_ref[row, slot] > 0).astype(jnp.int32)
                target = targets_ref[Place()[1], row, slot]
                mark = jnp.where(lane == 0, live, jnp.where(lane == 1, target >> 6, target & 63))
                marks = jnp.where((spot == row * slots + slot) & (lane < 3), mark, marks)
        unit_out[:, width:] = marks.astype(f32).astype(bf16)
        for copy in copies:
            copy.wait()


def forward(
    lens, targets, x, wq, wk, wv, wo, bq, bv, bo, gain1, shift1, wu, bu, wd, bd, gain2, shift2
):
    tokens, width = x.shape
    hidden = wu.shape[1]
    rows, slots = lens.shape
    length = tokens // rows
    group = 256
    groups = width // group
    chunk = 1024
    near = lambda j: jnp.minimum(j, groups - 1)
    far = lambda j: jnp.maximum(j - groups, 0)
    cols = pl.BlockSpec((width, group), lambda j: (0, near(j)))
    bias = pl.BlockSpec((group,), lambda j: (near(j),))
    act = pl.BlockSpec((tokens, group), lambda j: (0, near(j)))
    wide = pl.BlockSpec((tokens, chunk), lambda j: (0, far(j)))
    vec = whole((width,))
    full = whole((tokens, width))
    one = whole((tokens, 1))
    return pl.pallas_call(
        forward_kernel,
        grid=(groups + hidden // chunk,),
        in_specs=[
            smem(), smem(), full, cols, cols, cols,
            pl.BlockSpec((group, width), lambda j: (near(j), 0)), bias, bias, vec, vec, vec,
            pl.BlockSpec((width, chunk), lambda j: (0, far(j))),
            pl.BlockSpec((chunk,), lambda j: (far(j),)),
            pl.BlockSpec((chunk, width), lambda j: (far(j), 0)), vec, vec, vec,
        ],
        out_specs=[act] * 4 + [whole((rows, H, length)), hbm(), hbm(), one, wide, wide, full, one]
        + [whole((rows * slots, width)), whole((rows * slots, width + 128))],
        out_shape=[shaped((tokens, width), bf16)] * 4
        + [
            shaped((rows, H, length), f32),
            shaped((tokens, width), bf16),
            shaped((tokens, width), bf16),
            shaped((tokens, 1), f32),
            shaped((tokens, hidden), bf16),
            shaped((tokens, hidden), bf16),
            shaped((tokens, width), bf16),
            shaped((tokens, 1), f32),
            shaped((rows * slots, width), f32),
            shaped((rows * slots, width + 128), bf16),
        ],
        scratch_shapes=[
            pltpu.VMEM((rows, length, length), f32),
            pltpu.VMEM((tokens, width), f32),
            pltpu.VMEM((tokens, width), bf16),
            pltpu.VMEM((tokens, width), bf16),
            pltpu.SemaphoreType.DMA((2,)),
        ],
        compiler_params=params(60 << 20),
        cost_estimate=cost(8 * tokens * width * (width + hidden), 50 << 20),
        name="forward",
    )(lens, targets, x, wq, wk, wv, wo, bq, bv, bo, gain1, shift1, wu, bu, wd, bd, gain2, shift2)


def match_kernel(
    lens_ref, pool_ref, gain, inv_ref, *refs,
):
    row_refs, refs = refs[:8], refs[8:]
    (
    xhat_hbm, active_hbm, loss_out, grad_hbm, vec_out, send_hbm, keep_hbm, rows_ref, active_ref, xhat_ref, grad_out, both_ref, sems,
    ) = refs
    copies = Copies(sems)
    copies.start("xhat", xhat_hbm, xhat_ref)
    copies.start("active", active_hbm, active_ref)
    width = pool_ref.shape[1]
    slots = pool_ref.shape[0]
    rows, row_slots = lens_ref.shape
    length = xhat_ref.shape[0] // rows
    total = rows_ref.shape[1]
    outer = total // 4 // slots
    each = total // 4
    for i, block in enumerate(row_refs):
        rows_ref[i // 4, i % 4 * each : (i % 4 + 1) * each, :] = block[...].reshape(each, -1)
    spot = lax.broadcasted_iota(jnp.int32, (1, total), 1)
    group = spot // slots
    cores, sides, outers = group // (2 * outer), group // outer % 2, group % outer
    device = (Place()[4] ^ outers) * 2 + (Place()[3] ^ sides)
    numbers = ((Place()[1] ^ cores) * (2 * outer) + device) * slots + spot % slots
    passage_side = Place()[0]
    query_side = 1 - passage_side
    chunk = min(512, total)
    lane = lax.broadcasted_iota(jnp.int32, (8, 128), 1)
    passage_marks = rows_ref[passage_side, :, width:]
    passage_live = dot_rows((lane == 0).astype(bf16), passage_marks)[:1] > 0
    query_count = jnp.sum(rows_ref[query_side, :, width:][:, :1].astype(f32))
    per_query = 1.0 / query_count

    def part(i, carry):
        loss, as_query, as_passage = carry
        at = pl.ds(pl.multiple_of(i * chunk, chunk), chunk)
        marks = rows_ref[query_side, at, width:].astype(f32)
        live = marks[:, 0:1] > 0
        target = marks[:, 1:2].astype(jnp.int32) * 64 + marks[:, 2:3].astype(jnp.int32)
        queries = rows_ref[query_side, at, :width]
        passages = rows_ref[passage_side, :, :width]
        scores = dot_rows(queries, passages) * inverse_temp
        scores = jnp.where(passage_live, scores, masked_score)
        top = jnp.max(scores, axis=-1, keepdims=True)
        log_sum = top + jnp.log(jnp.sum(jnp.exp(scores - top), axis=-1, keepdims=True))
        is_target = numbers == target
        picked = jnp.sum(jnp.where(is_target, scores, 0.0), axis=-1, keepdims=True)
        loss = loss + jnp.sum(jnp.where(live, log_sum - picked, 0.0))
        chances = jnp.where(passage_live, jnp.exp(scores - log_sum), 0.0)
        grad = jnp.where(live, (chances - is_target.astype(f32)) * per_query, 0.0).astype(bf16)
        as_passage = as_passage + dot_cols(grad[:, :128], queries)[:slots]
        own = dot(grad[:slots], passages)
        as_query = jnp.where(i == 0, own, as_query)
        return loss, as_query, as_passage

    zeros = jnp.zeros((slots, width), f32)
    carry = (jnp.float32(0), zeros, zeros)
    if total == chunk:
        carry = part(0, carry)
    else:
        carry = lax.fori_loop(0, total // chunk, part, carry)
    loss, as_query, as_passage = carry
    loss_out[0, 0] = loss * per_query
    grad_unit = jnp.where(passage_side == 1, as_query, as_passage) * inverse_temp
    pooled = pool_ref[...]
    inverse = lax.rsqrt(jnp.sum(pooled * pooled, axis=-1, keepdims=True) + pool_eps)
    along = jnp.sum(grad_unit * pooled, axis=-1, keepdims=True)
    grad_pooled = inverse * grad_unit - pooled * (inverse * inverse * inverse) * along
    gain = line(gain)
    sums = []
    copies.wait("xhat")
    for row in range(rows):
        at = slice(row * length, (row + 1) * length)
        own = slice(row * row_slots, (row + 1) * row_slots)
        seg = segment_of(lens_ref, row, lax.broadcasted_iota(jnp.int32, (row_slots, length), 1))
        member = (seg == lax.broadcasted_iota(jnp.int32, (row_slots, length), 0)).astype(f32)
        count = jnp.maximum(jnp.sum(member, axis=-1, keepdims=True), 1.0)
        member = member.astype(bf16)
        high, low = split_low(grad_pooled[own] / count)
        grad_final = dot_cols(member, high) + dot_cols(member, low)
        scaled = xhat_ref[at, :].astype(f32)
        grad_sum = norm_back(grad_final, scaled, inv_ref[at, :], gain)
        grad_low = grad_sum.astype(bf16)
        grad_out[at, :] = grad_low
        sums.append(
            (
                jnp.sum(grad_final * scaled, axis=0, keepdims=True),
                jnp.sum(grad_final, axis=0, keepdims=True),
                jnp.sum(grad_low.astype(f32), axis=0, keepdims=True),
            )
        )
    for i in range(3):
        vec_out[i : i + 1, :] = sum(each[i] for each in sums)
    copies.start("grad", grad_out, grad_hbm)
    copies.wait("active")
    _, parts, sides, half, share = both_ref.shape
    turned = jnp.transpose(grad_out[...])
    for z in range(parts):
        at = slice(z * sides * share, (z + 1) * sides * share)
        both = dot(turned, active_ref[:, at]).astype(bf16)
        for core in range(2):
            for y in range(sides):
                lanes = slice(y * share, (y + 1) * share)
                both_ref[core, z, y] = both[core * half : (core + 1) * half, lanes]
        copies.start((z, 0), both_ref.at[Place()[5], z], send_hbm.at[z])
        copies.start((z, 1), both_ref.at[Place()[1], z], keep_hbm.at[z])
    copies.wait("grad", *[(z, i) for z in range(parts) for i in range(2)])


def match(lens, rows, pooled, xhat, inverse, gain, active):
    tokens, width = xhat.shape
    slots = pooled.shape[0]
    vmem = pl.BlockSpec(memory_space=pltpu.VMEM)
    return pl.pallas_call(
        match_kernel,
        in_specs=[smem()] + [vmem] * 11 + [hbm(), hbm()],
        out_specs=[smem(), hbm(), vmem, hbm(), hbm()],
        out_shape=[
            shaped((1, 1), f32),
            shaped((tokens, width), bf16),
            shaped((8, width), f32),
            shaped((4, 2, width // 2, active.shape[1] // 8), bf16),
            shaped((4, 2, width // 2, active.shape[1] // 8), bf16),
        ],
        scratch_shapes=[
            pltpu.VMEM((2, rows[0].size * 4 // (width + 128), width + 128), bf16),
            pltpu.VMEM(active.shape, bf16),
            pltpu.VMEM((tokens, width), bf16),
            pltpu.VMEM((tokens, width), bf16),
            pltpu.VMEM((2, 4, 2, width // 2, active.shape[1] // 8), bf16),
            pltpu.SemaphoreType.DMA((11,)),
        ],
        compiler_params=params(60 << 20),
        cost_estimate=cost(2e9, 10 << 20),
        name="match",
    )(lens, pooled, gain, inverse, *rows, xhat, active)


def hidden_kernel(
    grad_hbm, slope_hbm, wd_hbm, low_hbm, hidden_hbm, bias_out, send_hbm,
    grad_ref, slope_ref, wd_ref, low_ref, hidden_ref, send_ref, sems, send_sems,
):
    parts, width, chunk = 4, wd_ref.shape[1], wd_ref.shape[0] // 4

    def span(j):
        return pl.ds(pl.multiple_of(j * chunk, chunk), chunk)

    def wd_copy(j):
        return pltpu.make_async_copy(wd_hbm.at[span(j), :], wd_ref.at[span(j), :], sems.at[2 + j])

    def slope_copy(j):
        return pltpu.make_async_copy(slope_hbm.at[:, span(j)], slope_ref.at[:, span(j)], sems.at[6 + j])

    def hidden_copy(j):
        return pltpu.make_async_copy(hidden_ref.at[:, span(j)], hidden_hbm.at[:, span(j)], sems.at[10 + j])

    def send_copy(i):
        return pltpu.make_async_copy(send_ref.at[i], send_hbm.at[i], send_sems.at[i])

    grad_copy = pltpu.make_async_copy(grad_hbm, grad_ref, sems.at[0])
    low_copy = pltpu.make_async_copy(low_hbm, low_ref, sems.at[1])
    grad_copy.start()
    wd_copy(0).start()
    slope_copy(0).start()
    low_copy.start()
    for j in range(1, parts):
        wd_copy(j).start()
        slope_copy(j).start()
    grad_copy.wait()

    def step(j, carry):
        at = span(j)
        wd_copy(j).wait()
        slope_copy(j).wait()
        grad = dot_rows(grad_ref[...], wd_ref[at, :]) * slope_ref[:, at].astype(f32)
        grad_low = grad.astype(bf16)
        hidden_ref[:, at] = grad_low
        bias_out[:, at] = jnp.sum(grad_low.astype(f32), axis=0, keepdims=True)
        hidden_copy(j).start()

        @pl.when(j == 0)
        def _():
            low_copy.wait()

        @pl.when(j // 2 == Place()[5])
        def _():
            send_ref[j % 2] = dot_cols(low_ref[...], hidden_ref[:, at]).astype(bf16)
            send_copy(j % 2).start()

        return carry

    lax.fori_loop(0, parts, step, 0)
    for j in range(parts):
        hidden_copy(j).wait()
    for i in range(2):
        send_copy(i).wait()


def hidden_grad(grad, slope, wd, low):
    tokens, width = grad.shape
    hidden = wd.shape[0]
    chunk = hidden // 4
    return pl.pallas_call(
        hidden_kernel,
        in_specs=[hbm()] * 4,
        out_specs=[hbm(), pl.BlockSpec(memory_space=pltpu.VMEM), hbm()],
        out_shape=[
            shaped((tokens, hidden), bf16),
            shaped((1, hidden), f32),
            shaped((2, width, chunk), bf16),
        ],
        scratch_shapes=[
            pltpu.VMEM((tokens, width), bf16),
            pltpu.VMEM((tokens, hidden), bf16),
            pltpu.VMEM((hidden, width), bf16),
            pltpu.VMEM((tokens, width), bf16),
            pltpu.VMEM((tokens, hidden), bf16),
            pltpu.VMEM((2, width, chunk), bf16),
            pltpu.SemaphoreType.DMA((14,)),
            pltpu.SemaphoreType.DMA((2,)),
        ],
        compiler_params=params(60 << 20),
        cost_estimate=cost(3 * tokens * width * hidden, 22 << 20),
        name="hidden_grad",
    )(grad, slope, wd, low)


def feed_back_kernel(
    fast, inv_ref, gain, grad_hbm, hidden_hbm, wu_hbm, wo_hbm, xhat_hbm, low_hbm, mixed_hbm, got_hbm,
    vec_out, branch_hbm, back_hbm, send_hbm, keep_hbm, *refs,
):
    outs, refs = refs[: 4 * fast], refs[4 * fast :]
    grad_ref, hidden_ref, wu_ref, wo_ref, xhat_ref, low_ref, mixed_ref, got_ref, *refs = refs
    branch_ref, back_ref, send_ref, keep_ref, acc_ref, part_ref, sems, *pieces = refs
    tokens, width = grad_ref.shape
    half, narrow, chunk, parts = tokens // 2, width // 2, part_ref.shape[1], 4
    copies = Copies(sems)
    copies.start("grad", grad_hbm, grad_ref)
    for j in range(parts):
        at = slice(j * chunk, (j + 1) * chunk)
        copies.start(("hidden", j), hidden_hbm.at[:, at], hidden_ref.at[:, at])
        copies.start(("wu", j), wu_hbm.at[:, at], wu_ref.at[:, at])
        if j == 0:
            copies.start("low", low_hbm, low_ref)
            copies.start("got", got_hbm, got_ref)
    copies.start("xhat", xhat_hbm, xhat_ref)
    copies.start("wo", wo_hbm, wo_ref)
    copies.start("mixed", mixed_hbm, mixed_ref)
    copies.wait("grad")
    acc_ref[...] = grad_ref[...].astype(f32)
    for j in range(parts):
        at = slice(j * chunk, (j + 1) * chunk)
        copies.wait(("hidden", j), ("wu", j))
        for part in range(2):
            rows = slice(part * half, (part + 1) * half)
            acc_ref[rows, :] += dot_rows(hidden_ref[rows, at], wu_ref[:, at])
        if j == 0:
            copies.wait("low", "got")
        if not fast:
            continue
        size = pieces[0].shape[2]
        first = pieces[0].shape[3] - chunk

        @pl.when(j // 2 == Place()[1])
        def _():
            part_ref[...] = dot_cols(low_ref[...], hidden_ref[:, at]) + got_ref[j % 2].astype(f32)
            if j % 2 == 0:
                cut_rows(part_ref, pieces[:2], slice(0, chunk), False, size)
            else:
                lanes = slice(chunk, chunk + first)
                cut_rows(part_ref.at[:, :first], pieces[:2], lanes, False, size)
                lanes = slice(narrow, narrow + chunk - first)
                cut_rows(part_ref.at[:, first:], pieces[2:], lanes, True, size)

    for i in range(4 * fast):
        copies.start(("piece", i), pieces[i], outs[i])
    copies.wait("xhat", "wo", "mixed")
    tallies = []
    for part in range(2):
        rows = slice(part * half, (part + 1) * half)
        grad = acc_ref[rows, :]
        scaled = xhat_ref[rows, :].astype(f32)
        grad_low = norm_back(grad, scaled, inv_ref[rows, :], line(gain)).astype(bf16)
        branch_ref[rows, :] = grad_low
        copies.start(("branch", part), branch_ref.at[rows, :], branch_hbm.at[rows, :])
        back_ref[rows, :] = dot_rows(grad_low, wo_ref[...]).astype(bf16)
        copies.start(("back", part), back_ref.at[rows, :], back_hbm.at[rows, :])
        tallies.append(
            (
                jnp.sum(grad * scaled, axis=0, keepdims=True),
                jnp.sum(grad, axis=0, keepdims=True),
                jnp.sum(grad_low.astype(f32), axis=0, keepdims=True),
            )
        )
    for i in range(3):
        vec_out[i : i + 1, :] = tallies[0][i] + tallies[1][i]
    for i, out in ((1, send_ref), (0, keep_ref)):
        at = pl.ds(pl.multiple_of(Place()[1 + 4 * i] * narrow, narrow), narrow)
        out[...] = dot_cols(mixed_ref[...], branch_ref[:, at]).astype(bf16)
        copies.start(("out", i), out, (keep_hbm, send_hbm)[i])
    copies.wait(*[("piece", i) for i in range(4 * fast)])
    copies.wait(*[(name, i) for name in ("branch", "back", "out") for i in range(2)])


def feed_back(grad, grad_hidden, wu, wo, xhat, inverse, gain, low, mixed, got, fast):
    tokens, width = grad.shape
    hidden = wu.shape[1]
    chunk = hidden // 4
    narrow = width // 2
    first = chunk + width // 3
    pieces = [(2, 4, width // 16, first)] * 2 + [(2, 4, width // 16, 2 * chunk - first + narrow)] * 2
    pieces = [(each, bf16) for each in pieces] if fast else []
    full, strip = ((tokens, width), bf16), ((width, narrow), bf16)
    vmem = pl.BlockSpec(memory_space=pltpu.VMEM)
    scratch = [
        full, ((tokens, hidden), bf16), ((width, hidden), bf16), ((width, width), bf16), full, full, full,
        ((2, width, chunk), bf16), full, full, strip, strip, ((tokens, width), f32), ((width, chunk), f32),
    ]
    return pl.pallas_call(
        partial(feed_back_kernel, int(fast)),
        in_specs=[vmem, vmem] + [hbm()] * 8,
        out_specs=[vmem] + [hbm()] * (4 + len(pieces)),
        out_shape=[
            shaped((8, width), f32), shaped(*full), shaped(*full), shaped(*strip), shaped(*strip)
        ]
        + [shaped(*each) for each in pieces],
        scratch_shapes=[pltpu.VMEM(*each) for each in scratch]
        + [pltpu.SemaphoreType.DMA((24,))]
        + [pltpu.VMEM(*each) for each in pieces],
        compiler_params=params(60 << 20),
        cost_estimate=cost(4 * tokens * width * hidden, 30 << 20),
        name="feed_back",
    )(inverse, gain, grad, grad_hidden, wu, wo, xhat, low, mixed, got)


def join_kernel(keep_ref, got_ref, *refs):
    outs, acc_ref = refs[2:4], refs[4]
    acc_ref[...] = keep_ref[...].astype(f32) + got_ref[...].astype(f32)
    cut_rows(acc_ref, outs, slice(None), True, outs[0].shape[2])


def join_out(keep, got, pieces):
    width, narrow = keep.shape
    piece = pl.BlockSpec((2, 4, width // 16, narrow), lambda j: (0, 0, 0, 0))
    return pl.pallas_call(
        join_kernel,
        grid=(1,),
        in_specs=[whole(keep.shape), whole(got.shape)]
        + [pl.BlockSpec(memory_space=pl.ANY)] * 2,
        out_specs=[piece] * 2,
        out_shape=[shaped(each.shape, bf16) for each in pieces],
        input_output_aliases={2 + i: i for i in range(2)},
        scratch_shapes=[pltpu.VMEM((width, narrow), f32)],
        compiler_params=params(8 << 20),
        cost_estimate=cost(0, 3 << 20),
        name="join_out",
    )(keep, got, *pieces)


def probs_kernel(group, lens_ref, q_ref, k_ref, lse_ref, *refs):
    out, mask_ref = refs[-2:]
    step = pl.program_id(0)
    rows, length, _ = mask_ref.shape

    @pl.when(step == 0)
    def _():
        fill_mask(lens_ref, mask_ref)

    lane = lax.broadcasted_iota(jnp.int32, (1, 128), 1)
    pairs = q_ref.shape[1] // 128
    for pair in range(pairs):
        lanes = slice(pair * 128, (pair + 1) * 128)
        for row in range(rows):
            at = slice(row * length, (row + 1) * length)
            q = q_ref[at, lanes] * bf16(64 ** (-0.5))
            k = k_ref[at, lanes]
            for head in range(2):
                own = jnp.where((lane < 64) == (head == 0), q, bf16(0))
                place = ((step + group) * pairs + pair) * 2 + head
                log_total = lse_ref[row, pl.ds(place, 1), :]
                scores = dot_rows(k, own) + mask_ref[row]
                out[0, (row * pairs + pair) * 2 + head] = jnp.exp(scores - log_total).astype(bf16)


def probs_of(lens, q, k, lse, group, count, before=None):
    tokens, width = q.shape
    rows = lens.shape[0]
    length = tokens // rows
    lanes = 256
    heads = rows * lanes // 64
    act = pl.BlockSpec((tokens, lanes), lambda j: (0, j + group))
    return pl.pallas_call(
        partial(probs_kernel, group),
        grid=(count,),
        in_specs=[smem(), act, act, whole(lse.shape)] + ([] if before is None else [hbm()]),
        out_specs=pl.BlockSpec((1, heads, length, length), lambda j: (j + group, 0, 0, 0)),
        out_shape=shaped((width // lanes, heads, length, length), bf16),
        input_output_aliases={} if before is None else {4: 0},
        scratch_shapes=[pltpu.VMEM((rows, length, length), f32)],
        compiler_params=params(60 << 20),
        cost_estimate=cost(count * 4 * heads * length * length * 256, count << 22),
        name="probs",
    )(lens, q, k, lse, *(() if before is None else (before,)))


def attend_back_kernel(
    q_ref, k_ref, v_ref, probs_ref, mixed_ref, grad_ref, x_ref,
    first_sums, second_sums, up_sums, out, vec_out, send_out, keep_out, own_out, other_out, sums_ref, pack_ref,
):
    step = pl.program_id(0)
    length = probs_ref.shape[2]
    rows = q_ref.shape[0] // length

    lane = lax.broadcasted_iota(jnp.int32, (1, 128), 1)
    scale = 64 ** (-0.5)
    pairs = q_ref.shape[1] // 128
    for pair in range(pairs):
        lanes = slice(pair * 128, (pair + 1) * 128)
        query_sums, value_sums = [], []
        for row in range(rows):
            tokens = slice(row * length, (row + 1) * length)
            q = q_ref[tokens, lanes] * bf16(scale)
            k = k_ref[tokens, lanes]
            v = v_ref[tokens, lanes]
            grad = grad_ref[tokens, lanes]
            high, low = split_low(grad.astype(f32) * mixed_ref[tokens, lanes].astype(f32))
            grad_v = grad_k = grad_q = 0.0
            for head in range(2):
                mine = (lane < 64) == (head == 0)
                ones = jnp.broadcast_to(jnp.where(mine, 1.0, 0.0), (8, 128)).astype(bf16)
                inner = (dot_rows(ones, high) + dot_rows(ones, low))[:1]
                own_q = jnp.where(mine, q, bf16(0))
                own_grad = jnp.where(mine, grad, bf16(0))
                probs = probs_ref[0, (row * pairs + pair) * 2 + head]
                grad_scores = (probs.astype(f32) * (dot_rows(v, own_grad) - inner)).astype(bf16)
                grad_v = grad_v + dot(probs, own_grad)
                grad_k = grad_k + dot(grad_scores, own_q)
                grad_q = grad_q + dot_cols(jnp.where(mine, k, bf16(0)), grad_scores)
            grad_q = (jnp.transpose(grad_q) * scale).astype(bf16)
            grad_v = grad_v.astype(bf16)
            out[0, tokens, lanes] = grad_q
            out[1, tokens, lanes] = grad_k.astype(bf16)
            out[2, tokens, lanes] = grad_v
            query_sums.append(jnp.sum(grad_q.astype(f32), axis=0, keepdims=True))
            value_sums.append(jnp.sum(grad_v.astype(f32), axis=0, keepdims=True))
        vec_out[0:1, lanes] = sum(query_sums)
        vec_out[1:2, lanes] = sum(value_sums)
        at = pl.ds(pl.multiple_of((step * pairs + pair) * 128, 128), 128)
        sums_ref[0:1, at] = sum(query_sums)
        sums_ref[1:2, at] = sum(value_sums)
    for core, target in ((Place()[5], send_out), (Place()[1], keep_out)):
        lanes = pl.ds(pl.multiple_of(core * 128, 128), 128)
        grads = jnp.concatenate([out[i, :, lanes] for i in range(3)], axis=1)
        target[...] = dot_cols(x_ref[...], grads).astype(bf16)

    @pl.when(step == pl.num_programs(0) - 1)
    def _():
        sums = [sums_ref[i : i + 1, :] for i in range(2)]
        sums += [first_sums[2:3, :], second_sums[2:3, :], first_sums[0:1, :], first_sums[1:2, :]]
        sums += [second_sums[0:1, :], second_sums[1:2, :]]
        width = x_ref.shape[1]
        share = width // 8
        pack_ref[...] = jnp.zeros(pack_ref.shape, f32)
        for n in range(12):
            for d in range(8):
                if n < 8:
                    piece = sums[n][:, d * share : (d + 1) * share]
                else:
                    piece = up_sums[:, (d * 4 + n - 8) * share : (d * 4 + n - 7) * share]
                row = (d * 2 + n // 3 % 2) * (width // 16) + n % 3
                pack_ref[n // 6, row : row + 1, :share] = piece
        own_out[...] = pack_ref[Place()[1]].astype(bf16)
        other_out[...] = pack_ref[Place()[5]].astype(bf16)


def attend_back(q, k, v, probs, mixed, grad, x, first_sums, second_sums, up_sums):
    tokens, width = q.shape
    group = 256
    act = pl.BlockSpec((tokens, group), lambda j: (0, j))
    scores = pl.BlockSpec((1,) + probs.shape[1:], lambda j: (j, 0, 0, 0))
    return pl.pallas_call(
        attend_back_kernel,
        grid=(width // group,),
        in_specs=[act, act, act, scores, act, act, whole(x.shape)]
        + [whole(each.shape) for each in (first_sums, second_sums, up_sums)],
        out_specs=[
            pl.BlockSpec((3, tokens, group), lambda j: (0, 0, j)),
            pl.BlockSpec((8, group), lambda j: (0, j)),
            pl.BlockSpec((width, 384), lambda j: (0, j)),
            pl.BlockSpec((width, 384), lambda j: (0, j)),
            whole((width, 128)),
            whole((width, 128)),
        ],
        out_shape=[
            shaped((3, tokens, width), bf16),
            shaped((8, width), f32),
            shaped((width, width // group * 384), bf16),
            shaped((width, width // group * 384), bf16),
            shaped((width, 128), bf16),
            shaped((width, 128), bf16),
        ],
        scratch_shapes=[
            pltpu.VMEM((8, width), f32),
            pltpu.VMEM((2, width, 128), f32),
        ],
        compiler_params=params(60 << 20),
        cost_estimate=cost(20 * tokens * probs.shape[2] * width, 30 << 20),
        name="attend_back",
    )(q, k, v, probs, mixed, grad, x, first_sums, second_sums, up_sums)


def input_kernel(branch_hbm, grads_hbm, wq_hbm, wk_hbm, wv_hbm, out_hbm, branch_ref, grads_ref, weights_ref, out_ref, sems):
    copies = Copies(sems)
    for m, weight in enumerate((wq_hbm, wk_hbm, wv_hbm)):
        copies.start(("w", m), weight, weights_ref.at[m])
        copies.start(("g", m), grads_hbm.at[m], grads_ref.at[m])
        if m == 0:
            copies.start("branch", branch_hbm, branch_ref)
    tokens = out_ref.shape[0]
    parts = 4
    for m in range(3):
        copies.wait(("w", m), ("g", m))
        if m == 0:
            copies.wait("branch")
        for part in range(parts):
            rows = slice(part * tokens // parts, (part + 1) * tokens // parts)
            before = branch_ref[rows, :].astype(f32) if m == 0 else out_ref[rows, :]
            out_ref[rows, :] = before + dot_rows(grads_ref[m, rows, :], weights_ref[m])
            if m == 2:
                copies.start(("out", part), out_ref.at[rows, :], out_hbm.at[rows, :])
    copies.wait(*[("out", part) for part in range(parts)])


def input_grad(branch, grads, wq, wk, wv):
    tokens, width = branch.shape
    return pl.pallas_call(
        input_kernel,
        in_specs=[hbm()] * 5,
        out_specs=hbm(),
        out_shape=shaped((tokens, width), f32),
        scratch_shapes=[
            pltpu.VMEM((tokens, width), bf16),
            pltpu.VMEM((3, tokens, width), bf16),
            pltpu.VMEM((3, width, width), bf16),
            pltpu.VMEM((tokens, width), f32),
            pltpu.SemaphoreType.DMA((11,)),
        ],
        compiler_params=params(60 << 20),
        cost_estimate=cost(6 * tokens * width * width, 13 << 20),
        name="input_grad",
    )(branch, grads, wq, wk, wv)


def down_kernel(keep_hbm, got_hbm, *refs):
    outs, refs = refs[:4], refs[4:]
    keep_ref, got_ref, acc_ref, sems, *pieces = refs
    parts, _, half, _ = got_ref.shape
    copies = Copies(sems)
    for z in range(parts):
        copies.start(("keep", z), keep_hbm.at[z], keep_ref.at[z])
        copies.start(("got", z), got_hbm.at[z], got_ref.at[z])
    strip = half // 4
    for z in range(parts):
        copies.wait(("keep", z), ("got", z))
        for y in range(2):
            acc_ref[...] = keep_ref[z, y].astype(f32) + got_ref[z, y].astype(f32)
            for rel in range(2):
                at = pl.multiple_of((Place()[2] ^ rel) * 2 * strip, 2 * strip)
                pieces[rel][y, z] = acc_ref[pl.ds(at, strip), :].astype(bf16)

                @pl.when(Place()[3] == y ^ rel)
                def _():
                    for x in range(2):
                        rows = slice((2 * x + 1) * strip, (2 * x + 2) * strip)
                        pieces[2 + rel][x, z] = acc_ref[rows, :].astype(bf16)

        for i in range(4):
            copies.start(("piece", i, z), pieces[i].at[:, z], outs[i].at[:, z])
    copies.wait(*[("piece", i, z) for i in range(4) for z in range(parts)])


def down_grad(keep, got):
    parts, _, half, share = got.shape
    piece = (2, parts, half // 4, share)
    return pl.pallas_call(
        down_kernel,
        in_specs=[hbm()] * 2,
        out_specs=[hbm()] * 4,
        out_shape=[shaped(piece, bf16)] * 4,
        scratch_shapes=[
            pltpu.VMEM(got.shape, bf16),
            pltpu.VMEM(got.shape, bf16),
            pltpu.VMEM((half, share), f32),
            pltpu.SemaphoreType.DMA((24,)),
        ]
        + [pltpu.VMEM(piece, bf16)] * 4,
        compiler_params=params(60 << 20),
        cost_estimate=cost(0, 7 << 20),
        name="down_keep",
    )(keep, got)


def cut_rows(acc_ref, outs, at, by_y, size):
    outer = acc_ref.shape[0] // 4 // size
    for rel, out in enumerate(outs):
        for z in range(outer):
            for i in range(2):
                y, x = (Place()[3] ^ rel, i) if by_y else (i, Place()[2] ^ rel)
                row = pl.multiple_of(((z * 2 + y) * 2 + x) * size, size)
                out[i, z, :, at] = acc_ref[pl.ds(row, size), :].astype(bf16)


def head_kernel(vec_ref, got_vec_ref, keep_hbm, got_hbm, *refs):
    outs, (keep_ref, got_ref, acc_ref, sems) = refs[:4], refs[4:]
    width, total = keep_ref.shape
    half, size = outs[0].shape[3], outs[0].shape[2]
    parts = width // 4 // size
    span = width // parts
    copies = Copies(sems)
    for z in range(parts):
        rows = slice(z * span, (z + 1) * span)
        copies.start(("keep", z), keep_hbm.at[rows, :], keep_ref.at[rows, :])
        copies.start(("got", z), got_hbm.at[rows, :], got_ref.at[rows, :])
    for z in range(parts):
        rows = slice(z * span, (z + 1) * span)
        acc_ref[:, total:] = vec_ref[rows, :].astype(f32) + got_vec_ref[rows, :].astype(f32)
        copies.wait(("keep", z), ("got", z))
        acc_ref[:, :total] = keep_ref[rows, :].astype(f32) + got_ref[rows, :].astype(f32)
        for rel in range(2):
            for i in range(2):
                at = pl.multiple_of((i * 2 + (Place()[2] ^ rel)) * size, size)
                outs[rel][i, z] = acc_ref[pl.ds(at, size), :half].astype(bf16)
                at = pl.multiple_of(((Place()[3] ^ rel) * 2 + i) * size, size)
                outs[2 + rel][i, z] = acc_ref[pl.ds(at, size), half:].astype(bf16)


def head_grad(keep, vectors, got_vectors, got):
    width, total = keep.shape
    piece_shape = (2, 4, width // 16, (total + 128) // 2)
    vmem = pl.BlockSpec(memory_space=pltpu.VMEM)
    return pl.pallas_call(
        head_kernel,
        in_specs=[vmem, vmem] + [hbm()] * 2,
        out_specs=[vmem] * 4,
        out_shape=[shaped(piece_shape, bf16)] * 4,
        scratch_shapes=[
            pltpu.VMEM(keep.shape, bf16),
            pltpu.VMEM(keep.shape, bf16),
            pltpu.VMEM((width // 4, total + 128), f32),
            pltpu.SemaphoreType.DMA((8,)),
        ],
        compiler_params=params(12 << 20),
        cost_estimate=cost(0, 6 << 20),
        name="head_keep",
    )(vectors, got_vectors, keep, got)


def mix_kernel(which, parts, *refs):
    ins, outs = refs[:-parts], refs[-parts:]
    for rel, out in enumerate(outs):
        at = Place()[which] ^ rel if parts > 1 else 0
        total = ins[0][at].astype(f32)
        for ref in ins[1:]:
            total = total + ref[at].astype(f32)
        out[...] = total.astype(bf16)


def mix(which, arrays):
    parts = arrays[0].shape[0]
    return pl.pallas_call(
        partial(mix_kernel, which, parts),
        in_specs=[pl.BlockSpec(memory_space=pltpu.VMEM)] * len(arrays),
        out_specs=[pl.BlockSpec(memory_space=pltpu.VMEM)] * parts,
        out_shape=[shaped(arrays[0].shape[1:], bf16)] * parts,
        compiler_params=params(8 << 20),
        cost_estimate=cost(0, 2 * arrays[0].size * (len(arrays) + 1)),
        name="mix",
    )(*arrays)


def first_exchange(parts):
    return [parts[0], swap(parts[1], "tower", 2), parts[2], swap(parts[3], "dp", 1)]


def second_exchange(parts):
    return [parts[0], swap(parts[1], "dp", 1), parts[2], swap(parts[3], "tower", 2)]


def cross_kernel(*refs):
    ins, outs = refs[:4], refs[4:]
    for i in range(2):
        mine, got = ins[2 * i : 2 * i + 2]
        for rel in range(2):
            at = Place()[3 - i] ^ rel
            outs[2 * i + rel][...] = (mine[at].astype(f32) + got[at].astype(f32)).astype(bf16)


def cross(parts):
    vmem = pl.BlockSpec(memory_space=pltpu.VMEM)
    return pl.pallas_call(
        cross_kernel,
        in_specs=[vmem] * 4,
        out_specs=[vmem] * 4,
        out_shape=[shaped(each.shape[1:], bf16) for each in parts],
        compiler_params=params(8 << 20),
        cost_estimate=cost(0, 6 << 20),
        name="cross",
    )(*parts)


def outer_kernel(axis, *refs):
    ins, outs = refs[:4], refs[4:]
    for rel, out in enumerate(outs):
        at = Place()[4] ^ rel
        sums = [ins[2 * i][at].astype(f32) + ins[2 * i + 1][at].astype(f32) for i in range(2)]
        out[...] = jnp.concatenate(sums, axis=axis).astype(bf16)


def cut_halves(axis, parts):
    vmem = pl.BlockSpec(memory_space=pltpu.VMEM)
    outer = parts[0].shape[0]
    shape = list(parts[0].shape[1:])
    shape[axis] += parts[2].shape[1 + axis]
    return pl.pallas_call(
        partial(outer_kernel, axis),
        in_specs=[vmem] * 4,
        out_specs=[vmem] * outer,
        out_shape=[shaped(tuple(shape), bf16)] * outer,
        compiler_params=params(8 << 20),
        cost_estimate=cost(0, 3 << 20),
        name="cut_halves",
    )(*parts)


def exchange_outer(parts):
    return [parts[0]] + [swap(part, "dp", 2 * rel) for rel, part in enumerate(parts) if rel]


def join_outer(parts):
    return mix(4, [part[None] for part in parts])[0]


def spread_kernel(kind, *refs):
    blocks, outs = refs[:4], refs[4:]
    core, far = Place()[1], Place()[2]
    share = outs[0].shape[0]
    for i, block in enumerate(blocks):
        c, x = core ^ (i >> 1), far ^ (i & 1)
        value = block[...].astype(f32)
        size = value.shape[0]
        rows = pl.ds(pl.multiple_of(x * size, size), size)
        if kind == "down":
            at = pl.multiple_of((c * 2 + x) * size, size)
            refs[-1][pl.ds(at, size), :] = value
            continue
        half = outs[1].shape[1] // 2
        if kind == "up":
            total = outs[0].shape[1] // 2
            wide = pl.ds(pl.multiple_of(c * total, total), total)
            narrow = pl.ds(pl.multiple_of(c * half, half), half)
            first = total // 3 * 2
            outs[0][rows, wide] = jnp.concatenate([value[:, :first], value[:, first + half :]], axis=1)
            outs[1][rows, narrow] = value[:, first : first + half]
        else:
            groups = half // 128
            for j in range(groups):
                lanes = pl.ds(pl.multiple_of(j * 256 + c * 128, 128), 128)
                for m in range(3):
                    outs[m][rows, lanes] = value[:, (j * 3 + m) * 128 : (j * 3 + m + 1) * 128]
            refs[-1][c * 2 + x] = value[:16, 3 * half :]
    if kind == "down":
        outs[0][...] = jnp.transpose(refs[-1][...])
    if kind == "head":
        for n in range(8):
            outs[3 + n][...] = refs[-1][n // 3, n % 3 : n % 3 + 1, :share].reshape(-1)
        last = [refs[-1][n // 3, n % 3 : n % 3 + 1, :share] for n in range(8, 12)]
        outs[11][...] = jnp.concatenate(last, axis=1).reshape(-1)


def spread(kind, block, far, shapes):
    blocks = [block, far, swap(block, "tower", 1), swap(far, "tower", 1)]
    return pl.pallas_call(
        partial(spread_kernel, kind),
        in_specs=[pl.BlockSpec(memory_space=pltpu.VMEM)] * 4,
        out_specs=[pl.BlockSpec(memory_space=pltpu.VMEM)] * len(shapes),
        out_shape=[shaped(shape, f32) for shape in shapes],
        scratch_shapes=[pltpu.VMEM((4, 16, 128) if kind == "head" else shapes[0][::-1], f32)],
        compiler_params=params(8 << 20),
        cost_estimate=cost(0, 2 << 20),
        name="spread_" + kind,
    )(*blocks)


def shards(
    layer_input,
    seg_lengths,
    positives,
    query_weight,
    key_weight,
    value_weight,
    out_weight,
    up_weight,
    down_weight,
    query_bias,
    value_offset_bias,
    out_bias,
    up_bias,
    down_bias,
    first_gain,
    first_shift,
    second_gain,
    latter_norm_translation,
):
    row_count = layer_input.shape[1]
    row_len = layer_input.shape[2]
    width = layer_input.shape[3]
    slot_count = seg_lengths.shape[2]
    token_count = row_count * row_len
    dp_count = lax.axis_size("dp")
    flat_in = layer_input.reshape(token_count, width)
    lens = seg_lengths.reshape(row_count, slot_count)

    (
        q, k, v, mixed, lse, low, first_scaled, first_inverse,
        active, slope, second_scaled, second_inverse, pooled, unit,
    ) = forward(
        lens, positives, flat_in, query_weight, key_weight, value_weight, out_weight,
        query_bias, value_offset_bias, out_bias, first_gain, first_shift,
        up_weight, up_bias, down_weight, down_bias, second_gain, latter_norm_translation,
    )
    rows, probs = gather_all(
        unit,
        lambda: probs_of(lens, q, k, lse, 0, 1),
        lambda before: probs_of(lens, q, k, lse, 1, width // 256 - 1, before),
    )
    loss, grad_second, second_sums, down_half, down_keep = match(
        lens, rows, pooled, second_scaled, second_inverse, second_gain, active
    )
    loss = loss.reshape(())
    share = width // dp_count
    fast = dp_count == 8 and lax.axis_size("tower") == 4
    grad_hidden, up_sums, up_half = hidden_grad(grad_second, slope, down_weight, low)
    if fast:
        got = swap(down_half, "tower", 1)
        got, grad_hidden, up_half = lax.optimization_barrier((got, grad_hidden, up_half))
        down_parts = down_grad(down_keep, got)
        up_half = swap(up_half, "tower", 1)
        down_parts, grad_hidden, up_half = lax.optimization_barrier(
            (down_parts, grad_hidden, up_half)
        )
        down_parts = first_exchange(down_parts)
    first_sums, grad_branch, grad_mixed, out_half, out_keep, *up_parts = feed_back(
        grad_second, grad_hidden, up_weight, out_weight, first_scaled, first_inverse,
        first_gain, low, mixed, up_half, fast,
    )
    if fast:
        down_parts, out_half = lax.optimization_barrier((down_parts, out_half))
        out_half = swap(out_half, "tower", 1)
        down_parts = cross(down_parts)
        down_parts, out_half = lax.optimization_barrier((down_parts, out_half))
        up_parts[2:] = join_out(out_keep, out_half, up_parts[2:])
        up_parts, down_parts, grad_mixed = lax.optimization_barrier((up_parts, down_parts, grad_mixed))
        up_parts = first_exchange(up_parts)
        down_parts = second_exchange(down_parts)
    grads, head_sums, head_half, head_keep, vectors, other_vectors = attend_back(
        q, k, v, probs, mixed, grad_mixed, flat_in, first_sums, second_sums, up_sums
    )
    if fast:
        up_parts, down_parts, grads, head_half, other_vectors = lax.optimization_barrier(
            (up_parts, down_parts, grads, head_half, other_vectors)
        )
    if fast:
        got = swap(head_half, "tower", 1)
        got_vectors = swap(other_vectors, "tower", 1)
        down_parts = cut_halves(0, down_parts)
        up_parts = cross(up_parts)
        up_parts, down_parts, got = lax.optimization_barrier((up_parts, down_parts, got))
        up_parts = second_exchange(up_parts)
        down_parts = exchange_outer(down_parts)
        parts = head_grad(head_keep, vectors, got_vectors, got)
        up_parts, down_parts, parts, grads = lax.optimization_barrier(
            (up_parts, down_parts, parts, grads)
        )
        parts = first_exchange(parts)
        up_parts = exchange_outer(cut_halves(1, up_parts))
        down_part = join_outer(down_parts)
        down_part, parts = lax.optimization_barrier((down_part, parts))
        parts = cross(parts)
        parts, grads = lax.optimization_barrier((parts, grads))
        parts = second_exchange(parts)
        grad_input = input_grad(grad_branch, grads, query_weight, key_weight, value_weight)
        up_parts, parts, grad_input = lax.optimization_barrier((up_parts, parts, grad_input))
        parts = cut_halves(1, parts)
        up_parts, parts = lax.optimization_barrier((up_parts, parts))
        parts = exchange_outer(parts)
        up_part = join_outer(up_parts)
        down_far, up_far = swap(down_part, "tower", 2), swap(up_part, "tower", 2)
        up_far, down_far, parts = lax.optimization_barrier((up_far, down_far, parts))
        head_part = join_outer(parts)
        head_far = swap(head_part, "tower", 2)
        (total_down,) = spread("down", down_part, down_far, [(4 * share, width)])
        total_up, total_out = spread(
            "up", up_part, up_far, [(share, up_weight.shape[1]), (share, width)]
        )
        total_down, total_up, total_out, head_far = lax.optimization_barrier(
            (total_down, total_up, total_out, head_far)
        )
        total_query, total_key, total_value, *sums = spread(
            "head", head_part, head_far,
            [(share, width)] * 3 + [(share,)] * 8 + [(4 * share,)],
        )
    else:
        grad_input = input_grad(grad_branch, grads, query_weight, key_weight, value_weight)
        outer = dp_count // 2
        vectors = jnp.concatenate(
            [
                vec.reshape(dp_count, -1)
                for vec in (
                    head_sums[0],
                    head_sums[1],
                    first_sums[2],
                    second_sums[2],
                    first_sums[0],
                    first_sums[1],
                    second_sums[0],
                    second_sums[1],
                    up_sums,
                )
            ],
            axis=1,
        ).astype(bf16)

        def by_rows(grad):
            return grad.astype(bf16).reshape(outer, 2, share, 2, 2, width).transpose(3, 4, 1, 0, 2, 5)

        square = jnp.stack(
            [dot_cols(flat_in, grads[i]) for i in range(3)] + [dot_cols(mixed, grad_branch)], axis=1
        )
        vectors = vectors.reshape(outer, 2, 2, 2, -1).transpose(2, 3, 1, 0, 4)
        vectors = jnp.pad(vectors, ((0, 0),) * 4 + ((0, width - vectors.shape[-1]),))
        down = dot_cols(active, grad_second).astype(bf16)
        down = down.reshape(outer, 2, 2, 2, share, width).transpose(2, 3, 1, 0, 4, 5)
        total_down = sum_group(down).reshape(4 * share, width)
        total_up = sum_group(by_rows(dot_cols(low, grad_hidden))).reshape(4, share, width)
        total_up = total_up.transpose(1, 0, 2).reshape(share, 4 * width)
        last = jnp.concatenate([by_rows(square), vectors[:, :, :, :, None]], axis=4)
        last = sum_group(last).reshape(4, share + 1, width)
        total_query, total_key, total_value, total_out = [last[i, :share] for i in range(4)]
        short = last[:, share, : share * 3].reshape(-1)
        sums = [short[i * share : (i + 1) * share] for i in range(8)] + [short[8 * share :]]
    grad_input = grad_input.reshape(layer_input.shape)
    return (
        loss,
        grad_input,
        total_query,
        total_key,
        total_value,
        total_out,
        total_up,
        total_down,
        sums[0],
        sums[1],
        sums[2],
        sums[8],
        sums[3],
        *sums[4:8],
    )


def solution(mesh):
    in_specs = (P("tower", "dp", None, None), P("tower", "dp", None), P(None, "dp", None)) + (P(),) * 15
    out_specs = (P(), P("tower", "dp", None, None)) + (P("dp", None),) * 6 + (P("dp"),) * 9
    return jax.shard_map(shards, mesh=mesh, in_specs=in_specs, out_specs=out_specs, check_vma=False)
```

```python
from functools import partial

import jax
import jax.numpy as jnp
from jax import lax
from jax.experimental import pallas as pl
from jax.experimental.pallas import tpu as pltpu
from jax.sharding import PartitionSpec as P

H = 12

inverse_temp = 100.0
norm_eps = 1e-06
pool_eps = 1e-06
masked_score = -1e30
f32 = jnp.float32
bf16 = jnp.bfloat16


def swap(value, axis, bits):
    count = lax.axis_size(axis)
    return lax.ppermute(value, axis, [(place, place ^ bits) for place in range(count)])


def swap_both(value, tower_bits, dp_bits):
    if not tower_bits:
        return swap(value, "dp", dp_bits)
    if not dp_bits:
        return swap(value, "tower", tower_bits)
    towers = lax.axis_size("tower")
    total = towers * lax.axis_size("dp")
    moves = [(place, place ^ (dp_bits * towers + tower_bits)) for place in range(total)]
    return lax.ppermute(value, ("dp", "tower"), moves)


def outer_bits():
    outer = lax.axis_size("dp") // 2
    return [1 << k for k in range(outer.bit_length() - 1)]


def gather_all(block, early, late):
    outer = lax.axis_size("dp") // 2
    if outer <= 4:
        got = [swap(block, "dp", 2 * k) for k in range(1, outer)]
        got, beside = lax.optimization_barrier((got, early()))
        blocks = jnp.stack([block] + got)
    else:
        beside = early()
        blocks = block[None]
        for bit in outer_bits():
            blocks = jnp.concatenate([blocks, swap(blocks, "dp", 2 * bit)])
    sides = [swap_both(blocks, 2 * x, y) if x or y else blocks for x in range(2) for y in range(2)]
    sides, beside = lax.optimization_barrier((sides, late(beside)))
    pairs = [sides[:2], sides[2:]]
    return [each for pair in pairs for each in pair + [swap(side, "tower", 1) for side in pair]], beside


def pick(value, index):
    return lax.dynamic_index_in_dim(value, index, 0, keepdims=False)


def add_up(parts):
    total = parts[0].astype(f32)
    for part in parts[1:]:
        total = total + part.astype(f32)
    return total


def sum_group(blocks):
    tower_index = lax.axis_index("tower")
    dp_index = lax.axis_index("dp")
    core, far = tower_index & 1, tower_index >> 1
    side, place = dp_index & 1, dp_index >> 1
    got = swap(pick(blocks, 1 - core), "tower", 1)
    blocks = add_up([pick(blocks, core), got]).astype(bf16)
    blocks = blocks.reshape((4,) + blocks.shape[2:])
    own = far * 2 + side
    parts = [pick(blocks, own)]
    for rel in range(1, 4):
        parts.append(swap_both(pick(blocks, own ^ rel), 2 * (rel >> 1), rel & 1))
    blocks = add_up(parts).astype(bf16)
    for bit in reversed(outer_bits()):
        halves = blocks.reshape((2, bit) + blocks.shape[1:])
        mine = jnp.where(place & bit, 1, 0)
        got = swap(pick(halves, 1 - mine), "dp", 2 * bit)
        blocks = add_up([pick(halves, mine), got]).astype(bf16)
    low = blocks[0]
    got = swap(low, "tower", 2)
    pair = jnp.where(far == 0, jnp.stack([low, got]), jnp.stack([got, low]))
    got = swap(pair, "tower", 1)
    every = jnp.where(core == 0, jnp.stack([pair, got]), jnp.stack([got, pair]))
    return every.astype(f32)


def dot(left, right):
    return jnp.dot(left, right, preferred_element_type=f32)


def dot_rows(left, right):
    return lax.dot_general(left, right, (((1,), (1,)), ((), ())), preferred_element_type=f32)


def dot_cols(left, right):
    return lax.dot_general(left, right, (((0,), (0,)), ((), ())), preferred_element_type=f32)


def split_low(value):
    high = value.astype(bf16)
    return high, (value - high.astype(f32)).astype(bf16)


def segment_of(lens_ref, row, places):
    total = jnp.int32(0)
    seg = jnp.zeros(places.shape, jnp.int32)
    for slot in range(lens_ref.shape[1]):
        total = total + lens_ref[row, slot]
        seg = seg + (places >= total).astype(jnp.int32)
    return seg


def fill_mask(lens_ref, mask_ref):
    rows, length, _ = mask_ref.shape
    for row in range(rows):
        across = segment_of(lens_ref, row, lax.broadcasted_iota(jnp.int32, (1, length), 1))
        down = segment_of(lens_ref, row, lax.broadcasted_iota(jnp.int32, (length, 1), 0))
        mask_ref[row] = jnp.where(down == across, 0.0, masked_score)


def line(ref):
    return ref[...].reshape(1, -1).astype(f32)


class Place:
    def __getitem__(self, which):
        tower, dp = lax.axis_index("tower"), lax.axis_index("dp")
        core, x = tower & 1, tower >> 1
        return (1 - x, core, x, dp & 1, dp >> 1, 1 - core, dp >> 2)[which]


class Copies:
    def __init__(self, sems):
        self.sems, self.made = sems, {}

    def start(self, name, source, target):
        self.made[name] = pltpu.make_async_copy(source, target, self.sems.at[len(self.made)])
        self.made[name].start()

    def wait(self, *names):
        for name in names:
            self.made[name].wait()


def hbm():
    return pl.BlockSpec(memory_space=pl.ANY)


def whole(shape):
    return pl.BlockSpec(shape, lambda *_: (0,) * len(shape))


def smem():
    return pl.BlockSpec(memory_space=pltpu.SMEM)


def shaped(shape, kind):
    return jax.ShapeDtypeStruct(shape, kind)


def params(limit):
    return pltpu.CompilerParams(vmem_limit_bytes=limit)


def cost(flops, moved):
    return pl.CostEstimate(flops=int(flops), bytes_accessed=int(moved), transcendentals=0)


def norm_stats(value):
    middle = jnp.mean(value, axis=-1, keepdims=True)
    centered = value - middle
    inverse = lax.rsqrt(jnp.mean(centered * centered, axis=-1, keepdims=True) + norm_eps)
    return centered * inverse, inverse


def norm_back(grad, scaled, inverse, gain):
    grad = grad * gain
    return inverse * (
        grad
        - jnp.mean(grad, axis=-1, keepdims=True)
        - scaled * jnp.mean(grad * scaled, axis=-1, keepdims=True)
    )


def forward_kernel(
    lens_ref, targets_ref, x_ref, wq, wk, wv, wo, bq, bv, bo, gain1, shift1,
    wu_hbm, bu, wd_hbm, bd, gain2, shift2,
    q_out, k_out, v_out, mixed_out, lse_out, low_hbm, xhat1_hbm, inv1_out,
    act_hbm, slope_hbm, xhat2_hbm, inv2_out, pool_out, unit_out,
    mask_ref, acc_ref, low_ref, xhat1_ref, sems, wu_ref, wd_ref, act_ref, slope_ref, xhat2_ref,
    weight_sems, out_sems, last_sems,
):
    step = pl.program_id(0)
    steps = pl.num_programs(0)
    groups = x_ref.shape[1] // q_out.shape[1]
    rows, slots = lens_ref.shape
    tokens, width = x_ref.shape
    length = tokens // rows
    copies = [
        pltpu.make_async_copy(low_ref, low_hbm, sems.at[0]),
        pltpu.make_async_copy(xhat1_ref, xhat1_hbm, sems.at[1]),
    ]

    chunk = wu_ref.shape[1] // 3

    def weight_copies(c):
        at = pl.ds(pl.multiple_of(c * chunk, chunk), chunk)
        return (
            pltpu.make_async_copy(wu_hbm.at[:, at], wu_ref.at[:, at], weight_sems.at[0, c]),
            pltpu.make_async_copy(wd_hbm.at[at, :], wd_ref.at[at, :], weight_sems.at[1, c]),
        )

    def out_copies(c, row):
        at = pl.ds(pl.multiple_of(c * chunk, chunk), chunk)
        rows_at = pl.ds(row * length, length)
        return (
            pltpu.make_async_copy(
                act_ref.at[rows_at, at], act_hbm.at[rows_at, at], out_sems.at[0, row, c]
            ),
            pltpu.make_async_copy(
                slope_ref.at[rows_at, at], slope_hbm.at[rows_at, at], out_sems.at[1, row, c]
            ),
        )

    def last_copy(row):
        rows_at = pl.ds(row * length, length)
        return pltpu.make_async_copy(
            xhat2_ref.at[rows_at, :], xhat2_hbm.at[rows_at, :], last_sems.at[row]
        )

    @pl.when(step == 0)
    def _():
        for c in range(3):
            for copy in weight_copies(c):
                copy.start()
        fill_mask(lens_ref, mask_ref)
        acc_ref[...] = x_ref[...].astype(f32) + line(bo)

    @pl.when(step < groups)
    def _():
        x = x_ref[...]
        q_out[...] = (dot(x, wq[...]) + line(bq)).astype(bf16)
        k_out[...] = dot(x, wk[...]).astype(bf16)
        v_out[...] = (dot(x, wv[...]) + line(bv)).astype(bf16)
        lane = lax.broadcasted_iota(jnp.int32, (1, 128), 1)
        first_half = lane < 64
        pairs = q_out.shape[1] // 128
        scale = bf16(64 ** (-0.5))
        for row in range(rows):
            for pair in range(pairs):
                at = slice(row * length, (row + 1) * length)
                lanes = slice(pair * 128, (pair + 1) * 128)
                q = q_out[at, lanes] * scale
                k = k_out[at, lanes]
                v = v_out[at, lanes]
                outs, logs = [], []
                for head in range(2):
                    mine = first_half == (head == 0)
                    scores = dot_rows(jnp.where(mine, q, bf16(0)), k) + mask_ref[row]
                    top = jnp.max(scores, axis=-1, keepdims=True)
                    shifted = jnp.exp(scores - top).astype(bf16)
                    out = dot(shifted, jnp.where(mine, v, bf16(1)))
                    total = pltpu.roll(out, 64, 1)
                    outs.append(out / total)
                    logs.append(top + jnp.log(jnp.where(mine, total, out)))
                mixed_out[at, lanes] = jnp.where(first_half, outs[0], outs[1]).astype(bf16)
                logs = jnp.transpose(jnp.where(first_half, logs[0], logs[1]))
                place = (step * pairs + pair) * 2
                lse_out[row, pl.ds(place, 1), :] = logs[0:1]
                lse_out[row, pl.ds(place + 1, 1), :] = logs[64:65]
        acc_ref[...] += dot(mixed_out[...], wo[...])

    @pl.when(step == groups - 1)
    def _():
        for row in range(rows):
            at = slice(row * length, (row + 1) * length)
            scaled, inverse = norm_stats(acc_ref[at, :])
            first = scaled * line(gain1) + line(shift1)
            acc_ref[at, :] = first + line(bd)
            low_ref[at, :] = first.astype(bf16)
            xhat1_ref[at, :] = scaled.astype(bf16)
            inv1_out[at, :] = inverse
        for copy in copies:
            copy.start()

    @pl.when(step >= groups)
    def _():
        c = step - groups
        part = min(chunk, 512)
        for copy in weight_copies(c):
            copy.wait()
        whole_at = pl.ds(pl.multiple_of(c * chunk, chunk), chunk)
        for row in range(rows):
            at = slice(row * length, (row + 1) * length)
            for low in range(0, chunk, part):
                lanes = pl.ds(pl.multiple_of(c * chunk + low, part), part)
                hidden = dot(low_ref[at, :], wu_ref[:, lanes]) + line(bu)[:, low : low + part]
                share = 0.5 + 0.5 * lax.erf(hidden * 0.7071067811865476)
                bell = jnp.exp(hidden * hidden * -0.5) * 0.3989422804014327
                act_ref[at, lanes] = (hidden * share).astype(bf16)
                slope_ref[at, lanes] = (share + hidden * bell).astype(bf16)
            for copy in out_copies(c, row):
                copy.start()
            acc_ref[at, :] += dot(act_ref[at, whole_at], wd_ref[whole_at, :])

    @pl.when(step == steps - 1)
    def _():
        for row in range(rows):
            at = slice(row * length, (row + 1) * length)
            own = slice(row * slots, (row + 1) * slots)
            scaled, inverse = norm_stats(acc_ref[at, :])
            xhat2_ref[at, :] = scaled.astype(bf16)
            last_copy(row).start()
            inv2_out[at, :] = inverse
            final = scaled * line(gain2) + line(shift2)
            high, low = split_low(final)
            seg = segment_of(lens_ref, row, lax.broadcasted_iota(jnp.int32, (slots, length), 1))
            member = (seg == lax.broadcasted_iota(jnp.int32, (slots, length), 0)).astype(f32)
            count = jnp.maximum(jnp.sum(member, axis=-1, keepdims=True), 1.0)
            member = member.astype(bf16)
            pooled = (dot(member, high) + dot(member, low)) / count
            pool_out[own, :] = pooled
            norm_sq = jnp.sum(pooled * pooled, axis=-1, keepdims=True)
            unit_out[own, :width] = (pooled * lax.rsqrt(norm_sq + pool_eps)).astype(bf16)
        spot = lax.broadcasted_iota(jnp.int32, (rows * slots, 128), 0)
        lane = lax.broadcasted_iota(jnp.int32, (rows * slots, 128), 1)
        marks = jnp.zeros((rows * slots, 128), jnp.int32)
        for row in range(rows):
            for slot in range(slots):
                live = (lens_ref[row, slot] > 0).astype(jnp.int32)
                target = targets_ref[Place()[1], row, slot]
                mark = jnp.where(lane == 0, live, jnp.where(lane == 1, target >> 6, target & 63))
                marks = jnp.where((spot == row * slots + slot) & (lane < 3), mark, marks)
        unit_out[:, width:] = marks.astype(f32).astype(bf16)
        for copy in copies:
            copy.wait()
        for row in range(rows):
            last_copy(row).wait()
            for c in range(3):
                for copy in out_copies(c, row):
                    copy.wait()


def forward(
    lens, targets, x, wq, wk, wv, wo, bq, bv, bo, gain1, shift1, wu, bu, wd, bd, gain2, shift2
):
    tokens, width = x.shape
    hidden = wu.shape[1]
    rows, slots = lens.shape
    length = tokens // rows
    group = 256
    groups = width // group
    chunk = hidden // 3
    near = lambda j: jnp.minimum(j, groups - 1)
    far = lambda j: jnp.maximum(j - groups, 0)
    cols = pl.BlockSpec((width, group), lambda j: (0, near(j)))
    bias = pl.BlockSpec((group,), lambda j: (near(j),))
    act = pl.BlockSpec((tokens, group), lambda j: (0, near(j)))
    vec = whole((width,))
    full = whole((tokens, width))
    one = whole((tokens, 1))
    return pl.pallas_call(
        forward_kernel,
        grid=(groups + hidden // chunk,),
        in_specs=[
            smem(), smem(), full, cols, cols, cols,
            pl.BlockSpec((group, width), lambda j: (near(j), 0)), bias, bias, vec, vec, vec,
            hbm(), pl.BlockSpec((chunk,), lambda j: (far(j),)), hbm(), vec, vec, vec,
        ],
        out_specs=[act] * 4 + [whole((rows, H, length)), hbm(), hbm(), one, hbm(), hbm(), hbm(), one]
        + [whole((rows * slots, width)), whole((rows * slots, width + 128))],
        out_shape=[shaped((tokens, width), bf16)] * 4
        + [
            shaped((rows, H, length), f32),
            shaped((tokens, width), bf16),
            shaped((tokens, width), bf16),
            shaped((tokens, 1), f32),
            shaped((tokens, hidden), bf16),
            shaped((tokens, hidden), bf16),
            shaped((tokens, width), bf16),
            shaped((tokens, 1), f32),
            shaped((rows * slots, width), f32),
            shaped((rows * slots, width + 128), bf16),
        ],
        scratch_shapes=[
            pltpu.VMEM((rows, length, length), f32),
            pltpu.VMEM((tokens, width), f32),
            pltpu.VMEM((tokens, width), bf16),
            pltpu.VMEM((tokens, width), bf16),
            pltpu.SemaphoreType.DMA((2,)),
            pltpu.VMEM((width, hidden), bf16),
            pltpu.VMEM((hidden, width), bf16),
            pltpu.VMEM((tokens, hidden), bf16),
            pltpu.VMEM((tokens, hidden), bf16),
            pltpu.VMEM((tokens, width), bf16),
            pltpu.SemaphoreType.DMA((2, 3)),
            pltpu.SemaphoreType.DMA((2, rows, 3)),
            pltpu.SemaphoreType.DMA((rows,)),
        ],
        compiler_params=params(60 << 20),
        cost_estimate=cost(8 * tokens * width * (width + hidden), 50 << 20),
        name="forward",
    )(lens, targets, x, wq, wk, wv, wo, bq, bv, bo, gain1, shift1, wu, bu, wd, bd, gain2, shift2)


def match_kernel(
    lens_ref, pool_ref, gain, inv_ref, *refs,
):
    row_refs, refs = refs[:8], refs[8:]
    (
    xhat_hbm, active_hbm, loss_out, grad_hbm, vec_out, send_hbm, keep_hbm, rows_ref, active_ref, xhat_ref, grad_out, both_ref, sems,
    ) = refs
    copies = Copies(sems)
    copies.start("xhat", xhat_hbm, xhat_ref)
    copies.start("active", active_hbm, active_ref)
    width = pool_ref.shape[1]
    slots = pool_ref.shape[0]
    rows, row_slots = lens_ref.shape
    length = xhat_ref.shape[0] // rows
    total = rows_ref.shape[1]
    outer = total // 4 // slots
    each = total // 4
    for i, block in enumerate(row_refs):
        rows_ref[i // 4, i % 4 * each : (i % 4 + 1) * each, :] = block[...].reshape(each, -1)
    spot = lax.broadcasted_iota(jnp.int32, (1, total), 1)
    group = spot // slots
    cores, sides, outers = group // (2 * outer), group // outer % 2, group % outer
    device = (Place()[4] ^ outers) * 2 + (Place()[3] ^ sides)
    numbers = ((Place()[1] ^ cores) * (2 * outer) + device) * slots + spot % slots
    passage_side = Place()[0]
    query_side = 1 - passage_side
    chunk = min(512, total)
    lane = lax.broadcasted_iota(jnp.int32, (8, 128), 1)
    passage_marks = rows_ref[passage_side, :, width:]
    passage_live = dot_rows((lane == 0).astype(bf16), passage_marks)[:1] > 0
    query_count = jnp.sum(rows_ref[query_side, :, width:][:, :1].astype(f32))
    per_query = 1.0 / query_count

    def part(i, carry):
        loss, as_query, as_passage = carry
        at = pl.ds(pl.multiple_of(i * chunk, chunk), chunk)
        marks = rows_ref[query_side, at, width:].astype(f32)
        live = marks[:, 0:1] > 0
        target = marks[:, 1:2].astype(jnp.int32) * 64 + marks[:, 2:3].astype(jnp.int32)
        queries = rows_ref[query_side, at, :width]
        passages = rows_ref[passage_side, :, :width]
        scores = dot_rows(queries, passages) * inverse_temp
        scores = jnp.where(passage_live, scores, masked_score)
        top = jnp.max(scores, axis=-1, keepdims=True)
        log_sum = top + jnp.log(jnp.sum(jnp.exp(scores - top), axis=-1, keepdims=True))
        is_target = numbers == target
        picked = jnp.sum(jnp.where(is_target, scores, 0.0), axis=-1, keepdims=True)
        loss = loss + jnp.sum(jnp.where(live, log_sum - picked, 0.0))
        chances = jnp.where(passage_live, jnp.exp(scores - log_sum), 0.0)
        grad = jnp.where(live, (chances - is_target.astype(f32)) * per_query, 0.0).astype(bf16)
        as_passage = as_passage + dot_cols(grad[:, :128], queries)[:slots]
        own = dot(grad[:slots], passages)
        as_query = jnp.where(i == 0, own, as_query)
        return loss, as_query, as_passage

    zeros = jnp.zeros((slots, width), f32)
    carry = (jnp.float32(0), zeros, zeros)
    if total == chunk:
        carry = part(0, carry)
    else:
        carry = lax.fori_loop(0, total // chunk, part, carry)
    loss, as_query, as_passage = carry
    loss_out[0, 0] = loss * per_query
    grad_unit = jnp.where(passage_side == 1, as_query, as_passage) * inverse_temp
    pooled = pool_ref[...]
    inverse = lax.rsqrt(jnp.sum(pooled * pooled, axis=-1, keepdims=True) + pool_eps)
    along = jnp.sum(grad_unit * pooled, axis=-1, keepdims=True)
    grad_pooled = inverse * grad_unit - pooled * (inverse * inverse * inverse) * along
    gain = line(gain)
    sums = []
    copies.wait("xhat")
    for row in range(rows):
        at = slice(row * length, (row + 1) * length)
        own = slice(row * row_slots, (row + 1) * row_slots)
        seg = segment_of(lens_ref, row, lax.broadcasted_iota(jnp.int32, (row_slots, length), 1))
        member = (seg == lax.broadcasted_iota(jnp.int32, (row_slots, length), 0)).astype(f32)
        count = jnp.maximum(jnp.sum(member, axis=-1, keepdims=True), 1.0)
        member = member.astype(bf16)
        high, low = split_low(grad_pooled[own] / count)
        grad_final = dot_cols(member, high) + dot_cols(member, low)
        scaled = xhat_ref[at, :].astype(f32)
        grad_sum = norm_back(grad_final, scaled, inv_ref[at, :], gain)
        grad_low = grad_sum.astype(bf16)
        grad_out[at, :] = grad_low
        sums.append(
            (
                jnp.sum(grad_final * scaled, axis=0, keepdims=True),
                jnp.sum(grad_final, axis=0, keepdims=True),
                jnp.sum(grad_low.astype(f32), axis=0, keepdims=True),
            )
        )
    for i in range(3):
        vec_out[i : i + 1, :] = sum(each[i] for each in sums)
    copies.start("grad", grad_out, grad_hbm)
    copies.wait("active")
    _, parts, sides, half, share = both_ref.shape
    turned = jnp.transpose(grad_out[...])
    for z in range(parts):
        at = slice(z * sides * share, (z + 1) * sides * share)
        both = dot(turned, active_ref[:, at]).astype(bf16)
        for core in range(2):
            for y in range(sides):
                lanes = slice(y * share, (y + 1) * share)
                both_ref[core, z, y] = both[core * half : (core + 1) * half, lanes]
        copies.start((z, 0), both_ref.at[Place()[5], z], send_hbm.at[z])
        copies.start((z, 1), both_ref.at[Place()[1], z], keep_hbm.at[z])
    copies.wait("grad", *[(z, i) for z in range(parts) for i in range(2)])


def match(lens, rows, pooled, xhat, inverse, gain, active):
    tokens, width = xhat.shape
    slots = pooled.shape[0]
    vmem = pl.BlockSpec(memory_space=pltpu.VMEM)
    return pl.pallas_call(
        match_kernel,
        in_specs=[smem()] + [vmem] * 11 + [hbm(), hbm()],
        out_specs=[smem(), hbm(), vmem, hbm(), hbm()],
        out_shape=[
            shaped((1, 1), f32),
            shaped((tokens, width), bf16),
            shaped((8, width), f32),
            shaped((4, 2, width // 2, active.shape[1] // 8), bf16),
            shaped((4, 2, width // 2, active.shape[1] // 8), bf16),
        ],
        scratch_shapes=[
            pltpu.VMEM((2, rows[0].size * 4 // (width + 128), width + 128), bf16),
            pltpu.VMEM(active.shape, bf16),
            pltpu.VMEM((tokens, width), bf16),
            pltpu.VMEM((tokens, width), bf16),
            pltpu.VMEM((2, 4, 2, width // 2, active.shape[1] // 8), bf16),
            pltpu.SemaphoreType.DMA((11,)),
        ],
        compiler_params=params(60 << 20),
        cost_estimate=cost(2e9, 10 << 20),
        name="match",
    )(lens, pooled, gain, inverse, *rows, xhat, active)


def hidden_kernel(
    grad_hbm, slope_hbm, wd_hbm, low_hbm, hidden_hbm, bias_out, send_hbm,
    grad_ref, slope_ref, wd_ref, low_ref, hidden_ref, send_ref, sems, send_sems,
):
    parts, width, chunk = 4, wd_ref.shape[1], wd_ref.shape[0] // 4

    def span(j):
        return pl.ds(pl.multiple_of(j * chunk, chunk), chunk)

    def wd_copy(j):
        return pltpu.make_async_copy(wd_hbm.at[span(j), :], wd_ref.at[span(j), :], sems.at[2 + j])

    def slope_copy(j):
        return pltpu.make_async_copy(slope_hbm.at[:, span(j)], slope_ref.at[:, span(j)], sems.at[6 + j])

    def hidden_copy(j):
        return pltpu.make_async_copy(hidden_ref.at[:, span(j)], hidden_hbm.at[:, span(j)], sems.at[10 + j])

    def send_copy(i):
        return pltpu.make_async_copy(send_ref.at[i], send_hbm.at[i], send_sems.at[i])

    grad_copy = pltpu.make_async_copy(grad_hbm, grad_ref, sems.at[0])
    low_copy = pltpu.make_async_copy(low_hbm, low_ref, sems.at[1])
    grad_copy.start()
    wd_copy(0).start()
    slope_copy(0).start()
    low_copy.start()
    for j in range(1, parts):
        wd_copy(j).start()
        slope_copy(j).start()
    grad_copy.wait()

    def step(j, carry):
        at = span(j)
        wd_copy(j).wait()
        slope_copy(j).wait()
        grad = dot_rows(grad_ref[...], wd_ref[at, :]) * slope_ref[:, at].astype(f32)
        grad_low = grad.astype(bf16)
        hidden_ref[:, at] = grad_low
        bias_out[:, at] = jnp.sum(grad_low.astype(f32), axis=0, keepdims=True)
        hidden_copy(j).start()

        @pl.when(j == 0)
        def _():
            low_copy.wait()

        @pl.when(j // 2 == Place()[5])
        def _():
            send_ref[j % 2] = dot_cols(low_ref[...], hidden_ref[:, at]).astype(bf16)
            send_copy(j % 2).start()

        return carry

    lax.fori_loop(0, parts, step, 0)
    for j in range(parts):
        hidden_copy(j).wait()
    for i in range(2):
        send_copy(i).wait()


def hidden_grad(grad, slope, wd, low):
    tokens, width = grad.shape
    hidden = wd.shape[0]
    chunk = hidden // 4
    return pl.pallas_call(
        hidden_kernel,
        in_specs=[hbm()] * 4,
        out_specs=[hbm(), pl.BlockSpec(memory_space=pltpu.VMEM), hbm()],
        out_shape=[
            shaped((tokens, hidden), bf16),
            shaped((1, hidden), f32),
            shaped((2, width, chunk), bf16),
        ],
        scratch_shapes=[
            pltpu.VMEM((tokens, width), bf16),
            pltpu.VMEM((tokens, hidden), bf16),
            pltpu.VMEM((hidden, width), bf16),
            pltpu.VMEM((tokens, width), bf16),
            pltpu.VMEM((tokens, hidden), bf16),
            pltpu.VMEM((2, width, chunk), bf16),
            pltpu.SemaphoreType.DMA((14,)),
            pltpu.SemaphoreType.DMA((2,)),
        ],
        compiler_params=params(60 << 20),
        cost_estimate=cost(3 * tokens * width * hidden, 22 << 20),
        name="hidden_grad",
    )(grad, slope, wd, low)


def feed_back_kernel(
    fast, inv_ref, gain, grad_hbm, hidden_hbm, wu_hbm, wo_hbm, xhat_hbm, low_hbm, mixed_hbm, got_hbm,
    vec_out, branch_hbm, back_hbm, send_hbm, keep_hbm, *refs,
):
    outs, refs = refs[: 4 * fast], refs[4 * fast :]
    grad_ref, hidden_ref, wu_ref, wo_ref, xhat_ref, low_ref, mixed_ref, got_ref, *refs = refs
    branch_ref, back_ref, send_ref, keep_ref, acc_ref, part_ref, sems, *pieces = refs
    tokens, width = grad_ref.shape
    half, narrow, chunk, parts = tokens // 2, width // 2, part_ref.shape[1], 4
    copies = Copies(sems)
    copies.start("grad", grad_hbm, grad_ref)
    for j in range(parts):
        at = slice(j * chunk, (j + 1) * chunk)
        copies.start(("hidden", j), hidden_hbm.at[:, at], hidden_ref.at[:, at])
        copies.start(("wu", j), wu_hbm.at[:, at], wu_ref.at[:, at])
        if j == 0:
            copies.start("low", low_hbm, low_ref)
            copies.start("got", got_hbm, got_ref)
    copies.start("xhat", xhat_hbm, xhat_ref)
    copies.start("wo", wo_hbm, wo_ref)
    copies.start("mixed", mixed_hbm, mixed_ref)
    copies.wait("grad")
    acc_ref[...] = grad_ref[...].astype(f32)
    for j in range(parts):
        at = slice(j * chunk, (j + 1) * chunk)
        copies.wait(("hidden", j), ("wu", j))
        for part in range(2):
            rows = slice(part * half, (part + 1) * half)
            acc_ref[rows, :] += dot_rows(hidden_ref[rows, at], wu_ref[:, at])
        if j == 0:
            copies.wait("low", "got")
        if not fast:
            continue
        size = pieces[0].shape[2]
        first = pieces[0].shape[3] - chunk

        @pl.when(j // 2 == Place()[1])
        def _():
            part_ref[...] = dot_cols(low_ref[...], hidden_ref[:, at]) + got_ref[j % 2].astype(f32)
            if j % 2 == 0:
                cut_rows(part_ref, pieces[:2], slice(0, chunk), False, size)
            else:
                lanes = slice(chunk, chunk + first)
                cut_rows(part_ref.at[:, :first], pieces[:2], lanes, False, size)
                lanes = slice(narrow, narrow + chunk - first)
                cut_rows(part_ref.at[:, first:], pieces[2:], lanes, True, size)

    for i in range(4 * fast):
        copies.start(("piece", i), pieces[i], outs[i])
    copies.wait("xhat", "wo", "mixed")
    tallies = []
    for part in range(2):
        rows = slice(part * half, (part + 1) * half)
        grad = acc_ref[rows, :]
        scaled = xhat_ref[rows, :].astype(f32)
        grad_low = norm_back(grad, scaled, inv_ref[rows, :], line(gain)).astype(bf16)
        branch_ref[rows, :] = grad_low
        copies.start(("branch", part), branch_ref.at[rows, :], branch_hbm.at[rows, :])
        back_ref[rows, :] = dot_rows(grad_low, wo_ref[...]).astype(bf16)
        copies.start(("back", part), back_ref.at[rows, :], back_hbm.at[rows, :])
        tallies.append(
            (
                jnp.sum(grad * scaled, axis=0, keepdims=True),
                jnp.sum(grad, axis=0, keepdims=True),
                jnp.sum(grad_low.astype(f32), axis=0, keepdims=True),
            )
        )
    for i in range(3):
        vec_out[i : i + 1, :] = tallies[0][i] + tallies[1][i]
    for i, out in ((1, send_ref), (0, keep_ref)):
        at = pl.ds(pl.multiple_of(Place()[1 + 4 * i] * narrow, narrow), narrow)
        out[...] = dot_cols(mixed_ref[...], branch_ref[:, at]).astype(bf16)
        copies.start(("out", i), out, (keep_hbm, send_hbm)[i])
    copies.wait(*[("piece", i) for i in range(4 * fast)])
    copies.wait(*[(name, i) for name in ("branch", "back", "out") for i in range(2)])


def feed_back(grad, grad_hidden, wu, wo, xhat, inverse, gain, low, mixed, got, fast):
    tokens, width = grad.shape
    hidden = wu.shape[1]
    chunk = hidden // 4
    narrow = width // 2
    first = chunk + width // 3
    pieces = [(2, 4, width // 16, first)] * 2 + [(2, 4, width // 16, 2 * chunk - first + narrow)] * 2
    pieces = [(each, bf16) for each in pieces] if fast else []
    full, strip = ((tokens, width), bf16), ((width, narrow), bf16)
    vmem = pl.BlockSpec(memory_space=pltpu.VMEM)
    scratch = [
        full, ((tokens, hidden), bf16), ((width, hidden), bf16), ((width, width), bf16), full, full, full,
        ((2, width, chunk), bf16), full, full, strip, strip, ((tokens, width), f32), ((width, chunk), f32),
    ]
    return pl.pallas_call(
        partial(feed_back_kernel, int(fast)),
        in_specs=[vmem, vmem] + [hbm()] * 8,
        out_specs=[vmem] + [hbm()] * (4 + len(pieces)),
        out_shape=[
            shaped((8, width), f32), shaped(*full), shaped(*full), shaped(*strip), shaped(*strip)
        ]
        + [shaped(*each) for each in pieces],
        scratch_shapes=[pltpu.VMEM(*each) for each in scratch]
        + [pltpu.SemaphoreType.DMA((24,))]
        + [pltpu.VMEM(*each) for each in pieces],
        compiler_params=params(60 << 20),
        cost_estimate=cost(4 * tokens * width * hidden, 30 << 20),
        name="feed_back",
    )(inverse, gain, grad, grad_hidden, wu, wo, xhat, low, mixed, got)


def join_kernel(keep_ref, got_ref, *refs):
    outs, acc_ref = refs[2:4], refs[4]
    acc_ref[...] = keep_ref[...].astype(f32) + got_ref[...].astype(f32)
    cut_rows(acc_ref, outs, slice(None), True, outs[0].shape[2])


def join_out(keep, got, pieces):
    width, narrow = keep.shape
    piece = pl.BlockSpec((2, 4, width // 16, narrow), lambda j: (0, 0, 0, 0))
    return pl.pallas_call(
        join_kernel,
        grid=(1,),
        in_specs=[whole(keep.shape), whole(got.shape)]
        + [pl.BlockSpec(memory_space=pl.ANY)] * 2,
        out_specs=[piece] * 2,
        out_shape=[shaped(each.shape, bf16) for each in pieces],
        input_output_aliases={2 + i: i for i in range(2)},
        scratch_shapes=[pltpu.VMEM((width, narrow), f32)],
        compiler_params=params(8 << 20),
        cost_estimate=cost(0, 3 << 20),
        name="join_out",
    )(keep, got, *pieces)


def probs_kernel(group, lens_ref, q_ref, k_ref, lse_ref, *refs):
    out, mask_ref = refs[-2:]
    step = pl.program_id(0)
    rows, length, _ = mask_ref.shape

    @pl.when(step == 0)
    def _():
        fill_mask(lens_ref, mask_ref)

    lane = lax.broadcasted_iota(jnp.int32, (1, 128), 1)
    pairs = q_ref.shape[1] // 128
    for pair in range(pairs):
        lanes = slice(pair * 128, (pair + 1) * 128)
        for row in range(rows):
            at = slice(row * length, (row + 1) * length)
            q = q_ref[at, lanes] * bf16(64 ** (-0.5))
            k = k_ref[at, lanes]
            for head in range(2):
                own = jnp.where((lane < 64) == (head == 0), q, bf16(0))
                place = ((step + group) * pairs + pair) * 2 + head
                log_total = lse_ref[row, pl.ds(place, 1), :]
                scores = dot_rows(k, own) + mask_ref[row]
                out[0, (row * pairs + pair) * 2 + head] = jnp.exp(scores - log_total).astype(bf16)


def probs_of(lens, q, k, lse, group, count, before=None):
    tokens, width = q.shape
    rows = lens.shape[0]
    length = tokens // rows
    lanes = 256
    heads = rows * lanes // 64
    act = pl.BlockSpec((tokens, lanes), lambda j: (0, j + group))
    return pl.pallas_call(
        partial(probs_kernel, group),
        grid=(count,),
        in_specs=[smem(), act, act, whole(lse.shape)] + ([] if before is None else [hbm()]),
        out_specs=pl.BlockSpec((1, heads, length, length), lambda j: (j + group, 0, 0, 0)),
        out_shape=shaped((width // lanes, heads, length, length), bf16),
        input_output_aliases={} if before is None else {4: 0},
        scratch_shapes=[pltpu.VMEM((rows, length, length), f32)],
        compiler_params=params(60 << 20),
        cost_estimate=cost(count * 4 * heads * length * length * 256, count << 22),
        name="probs",
    )(lens, q, k, lse, *(() if before is None else (before,)))


def attend_back_kernel(
    q_ref, k_ref, v_ref, probs_ref, mixed_ref, grad_ref, x_ref,
    first_sums, second_sums, up_sums, out, vec_out, send_out, keep_out, own_out, other_out, sums_ref, pack_ref,
):
    step = pl.program_id(0)
    length = probs_ref.shape[2]
    rows = q_ref.shape[0] // length

    lane = lax.broadcasted_iota(jnp.int32, (1, 128), 1)
    scale = 64 ** (-0.5)
    pairs = q_ref.shape[1] // 128
    for pair in range(pairs):
        lanes = slice(pair * 128, (pair + 1) * 128)
        query_sums, value_sums = [], []
        for row in range(rows):
            tokens = slice(row * length, (row + 1) * length)
            q = q_ref[tokens, lanes] * bf16(scale)
            k = k_ref[tokens, lanes]
            v = v_ref[tokens, lanes]
            grad = grad_ref[tokens, lanes]
            high, low = split_low(grad.astype(f32) * mixed_ref[tokens, lanes].astype(f32))
            grad_v = grad_k = grad_q = 0.0
            for head in range(2):
                mine = (lane < 64) == (head == 0)
                ones = jnp.broadcast_to(jnp.where(mine, 1.0, 0.0), (8, 128)).astype(bf16)
                inner = (dot_rows(ones, high) + dot_rows(ones, low))[:1]
                own_q = jnp.where(mine, q, bf16(0))
                own_grad = jnp.where(mine, grad, bf16(0))
                probs = probs_ref[0, (row * pairs + pair) * 2 + head]
                grad_scores = (probs.astype(f32) * (dot_rows(v, own_grad) - inner)).astype(bf16)
                grad_v = grad_v + dot(probs, own_grad)
                grad_k = grad_k + dot(grad_scores, own_q)
                grad_q = grad_q + dot_cols(jnp.where(mine, k, bf16(0)), grad_scores)
            grad_q = (jnp.transpose(grad_q) * scale).astype(bf16)
            grad_v = grad_v.astype(bf16)
            out[0, tokens, lanes] = grad_q
            out[1, tokens, lanes] = grad_k.astype(bf16)
            out[2, tokens, lanes] = grad_v
            query_sums.append(jnp.sum(grad_q.astype(f32), axis=0, keepdims=True))
            value_sums.append(jnp.sum(grad_v.astype(f32), axis=0, keepdims=True))
        vec_out[0:1, lanes] = sum(query_sums)
        vec_out[1:2, lanes] = sum(value_sums)
        at = pl.ds(pl.multiple_of((step * pairs + pair) * 128, 128), 128)
        sums_ref[0:1, at] = sum(query_sums)
        sums_ref[1:2, at] = sum(value_sums)
    for core, target in ((Place()[5], send_out), (Place()[1], keep_out)):
        lanes = pl.ds(pl.multiple_of(core * 128, 128), 128)
        grads = jnp.concatenate([out[i, :, lanes] for i in range(3)], axis=1)
        target[...] = dot_cols(x_ref[...], grads).astype(bf16)

    @pl.when(step == pl.num_programs(0) - 1)
    def _():
        sums = [sums_ref[i : i + 1, :] for i in range(2)]
        sums += [first_sums[2:3, :], second_sums[2:3, :], first_sums[0:1, :], first_sums[1:2, :]]
        sums += [second_sums[0:1, :], second_sums[1:2, :]]
        width = x_ref.shape[1]
        share = width // 8
        pack_ref[...] = jnp.zeros(pack_ref.shape, f32)
        for n in range(12):
            for d in range(8):
                if n < 8:
                    piece = sums[n][:, d * share : (d + 1) * share]
                else:
                    piece = up_sums[:, (d * 4 + n - 8) * share : (d * 4 + n - 7) * share]
                row = (d * 2 + n // 3 % 2) * (width // 16) + n % 3
                pack_ref[n // 6, row : row + 1, :share] = piece
        own_out[...] = pack_ref[Place()[1]].astype(bf16)
        other_out[...] = pack_ref[Place()[5]].astype(bf16)


def attend_back(q, k, v, probs, mixed, grad, x, first_sums, second_sums, up_sums):
    tokens, width = q.shape
    group = 256
    act = pl.BlockSpec((tokens, group), lambda j: (0, j))
    scores = pl.BlockSpec((1,) + probs.shape[1:], lambda j: (j, 0, 0, 0))
    return pl.pallas_call(
        attend_back_kernel,
        grid=(width // group,),
        in_specs=[act, act, act, scores, act, act, whole(x.shape)]
        + [whole(each.shape) for each in (first_sums, second_sums, up_sums)],
        out_specs=[
            pl.BlockSpec((3, tokens, group), lambda j: (0, 0, j)),
            pl.BlockSpec((8, group), lambda j: (0, j)),
            pl.BlockSpec((width, 384), lambda j: (0, j)),
            pl.BlockSpec((width, 384), lambda j: (0, j)),
            whole((width, 128)),
            whole((width, 128)),
        ],
        out_shape=[
            shaped((3, tokens, width), bf16),
            shaped((8, width), f32),
            shaped((width, width // group * 384), bf16),
            shaped((width, width // group * 384), bf16),
            shaped((width, 128), bf16),
            shaped((width, 128), bf16),
        ],
        scratch_shapes=[
            pltpu.VMEM((8, width), f32),
            pltpu.VMEM((2, width, 128), f32),
        ],
        compiler_params=params(60 << 20),
        cost_estimate=cost(20 * tokens * probs.shape[2] * width, 30 << 20),
        name="attend_back",
    )(q, k, v, probs, mixed, grad, x, first_sums, second_sums, up_sums)


def input_kernel(branch_hbm, grads_hbm, wq_hbm, wk_hbm, wv_hbm, out_hbm, branch_ref, grads_ref, weights_ref, out_ref, sems):
    copies = Copies(sems)
    for m, weight in enumerate((wq_hbm, wk_hbm, wv_hbm)):
        copies.start(("w", m), weight, weights_ref.at[m])
        copies.start(("g", m), grads_hbm.at[m], grads_ref.at[m])
        if m == 0:
            copies.start("branch", branch_hbm, branch_ref)
    tokens = out_ref.shape[0]
    parts = 4
    for m in range(3):
        copies.wait(("w", m), ("g", m))
        if m == 0:
            copies.wait("branch")
        for part in range(parts):
            rows = slice(part * tokens // parts, (part + 1) * tokens // parts)
            before = branch_ref[rows, :].astype(f32) if m == 0 else out_ref[rows, :]
            out_ref[rows, :] = before + dot_rows(grads_ref[m, rows, :], weights_ref[m])
            if m == 2:
                copies.start(("out", part), out_ref.at[rows, :], out_hbm.at[rows, :])
    copies.wait(*[("out", part) for part in range(parts)])


def input_grad(branch, grads, wq, wk, wv):
    tokens, width = branch.shape
    return pl.pallas_call(
        input_kernel,
        in_specs=[hbm()] * 5,
        out_specs=hbm(),
        out_shape=shaped((tokens, width), f32),
        scratch_shapes=[
            pltpu.VMEM((tokens, width), bf16),
            pltpu.VMEM((3, tokens, width), bf16),
            pltpu.VMEM((3, width, width), bf16),
            pltpu.VMEM((tokens, width), f32),
            pltpu.SemaphoreType.DMA((11,)),
        ],
        compiler_params=params(60 << 20),
        cost_estimate=cost(6 * tokens * width * width, 13 << 20),
        name="input_grad",
    )(branch, grads, wq, wk, wv)


def down_kernel(keep_hbm, got_hbm, *refs):
    outs, refs = refs[:4], refs[4:]
    keep_ref, got_ref, acc_ref, sems, *pieces = refs
    parts, _, half, _ = got_ref.shape
    copies = Copies(sems)
    for z in range(parts):
        copies.start(("keep", z), keep_hbm.at[z], keep_ref.at[z])
        copies.start(("got", z), got_hbm.at[z], got_ref.at[z])
    strip = half // 4
    for z in range(parts):
        copies.wait(("keep", z), ("got", z))
        for y in range(2):
            acc_ref[...] = keep_ref[z, y].astype(f32) + got_ref[z, y].astype(f32)
            for rel in range(2):
                at = pl.multiple_of((Place()[2] ^ rel) * 2 * strip, 2 * strip)
                pieces[rel][y, z] = acc_ref[pl.ds(at, strip), :].astype(bf16)

                @pl.when(Place()[3] == y ^ rel)
                def _():
                    for x in range(2):
                        rows = slice((2 * x + 1) * strip, (2 * x + 2) * strip)
                        pieces[2 + rel][x, z] = acc_ref[rows, :].astype(bf16)

        for i in range(4):
            copies.start(("piece", i, z), pieces[i].at[:, z], outs[i].at[:, z])
    copies.wait(*[("piece", i, z) for i in range(4) for z in range(parts)])


def down_grad(keep, got):
    parts, _, half, share = got.shape
    piece = (2, parts, half // 4, share)
    return pl.pallas_call(
        down_kernel,
        in_specs=[hbm()] * 2,
        out_specs=[hbm()] * 4,
        out_shape=[shaped(piece, bf16)] * 4,
        scratch_shapes=[
            pltpu.VMEM(got.shape, bf16),
            pltpu.VMEM(got.shape, bf16),
            pltpu.VMEM((half, share), f32),
            pltpu.SemaphoreType.DMA((24,)),
        ]
        + [pltpu.VMEM(piece, bf16)] * 4,
        compiler_params=params(60 << 20),
        cost_estimate=cost(0, 7 << 20),
        name="down_keep",
    )(keep, got)


def cut_rows(acc_ref, outs, at, by_y, size):
    outer = acc_ref.shape[0] // 4 // size
    for rel, out in enumerate(outs):
        for z in range(outer):
            for i in range(2):
                y, x = (Place()[3] ^ rel, i) if by_y else (i, Place()[2] ^ rel)
                row = pl.multiple_of(((z * 2 + y) * 2 + x) * size, size)
                out[i, z, :, at] = acc_ref[pl.ds(row, size), :].astype(bf16)


def head_kernel(vec_ref, got_vec_ref, keep_hbm, got_hbm, *refs):
    outs, (keep_ref, got_ref, acc_ref, sems) = refs[:4], refs[4:]
    width, total = keep_ref.shape
    half, size = outs[0].shape[3], outs[0].shape[2]
    parts = width // 4 // size
    span = width // parts
    copies = Copies(sems)
    for z in range(parts):
        rows = slice(z * span, (z + 1) * span)
        copies.start(("keep", z), keep_hbm.at[rows, :], keep_ref.at[rows, :])
        copies.start(("got", z), got_hbm.at[rows, :], got_ref.at[rows, :])
    for z in range(parts):
        rows = slice(z * span, (z + 1) * span)
        acc_ref[:, total:] = vec_ref[rows, :].astype(f32) + got_vec_ref[rows, :].astype(f32)
        copies.wait(("keep", z), ("got", z))
        acc_ref[:, :total] = keep_ref[rows, :].astype(f32) + got_ref[rows, :].astype(f32)
        for rel in range(2):
            for i in range(2):
                at = pl.multiple_of((i * 2 + (Place()[2] ^ rel)) * size, size)
                outs[rel][i, z] = acc_ref[pl.ds(at, size), :half].astype(bf16)
                at = pl.multiple_of(((Place()[3] ^ rel) * 2 + i) * size, size)
                outs[2 + rel][i, z] = acc_ref[pl.ds(at, size), half:].astype(bf16)


def head_grad(keep, vectors, got_vectors, got):
    width, total = keep.shape
    piece_shape = (2, 4, width // 16, (total + 128) // 2)
    vmem = pl.BlockSpec(memory_space=pltpu.VMEM)
    return pl.pallas_call(
        head_kernel,
        in_specs=[vmem, vmem] + [hbm()] * 2,
        out_specs=[vmem] * 4,
        out_shape=[shaped(piece_shape, bf16)] * 4,
        scratch_shapes=[
            pltpu.VMEM(keep.shape, bf16),
            pltpu.VMEM(keep.shape, bf16),
            pltpu.VMEM((width // 4, total + 128), f32),
            pltpu.SemaphoreType.DMA((8,)),
        ],
        compiler_params=params(12 << 20),
        cost_estimate=cost(0, 6 << 20),
        name="head_keep",
    )(vectors, got_vectors, keep, got)


def mix_kernel(which, parts, *refs):
    ins, outs = refs[:-parts], refs[-parts:]
    for rel, out in enumerate(outs):
        at = Place()[which] ^ rel if parts > 1 else 0
        total = ins[0][at].astype(f32)
        for ref in ins[1:]:
            total = total + ref[at].astype(f32)
        out[...] = total.astype(bf16)


def mix(which, arrays):
    parts = arrays[0].shape[0]
    return pl.pallas_call(
        partial(mix_kernel, which, parts),
        in_specs=[pl.BlockSpec(memory_space=pltpu.VMEM)] * len(arrays),
        out_specs=[pl.BlockSpec(memory_space=pltpu.VMEM)] * parts,
        out_shape=[shaped(arrays[0].shape[1:], bf16)] * parts,
        compiler_params=params(8 << 20),
        cost_estimate=cost(0, 2 * arrays[0].size * (len(arrays) + 1)),
        name="mix",
    )(*arrays)


def first_exchange(parts):
    return [parts[0], swap(parts[1], "tower", 2), parts[2], swap(parts[3], "dp", 1)]


def second_exchange(parts):
    return [parts[0], swap(parts[1], "dp", 1), parts[2], swap(parts[3], "tower", 2)]


def cross_kernel(*refs):
    ins, outs = refs[:4], refs[4:]
    for i in range(2):
        mine, got = ins[2 * i : 2 * i + 2]
        for rel in range(2):
            at = Place()[3 - i] ^ rel
            outs[2 * i + rel][...] = (mine[at].astype(f32) + got[at].astype(f32)).astype(bf16)


def cross(parts):
    vmem = pl.BlockSpec(memory_space=pltpu.VMEM)
    return pl.pallas_call(
        cross_kernel,
        in_specs=[vmem] * 4,
        out_specs=[vmem] * 4,
        out_shape=[shaped(each.shape[1:], bf16) for each in parts],
        compiler_params=params(8 << 20),
        cost_estimate=cost(0, 6 << 20),
        name="cross",
    )(*parts)


def outer_kernel(axis, *refs):
    ins, outs = refs[:4], refs[4:]
    for rel, out in enumerate(outs):
        at = Place()[4] ^ rel
        sums = [ins[2 * i][at].astype(f32) + ins[2 * i + 1][at].astype(f32) for i in range(2)]
        out[...] = jnp.concatenate(sums, axis=axis).astype(bf16)


def cut_halves(axis, parts):
    vmem = pl.BlockSpec(memory_space=pltpu.VMEM)
    outer = parts[0].shape[0]
    shape = list(parts[0].shape[1:])
    shape[axis] += parts[2].shape[1 + axis]
    return pl.pallas_call(
        partial(outer_kernel, axis),
        in_specs=[vmem] * 4,
        out_specs=[vmem] * outer,
        out_shape=[shaped(tuple(shape), bf16)] * outer,
        compiler_params=params(8 << 20),
        cost_estimate=cost(0, 3 << 20),
        name="cut_halves",
    )(*parts)


def near_kernel(axis, *refs):
    ins, outs = refs[:4], refs[4:]
    for rel, out in enumerate(outs):
        for upper in range(out.shape[0]):
            at = upper * 2 + ((Place()[4] & 1) ^ rel)
            sums = [ins[2 * i][at].astype(f32) + ins[2 * i + 1][at].astype(f32) for i in range(2)]
            out[upper] = jnp.concatenate(sums, axis=axis).astype(bf16)


def cut_near(axis, parts):
    vmem = pl.BlockSpec(memory_space=pltpu.VMEM)
    shape = list(parts[0].shape[1:])
    shape[axis] += parts[2].shape[1 + axis]
    return pl.pallas_call(
        partial(near_kernel, axis),
        in_specs=[vmem] * 4,
        out_specs=[vmem] * 2,
        out_shape=[shaped((parts[0].shape[0] // 2, *shape), bf16)] * 2,
        compiler_params=params(8 << 20),
        cost_estimate=cost(0, 3 << 20),
        name="cut_near",
    )(*parts)


def near_exchange(parts):
    return [parts[0], swap(parts[1], "dp", 2)]


def far_exchange(parts):
    return [parts[0], swap(parts[1], "dp", 4)]


def exchange_outer(parts):
    return [parts[0]] + [swap(part, "dp", 2 * rel) for rel, part in enumerate(parts) if rel]


def join_outer(parts):
    return mix(4, [part[None] for part in parts])[0]


def spread_kernel(kind, *refs):
    blocks, outs = refs[:4], refs[4:]
    core, far = Place()[1], Place()[2]
    share = outs[0].shape[0]
    for i, block in enumerate(blocks):
        c, x = core ^ (i >> 1), far ^ (i & 1)
        value = block[...].astype(f32)
        size = value.shape[0]
        rows = pl.ds(pl.multiple_of(x * size, size), size)
        if kind == "down":
            at = pl.multiple_of((c * 2 + x) * size, size)
            refs[-1][pl.ds(at, size), :] = value
            continue
        half = outs[1].shape[1] // 2
        if kind == "up":
            total = outs[0].shape[1] // 2
            wide = pl.ds(pl.multiple_of(c * total, total), total)
            narrow = pl.ds(pl.multiple_of(c * half, half), half)
            first = total // 3 * 2
            outs[0][rows, wide] = jnp.concatenate([value[:, :first], value[:, first + half :]], axis=1)
            outs[1][rows, narrow] = value[:, first : first + half]
        else:
            groups = half // 128
            for j in range(groups):
                lanes = pl.ds(pl.multiple_of(j * 256 + c * 128, 128), 128)
                for m in range(3):
                    outs[m][rows, lanes] = value[:, (j * 3 + m) * 128 : (j * 3 + m + 1) * 128]
            refs[-1][c * 2 + x] = value[:16, 3 * half :]
    if kind == "down":
        outs[0][...] = jnp.transpose(refs[-1][...])
    if kind == "head":
        for n in range(8):
            outs[3 + n][...] = refs[-1][n // 3, n % 3 : n % 3 + 1, :share].reshape(-1)
        last = [refs[-1][n // 3, n % 3 : n % 3 + 1, :share] for n in range(8, 12)]
        outs[11][...] = jnp.concatenate(last, axis=1).reshape(-1)


def spread(kind, block, far, shapes):
    blocks = [block, far, swap(block, "tower", 1), swap(far, "tower", 1)]
    return pl.pallas_call(
        partial(spread_kernel, kind),
        in_specs=[pl.BlockSpec(memory_space=pltpu.VMEM)] * 4,
        out_specs=[pl.BlockSpec(memory_space=pltpu.VMEM)] * len(shapes),
        out_shape=[shaped(shape, f32) for shape in shapes],
        scratch_shapes=[pltpu.VMEM((4, 16, 128) if kind == "head" else shapes[0][::-1], f32)],
        compiler_params=params(8 << 20),
        cost_estimate=cost(0, 2 << 20),
        name="spread_" + kind,
    )(*blocks)


def shards(
    layer_input,
    seg_lengths,
    positives,
    query_weight,
    key_weight,
    value_weight,
    out_weight,
    up_weight,
    down_weight,
    query_bias,
    value_offset_bias,
    out_bias,
    up_bias,
    down_bias,
    first_gain,
    first_shift,
    second_gain,
    latter_norm_translation,
):
    row_count = layer_input.shape[1]
    row_len = layer_input.shape[2]
    width = layer_input.shape[3]
    slot_count = seg_lengths.shape[2]
    token_count = row_count * row_len
    dp_count = lax.axis_size("dp")
    flat_in = layer_input.reshape(token_count, width)
    lens = seg_lengths.reshape(row_count, slot_count)

    (
        q, k, v, mixed, lse, low, first_scaled, first_inverse,
        active, slope, second_scaled, second_inverse, pooled, unit,
    ) = forward(
        lens, positives, flat_in, query_weight, key_weight, value_weight, out_weight,
        query_bias, value_offset_bias, out_bias, first_gain, first_shift,
        up_weight, up_bias, down_weight, down_bias, second_gain, latter_norm_translation,
    )
    rows, probs = gather_all(
        unit,
        lambda: probs_of(lens, q, k, lse, 0, 1),
        lambda before: probs_of(lens, q, k, lse, 1, width // 256 - 1, before),
    )
    loss, grad_second, second_sums, down_half, down_keep = match(
        lens, rows, pooled, second_scaled, second_inverse, second_gain, active
    )
    loss = loss.reshape(())
    share = width // dp_count
    fast = dp_count == 8 and lax.axis_size("tower") == 4
    grad_hidden, up_sums, up_half = hidden_grad(grad_second, slope, down_weight, low)
    if fast:
        got = swap(down_half, "tower", 1)
        got, grad_hidden, up_half = lax.optimization_barrier((got, grad_hidden, up_half))
        down_parts = down_grad(down_keep, got)
        up_half = swap(up_half, "tower", 1)
        down_parts, grad_hidden, up_half = lax.optimization_barrier(
            (down_parts, grad_hidden, up_half)
        )
        down_parts = first_exchange(down_parts)
    first_sums, grad_branch, grad_mixed, out_half, out_keep, *up_parts = feed_back(
        grad_second, grad_hidden, up_weight, out_weight, first_scaled, first_inverse,
        first_gain, low, mixed, up_half, fast,
    )
    if fast:
        down_parts, out_half = lax.optimization_barrier((down_parts, out_half))
        out_half = swap(out_half, "tower", 1)
        down_parts = cross(down_parts)
        down_parts, out_half = lax.optimization_barrier((down_parts, out_half))
        up_parts[2:] = join_out(out_keep, out_half, up_parts[2:])
        up_parts, down_parts, grad_mixed = lax.optimization_barrier((up_parts, down_parts, grad_mixed))
        up_parts = first_exchange(up_parts)
        down_parts = second_exchange(down_parts)
    grads, head_sums, head_half, head_keep, vectors, other_vectors = attend_back(
        q, k, v, probs, mixed, grad_mixed, flat_in, first_sums, second_sums, up_sums
    )
    if fast:
        up_parts, down_parts, grads, head_half, other_vectors = lax.optimization_barrier(
            (up_parts, down_parts, grads, head_half, other_vectors)
        )
    if fast:
        got = swap(head_half, "tower", 1)
        got_vectors = swap(other_vectors, "tower", 1)
        down_parts = cut_near(0, down_parts)
        up_parts = cross(up_parts)
        up_parts, down_parts, got = lax.optimization_barrier((up_parts, down_parts, got))
        up_parts = second_exchange(up_parts)
        down_parts = near_exchange(down_parts)
        parts = head_grad(head_keep, vectors, got_vectors, got)
        up_parts, down_parts, parts, grads = lax.optimization_barrier(
            (up_parts, down_parts, parts, grads)
        )
        parts = first_exchange(parts)
        down_parts = far_exchange(mix(6, down_parts))
        up_parts = near_exchange(cut_near(1, up_parts))
        grad_input = input_grad(grad_branch, grads, query_weight, key_weight, value_weight)
        down_parts, up_parts, parts, grad_input = lax.optimization_barrier(
            (down_parts, up_parts, parts, grad_input)
        )
        parts = cross(parts)
        up_parts = mix(6, up_parts)
        down_part = join_outer(down_parts)
        down_part, up_parts, parts = lax.optimization_barrier((down_part, up_parts, parts))
        up_parts = far_exchange(up_parts)
        parts = second_exchange(parts)
        up_parts, parts = lax.optimization_barrier((up_parts, parts))
        parts = cut_halves(1, parts)
        up_parts, parts = lax.optimization_barrier((up_parts, parts))
        parts = exchange_outer(parts)
        up_part = join_outer(up_parts)
        down_far, up_far = swap(down_part, "tower", 2), swap(up_part, "tower", 2)
        up_far, down_far, parts = lax.optimization_barrier((up_far, down_far, parts))
        head_part = join_outer(parts)
        head_far = swap(head_part, "tower", 2)
        (total_down,) = spread("down", down_part, down_far, [(4 * share, width)])
        total_up, total_out = spread(
            "up", up_part, up_far, [(share, up_weight.shape[1]), (share, width)]
        )
        total_down, total_up, total_out, head_far = lax.optimization_barrier(
            (total_down, total_up, total_out, head_far)
        )
        total_query, total_key, total_value, *sums = spread(
            "head", head_part, head_far,
            [(share, width)] * 3 + [(share,)] * 8 + [(4 * share,)],
        )
    else:
        grad_input = input_grad(grad_branch, grads, query_weight, key_weight, value_weight)
        outer = dp_count // 2
        vectors = jnp.concatenate(
            [
                vec.reshape(dp_count, -1)
                for vec in (
                    head_sums[0],
                    head_sums[1],
                    first_sums[2],
                    second_sums[2],
                    first_sums[0],
                    first_sums[1],
                    second_sums[0],
                    second_sums[1],
                    up_sums,
                )
            ],
            axis=1,
        ).astype(bf16)

        def by_rows(grad):
            return grad.astype(bf16).reshape(outer, 2, share, 2, 2, width).transpose(3, 4, 1, 0, 2, 5)

        square = jnp.stack(
            [dot_cols(flat_in, grads[i]) for i in range(3)] + [dot_cols(mixed, grad_branch)], axis=1
        )
        vectors = vectors.reshape(outer, 2, 2, 2, -1).transpose(2, 3, 1, 0, 4)
        vectors = jnp.pad(vectors, ((0, 0),) * 4 + ((0, width - vectors.shape[-1]),))
        down = dot_cols(active, grad_second).astype(bf16)
        down = down.reshape(outer, 2, 2, 2, share, width).transpose(2, 3, 1, 0, 4, 5)
        total_down = sum_group(down).reshape(4 * share, width)
        total_up = sum_group(by_rows(dot_cols(low, grad_hidden))).reshape(4, share, width)
        total_up = total_up.transpose(1, 0, 2).reshape(share, 4 * width)
        last = jnp.concatenate([by_rows(square), vectors[:, :, :, :, None]], axis=4)
        last = sum_group(last).reshape(4, share + 1, width)
        total_query, total_key, total_value, total_out = [last[i, :share] for i in range(4)]
        short = last[:, share, : share * 3].reshape(-1)
        sums = [short[i * share : (i + 1) * share] for i in range(8)] + [short[8 * share :]]
    grad_input = grad_input.reshape(layer_input.shape)
    return (
        loss,
        grad_input,
        total_query,
        total_key,
        total_value,
        total_out,
        total_up,
        total_down,
        sums[0],
        sums[1],
        sums[2],
        sums[8],
        sums[3],
        *sums[4:8],
    )


def solution(mesh):
    in_specs = (P("tower", "dp", None, None), P("tower", "dp", None), P(None, "dp", None)) + (P(),) * 15
    out_specs = (P(), P("tower", "dp", None, None)) + (P("dp", None),) * 6 + (P("dp"),) * 9
    return jax.shard_map(shards, mesh=mesh, in_specs=in_specs, out_specs=out_specs, check_vma=False)
```

```python
from functools import partial

import jax
import jax.numpy as jnp
from jax import lax
from jax.experimental import pallas as pl
from jax.experimental.pallas import tpu as pltpu
from jax.sharding import PartitionSpec as P

H = 12

inverse_temp = 100.0
norm_eps = 1e-06
pool_eps = 1e-06
masked_score = -1e30
f32 = jnp.float32
bf16 = jnp.bfloat16


def swap(value, axis, bits):
    count = lax.axis_size(axis)
    return lax.ppermute(value, axis, [(place, place ^ bits) for place in range(count)])


def swap_both(value, tower_bits, dp_bits):
    if not tower_bits:
        return swap(value, "dp", dp_bits)
    if not dp_bits:
        return swap(value, "tower", tower_bits)
    towers = lax.axis_size("tower")
    total = towers * lax.axis_size("dp")
    moves = [(place, place ^ (dp_bits * towers + tower_bits)) for place in range(total)]
    return lax.ppermute(value, ("dp", "tower"), moves)


def outer_bits():
    outer = lax.axis_size("dp") // 2
    return [1 << k for k in range(outer.bit_length() - 1)]


def gather_all(block, early, late):
    outer = lax.axis_size("dp") // 2
    if outer <= 4:
        got = [swap(block, "dp", 2 * k) for k in range(1, outer)]
        got, beside = lax.optimization_barrier((got, early()))
        blocks = jnp.stack([block] + got)
    else:
        beside = early()
        blocks = block[None]
        for bit in outer_bits():
            blocks = jnp.concatenate([blocks, swap(blocks, "dp", 2 * bit)])
    sides = [swap_both(blocks, 2 * x, y) if x or y else blocks for x in range(2) for y in range(2)]
    sides, beside = lax.optimization_barrier((sides, late(beside)))
    pairs = [sides[:2], sides[2:]]
    return [each for pair in pairs for each in pair + [swap(side, "tower", 1) for side in pair]], beside


def pick(value, index):
    return lax.dynamic_index_in_dim(value, index, 0, keepdims=False)


def add_up(parts):
    total = parts[0].astype(f32)
    for part in parts[1:]:
        total = total + part.astype(f32)
    return total


def sum_group(blocks):
    tower_index = lax.axis_index("tower")
    dp_index = lax.axis_index("dp")
    core, far = tower_index & 1, tower_index >> 1
    side, place = dp_index & 1, dp_index >> 1
    got = swap(pick(blocks, 1 - core), "tower", 1)
    blocks = add_up([pick(blocks, core), got]).astype(bf16)
    blocks = blocks.reshape((4,) + blocks.shape[2:])
    own = far * 2 + side
    parts = [pick(blocks, own)]
    for rel in range(1, 4):
        parts.append(swap_both(pick(blocks, own ^ rel), 2 * (rel >> 1), rel & 1))
    blocks = add_up(parts).astype(bf16)
    for bit in reversed(outer_bits()):
        halves = blocks.reshape((2, bit) + blocks.shape[1:])
        mine = jnp.where(place & bit, 1, 0)
        got = swap(pick(halves, 1 - mine), "dp", 2 * bit)
        blocks = add_up([pick(halves, mine), got]).astype(bf16)
    low = blocks[0]
    got = swap(low, "tower", 2)
    pair = jnp.where(far == 0, jnp.stack([low, got]), jnp.stack([got, low]))
    got = swap(pair, "tower", 1)
    every = jnp.where(core == 0, jnp.stack([pair, got]), jnp.stack([got, pair]))
    return every.astype(f32)


def dot(left, right):
    return jnp.dot(left, right, preferred_element_type=f32)


def dot_rows(left, right):
    return lax.dot_general(left, right, (((1,), (1,)), ((), ())), preferred_element_type=f32)


def dot_cols(left, right):
    return lax.dot_general(left, right, (((0,), (0,)), ((), ())), preferred_element_type=f32)


def split_low(value):
    high = value.astype(bf16)
    return high, (value - high.astype(f32)).astype(bf16)


def segment_of(lens_ref, row, places):
    total = jnp.int32(0)
    seg = jnp.zeros(places.shape, jnp.int32)
    for slot in range(lens_ref.shape[1]):
        total = total + lens_ref[row, slot]
        seg = seg + (places >= total).astype(jnp.int32)
    return seg


def fill_mask(lens_ref, mask_ref):
    rows, length, _ = mask_ref.shape
    for row in range(rows):
        across = segment_of(lens_ref, row, lax.broadcasted_iota(jnp.int32, (1, length), 1))
        down = segment_of(lens_ref, row, lax.broadcasted_iota(jnp.int32, (length, 1), 0))
        mask_ref[row] = jnp.where(down == across, 0.0, masked_score)


def line(ref):
    return ref[...].reshape(1, -1).astype(f32)


class Place:
    def __getitem__(self, which):
        tower, dp = lax.axis_index("tower"), lax.axis_index("dp")
        core, x = tower & 1, tower >> 1
        return (1 - x, core, x, dp & 1, dp >> 1, 1 - core, dp >> 2)[which]


class Copies:
    def __init__(self, sems):
        self.sems, self.made = sems, {}

    def start(self, name, source, target):
        self.made[name] = pltpu.make_async_copy(source, target, self.sems.at[len(self.made)])
        self.made[name].start()

    def wait(self, *names):
        for name in names:
            self.made[name].wait()


def hbm():
    return pl.BlockSpec(memory_space=pl.ANY)


def whole(shape):
    return pl.BlockSpec(shape, lambda *_: (0,) * len(shape))


def smem():
    return pl.BlockSpec(memory_space=pltpu.SMEM)


def shaped(shape, kind):
    return jax.ShapeDtypeStruct(shape, kind)


def params(limit):
    return pltpu.CompilerParams(vmem_limit_bytes=limit)


def cost(flops, moved):
    return pl.CostEstimate(flops=int(flops), bytes_accessed=int(moved), transcendentals=0)


def norm_stats(value):
    middle = jnp.mean(value, axis=-1, keepdims=True)
    centered = value - middle
    inverse = lax.rsqrt(jnp.mean(centered * centered, axis=-1, keepdims=True) + norm_eps)
    return centered * inverse, inverse


def norm_back(grad, scaled, inverse, gain):
    grad = grad * gain
    return inverse * (
        grad
        - jnp.mean(grad, axis=-1, keepdims=True)
        - scaled * jnp.mean(grad * scaled, axis=-1, keepdims=True)
    )


def forward_kernel(
    lens_ref, targets_ref, x_ref, wq, wk, wv, wo, bq, bv, bo, gain1, shift1,
    wu_hbm, bu, wd_hbm, bd, gain2, shift2,
    q_out, k_out, v_out, mixed_out, lse_out, low_hbm, xhat1_hbm, inv1_out,
    act_hbm, slope_hbm, xhat2_hbm, inv2_out, pool_out, unit_out,
    mask_ref, acc_ref, low_ref, xhat1_ref, sems, wu_ref, wd_ref, act_ref, slope_ref, xhat2_ref,
    weight_sems, out_sems, last_sems,
):
    step = pl.program_id(0)
    steps = pl.num_programs(0)
    groups = x_ref.shape[1] // q_out.shape[1]
    rows, slots = lens_ref.shape
    tokens, width = x_ref.shape
    length = tokens // rows
    copies = [
        pltpu.make_async_copy(low_ref, low_hbm, sems.at[0]),
        pltpu.make_async_copy(xhat1_ref, xhat1_hbm, sems.at[1]),
    ]

    chunk = wu_ref.shape[1] // 3

    def weight_copies(c):
        at = pl.ds(pl.multiple_of(c * chunk, chunk), chunk)
        return (
            pltpu.make_async_copy(wu_hbm.at[:, at], wu_ref.at[:, at], weight_sems.at[0, c]),
            pltpu.make_async_copy(wd_hbm.at[at, :], wd_ref.at[at, :], weight_sems.at[1, c]),
        )

    def out_copies(c, row):
        at = pl.ds(pl.multiple_of(c * chunk, chunk), chunk)
        rows_at = pl.ds(row * length, length)
        return (
            pltpu.make_async_copy(
                act_ref.at[rows_at, at], act_hbm.at[rows_at, at], out_sems.at[0, row, c]
            ),
            pltpu.make_async_copy(
                slope_ref.at[rows_at, at], slope_hbm.at[rows_at, at], out_sems.at[1, row, c]
            ),
        )

    def last_copy(row):
        rows_at = pl.ds(row * length, length)
        return pltpu.make_async_copy(
            xhat2_ref.at[rows_at, :], xhat2_hbm.at[rows_at, :], last_sems.at[row]
        )

    @pl.when(step == 0)
    def _():
        for c in range(3):
            for copy in weight_copies(c):
                copy.start()
        fill_mask(lens_ref, mask_ref)
        acc_ref[...] = x_ref[...].astype(f32) + line(bo)

    @pl.when(step < groups)
    def _():
        x = x_ref[...]
        q_out[...] = (dot(x, wq[...]) + line(bq)).astype(bf16)
        k_out[...] = dot(x, wk[...]).astype(bf16)
        v_out[...] = (dot(x, wv[...]) + line(bv)).astype(bf16)
        lane = lax.broadcasted_iota(jnp.int32, (1, 128), 1)
        first_half = lane < 64
        pairs = q_out.shape[1] // 128
        scale = bf16(64 ** (-0.5))
        for row in range(rows):
            for pair in range(pairs):
                at = slice(row * length, (row + 1) * length)
                lanes = slice(pair * 128, (pair + 1) * 128)
                q = q_out[at, lanes] * scale
                k = k_out[at, lanes]
                v = v_out[at, lanes]
                outs, logs = [], []
                for head in range(2):
                    mine = first_half == (head == 0)
                    scores = dot_rows(jnp.where(mine, q, bf16(0)), k) + mask_ref[row]
                    top = jnp.max(scores, axis=-1, keepdims=True)
                    shifted = jnp.exp(scores - top).astype(bf16)
                    out = dot(shifted, jnp.where(mine, v, bf16(1)))
                    total = pltpu.roll(out, 64, 1)
                    outs.append(out / total)
                    logs.append(top + jnp.log(jnp.where(mine, total, out)))
                mixed_out[at, lanes] = jnp.where(first_half, outs[0], outs[1]).astype(bf16)
                logs = jnp.transpose(jnp.where(first_half, logs[0], logs[1]))
                place = (step * pairs + pair) * 2
                lse_out[row, pl.ds(place, 1), :] = logs[0:1]
                lse_out[row, pl.ds(place + 1, 1), :] = logs[64:65]
        acc_ref[...] += dot(mixed_out[...], wo[...])

    @pl.when(step == groups - 1)
    def _():
        for row in range(rows):
            at = slice(row * length, (row + 1) * length)
            scaled, inverse = norm_stats(acc_ref[at, :])
            first = scaled * line(gain1) + line(shift1)
            acc_ref[at, :] = first + line(bd)
            low_ref[at, :] = first.astype(bf16)
            xhat1_ref[at, :] = scaled.astype(bf16)
            inv1_out[at, :] = inverse
        for copy in copies:
            copy.start()

    @pl.when(step >= groups)
    def _():
        c = step - groups
        part = min(chunk, 512)
        for copy in weight_copies(c):
            copy.wait()
        whole_at = pl.ds(pl.multiple_of(c * chunk, chunk), chunk)
        for row in range(rows):
            at = slice(row * length, (row + 1) * length)
            for low in range(0, chunk, part):
                lanes = pl.ds(pl.multiple_of(c * chunk + low, part), part)
                hidden = dot(low_ref[at, :], wu_ref[:, lanes]) + line(bu)[:, low : low + part]
                share = 0.5 + 0.5 * lax.erf(hidden * 0.7071067811865476)
                bell = jnp.exp(hidden * hidden * -0.5) * 0.3989422804014327
                act_ref[at, lanes] = (hidden * share).astype(bf16)
                slope_ref[at, lanes] = (share + hidden * bell).astype(bf16)
            for copy in out_copies(c, row):
                copy.start()
            acc_ref[at, :] += dot(act_ref[at, whole_at], wd_ref[whole_at, :])

    @pl.when(step == steps - 1)
    def _():
        for row in range(rows):
            at = slice(row * length, (row + 1) * length)
            own = slice(row * slots, (row + 1) * slots)
            scaled, inverse = norm_stats(acc_ref[at, :])
            xhat2_ref[at, :] = scaled.astype(bf16)
            last_copy(row).start()
            inv2_out[at, :] = inverse
            final = scaled * line(gain2) + line(shift2)
            high, low = split_low(final)
            seg = segment_of(lens_ref, row, lax.broadcasted_iota(jnp.int32, (slots, length), 1))
            member = (seg == lax.broadcasted_iota(jnp.int32, (slots, length), 0)).astype(f32)
            count = jnp.maximum(jnp.sum(member, axis=-1, keepdims=True), 1.0)
            member = member.astype(bf16)
            pooled = (dot(member, high) + dot(member, low)) / count
            pool_out[own, :] = pooled
            norm_sq = jnp.sum(pooled * pooled, axis=-1, keepdims=True)
            unit_out[own, :width] = (pooled * lax.rsqrt(norm_sq + pool_eps)).astype(bf16)
        spot = lax.broadcasted_iota(jnp.int32, (rows * slots, 128), 0)
        lane = lax.broadcasted_iota(jnp.int32, (rows * slots, 128), 1)
        marks = jnp.zeros((rows * slots, 128), jnp.int32)
        for row in range(rows):
            for slot in range(slots):
                live = (lens_ref[row, slot] > 0).astype(jnp.int32)
                target = targets_ref[Place()[1], row, slot]
                mark = jnp.where(lane == 0, live, jnp.where(lane == 1, target >> 6, target & 63))
                marks = jnp.where((spot == row * slots + slot) & (lane < 3), mark, marks)
        unit_out[:, width:] = marks.astype(f32).astype(bf16)
        for copy in copies:
            copy.wait()
        for row in range(rows):
            last_copy(row).wait()
            for c in range(3):
                for copy in out_copies(c, row):
                    copy.wait()


def forward(
    lens, targets, x, wq, wk, wv, wo, bq, bv, bo, gain1, shift1, wu, bu, wd, bd, gain2, shift2
):
    tokens, width = x.shape
    hidden = wu.shape[1]
    rows, slots = lens.shape
    length = tokens // rows
    group = 256
    groups = width // group
    chunk = hidden // 3
    near = lambda j: jnp.minimum(j, groups - 1)
    far = lambda j: jnp.maximum(j - groups, 0)
    cols = pl.BlockSpec((width, group), lambda j: (0, near(j)))
    bias = pl.BlockSpec((group,), lambda j: (near(j),))
    act = pl.BlockSpec((tokens, group), lambda j: (0, near(j)))
    vec = whole((width,))
    full = whole((tokens, width))
    one = whole((tokens, 1))
    return pl.pallas_call(
        forward_kernel,
        grid=(groups + hidden // chunk,),
        in_specs=[
            smem(), smem(), full, cols, cols, cols,
            pl.BlockSpec((group, width), lambda j: (near(j), 0)), bias, bias, vec, vec, vec,
            hbm(), pl.BlockSpec((chunk,), lambda j: (far(j),)), hbm(), vec, vec, vec,
        ],
        out_specs=[act] * 4 + [whole((rows, H, length)), hbm(), hbm(), one, hbm(), hbm(), hbm(), one]
        + [whole((rows * slots, width)), whole((rows * slots, width + 128))],
        out_shape=[shaped((tokens, width), bf16)] * 4
        + [
            shaped((rows, H, length), f32),
            shaped((tokens, width), bf16),
            shaped((tokens, width), bf16),
            shaped((tokens, 1), f32),
            shaped((tokens, hidden), bf16),
            shaped((tokens, hidden), bf16),
            shaped((tokens, width), bf16),
            shaped((tokens, 1), f32),
            shaped((rows * slots, width), f32),
            shaped((rows * slots, width + 128), bf16),
        ],
        scratch_shapes=[
            pltpu.VMEM((rows, length, length), f32),
            pltpu.VMEM((tokens, width), f32),
            pltpu.VMEM((tokens, width), bf16),
            pltpu.VMEM((tokens, width), bf16),
            pltpu.SemaphoreType.DMA((2,)),
            pltpu.VMEM((width, hidden), bf16),
            pltpu.VMEM((hidden, width), bf16),
            pltpu.VMEM((tokens, hidden), bf16),
            pltpu.VMEM((tokens, hidden), bf16),
            pltpu.VMEM((tokens, width), bf16),
            pltpu.SemaphoreType.DMA((2, 3)),
            pltpu.SemaphoreType.DMA((2, rows, 3)),
            pltpu.SemaphoreType.DMA((rows,)),
        ],
        compiler_params=params(60 << 20),
        cost_estimate=cost(8 * tokens * width * (width + hidden), 50 << 20),
        name="forward",
    )(lens, targets, x, wq, wk, wv, wo, bq, bv, bo, gain1, shift1, wu, bu, wd, bd, gain2, shift2)


def match_kernel(
    lens_ref, pool_ref, gain, inv_ref, *refs,
):
    row_refs, refs = refs[:8], refs[8:]
    (
    xhat_hbm, active_hbm, loss_out, grad_hbm, vec_out, send_hbm, keep_hbm, rows_ref, active_ref, xhat_ref, grad_out, both_ref, sems,
    ) = refs
    copies = Copies(sems)
    copies.start("xhat", xhat_hbm, xhat_ref)
    copies.start("active", active_hbm, active_ref)
    width = pool_ref.shape[1]
    slots = pool_ref.shape[0]
    rows, row_slots = lens_ref.shape
    length = xhat_ref.shape[0] // rows
    total = rows_ref.shape[1]
    outer = total // 4 // slots
    each = total // 4
    for i, block in enumerate(row_refs):
        rows_ref[i // 4, i % 4 * each : (i % 4 + 1) * each, :] = block[...].reshape(each, -1)
    spot = lax.broadcasted_iota(jnp.int32, (1, total), 1)
    group = spot // slots
    cores, sides, outers = group // (2 * outer), group // outer % 2, group % outer
    device = (Place()[4] ^ outers) * 2 + (Place()[3] ^ sides)
    numbers = ((Place()[1] ^ cores) * (2 * outer) + device) * slots + spot % slots
    passage_side = Place()[0]
    query_side = 1 - passage_side
    chunk = min(512, total)
    lane = lax.broadcasted_iota(jnp.int32, (8, 128), 1)
    passage_marks = rows_ref[passage_side, :, width:]
    passage_live = dot_rows((lane == 0).astype(bf16), passage_marks)[:1] > 0
    query_count = jnp.sum(rows_ref[query_side, :, width:][:, :1].astype(f32))
    per_query = 1.0 / query_count

    def part(i, carry):
        loss, as_query, as_passage = carry
        at = pl.ds(pl.multiple_of(i * chunk, chunk), chunk)
        marks = rows_ref[query_side, at, width:].astype(f32)
        live = marks[:, 0:1] > 0
        target = marks[:, 1:2].astype(jnp.int32) * 64 + marks[:, 2:3].astype(jnp.int32)
        queries = rows_ref[query_side, at, :width]
        passages = rows_ref[passage_side, :, :width]
        scores = dot_rows(queries, passages) * inverse_temp
        scores = jnp.where(passage_live, scores, masked_score)
        top = jnp.max(scores, axis=-1, keepdims=True)
        log_sum = top + jnp.log(jnp.sum(jnp.exp(scores - top), axis=-1, keepdims=True))
        is_target = numbers == target
        picked = jnp.sum(jnp.where(is_target, scores, 0.0), axis=-1, keepdims=True)
        loss = loss + jnp.sum(jnp.where(live, log_sum - picked, 0.0))
        chances = jnp.where(passage_live, jnp.exp(scores - log_sum), 0.0)
        grad = jnp.where(live, (chances - is_target.astype(f32)) * per_query, 0.0).astype(bf16)
        as_passage = as_passage + dot_cols(grad[:, :128], queries)[:slots]
        own = dot(grad[:slots], passages)
        as_query = jnp.where(i == 0, own, as_query)
        return loss, as_query, as_passage

    zeros = jnp.zeros((slots, width), f32)
    carry = (jnp.float32(0), zeros, zeros)
    if total == chunk:
        carry = part(0, carry)
    else:
        carry = lax.fori_loop(0, total // chunk, part, carry)
    loss, as_query, as_passage = carry
    loss_out[0, 0] = loss * per_query
    grad_unit = jnp.where(passage_side == 1, as_query, as_passage) * inverse_temp
    pooled = pool_ref[...]
    inverse = lax.rsqrt(jnp.sum(pooled * pooled, axis=-1, keepdims=True) + pool_eps)
    along = jnp.sum(grad_unit * pooled, axis=-1, keepdims=True)
    grad_pooled = inverse * grad_unit - pooled * (inverse * inverse * inverse) * along
    gain = line(gain)
    sums = []
    copies.wait("xhat")
    for row in range(rows):
        at = slice(row * length, (row + 1) * length)
        own = slice(row * row_slots, (row + 1) * row_slots)
        seg = segment_of(lens_ref, row, lax.broadcasted_iota(jnp.int32, (row_slots, length), 1))
        member = (seg == lax.broadcasted_iota(jnp.int32, (row_slots, length), 0)).astype(f32)
        count = jnp.maximum(jnp.sum(member, axis=-1, keepdims=True), 1.0)
        member = member.astype(bf16)
        high, low = split_low(grad_pooled[own] / count)
        grad_final = dot_cols(member, high) + dot_cols(member, low)
        scaled = xhat_ref[at, :].astype(f32)
        grad_sum = norm_back(grad_final, scaled, inv_ref[at, :], gain)
        grad_low = grad_sum.astype(bf16)
        grad_out[at, :] = grad_low
        sums.append(
            (
                jnp.sum(grad_final * scaled, axis=0, keepdims=True),
                jnp.sum(grad_final, axis=0, keepdims=True),
                jnp.sum(grad_low.astype(f32), axis=0, keepdims=True),
            )
        )
    for i in range(3):
        vec_out[i : i + 1, :] = sum(each[i] for each in sums)
    copies.start("grad", grad_out, grad_hbm)
    copies.wait("active")
    _, parts, sides, half, share = both_ref.shape
    turned = jnp.transpose(grad_out[...])
    for z in range(parts):
        at = slice(z * sides * share, (z + 1) * sides * share)
        both = dot(turned, active_ref[:, at]).astype(bf16)
        for core in range(2):
            for y in range(sides):
                lanes = slice(y * share, (y + 1) * share)
                both_ref[core, z, y] = both[core * half : (core + 1) * half, lanes]
        copies.start((z, 0), both_ref.at[Place()[5], z], send_hbm.at[z])
        copies.start((z, 1), both_ref.at[Place()[1], z], keep_hbm.at[z])
    copies.wait("grad", *[(z, i) for z in range(parts) for i in range(2)])


def match(lens, rows, pooled, xhat, inverse, gain, active):
    tokens, width = xhat.shape
    slots = pooled.shape[0]
    vmem = pl.BlockSpec(memory_space=pltpu.VMEM)
    return pl.pallas_call(
        match_kernel,
        in_specs=[smem()] + [vmem] * 11 + [hbm(), hbm()],
        out_specs=[smem(), hbm(), vmem, hbm(), hbm()],
        out_shape=[
            shaped((1, 1), f32),
            shaped((tokens, width), bf16),
            shaped((8, width), f32),
            shaped((4, 2, width // 2, active.shape[1] // 8), bf16),
            shaped((4, 2, width // 2, active.shape[1] // 8), bf16),
        ],
        scratch_shapes=[
            pltpu.VMEM((2, rows[0].size * 4 // (width + 128), width + 128), bf16),
            pltpu.VMEM(active.shape, bf16),
            pltpu.VMEM((tokens, width), bf16),
            pltpu.VMEM((tokens, width), bf16),
            pltpu.VMEM((2, 4, 2, width // 2, active.shape[1] // 8), bf16),
            pltpu.SemaphoreType.DMA((11,)),
        ],
        compiler_params=params(60 << 20),
        cost_estimate=cost(2e9, 10 << 20),
        name="match",
    )(lens, pooled, gain, inverse, *rows, xhat, active)


def hidden_kernel(
    grad_hbm, slope_hbm, wd_hbm, low_hbm, hidden_hbm, bias_out, send_hbm,
    grad_ref, slope_ref, wd_ref, low_ref, hidden_ref, send_ref, sems, send_sems,
):
    parts, width, chunk = 4, wd_ref.shape[1], wd_ref.shape[0] // 4

    def span(j):
        return pl.ds(pl.multiple_of(j * chunk, chunk), chunk)

    def wd_copy(j):
        return pltpu.make_async_copy(wd_hbm.at[span(j), :], wd_ref.at[span(j), :], sems.at[2 + j])

    def slope_copy(j):
        return pltpu.make_async_copy(slope_hbm.at[:, span(j)], slope_ref.at[:, span(j)], sems.at[6 + j])

    def hidden_copy(j):
        return pltpu.make_async_copy(hidden_ref.at[:, span(j)], hidden_hbm.at[:, span(j)], sems.at[10 + j])

    def send_copy(i):
        return pltpu.make_async_copy(send_ref.at[i], send_hbm.at[i], send_sems.at[i])

    grad_copy = pltpu.make_async_copy(grad_hbm, grad_ref, sems.at[0])
    low_copy = pltpu.make_async_copy(low_hbm, low_ref, sems.at[1])
    grad_copy.start()
    wd_copy(0).start()
    slope_copy(0).start()
    low_copy.start()
    for j in range(1, parts):
        wd_copy(j).start()
        slope_copy(j).start()
    grad_copy.wait()

    def step(j, carry):
        at = span(j)
        wd_copy(j).wait()
        slope_copy(j).wait()
        grad = dot_rows(grad_ref[...], wd_ref[at, :]) * slope_ref[:, at].astype(f32)
        grad_low = grad.astype(bf16)
        hidden_ref[:, at] = grad_low
        bias_out[:, at] = jnp.sum(grad_low.astype(f32), axis=0, keepdims=True)
        hidden_copy(j).start()

        @pl.when(j == 0)
        def _():
            low_copy.wait()

        @pl.when(j // 2 == Place()[5])
        def _():
            send_ref[j % 2] = dot_cols(low_ref[...], hidden_ref[:, at]).astype(bf16)
            send_copy(j % 2).start()

        return carry

    lax.fori_loop(0, parts, step, 0)
    for j in range(parts):
        hidden_copy(j).wait()
    for i in range(2):
        send_copy(i).wait()


def hidden_grad(grad, slope, wd, low):
    tokens, width = grad.shape
    hidden = wd.shape[0]
    chunk = hidden // 4
    return pl.pallas_call(
        hidden_kernel,
        in_specs=[hbm()] * 4,
        out_specs=[hbm(), pl.BlockSpec(memory_space=pltpu.VMEM), hbm()],
        out_shape=[
            shaped((tokens, hidden), bf16),
            shaped((1, hidden), f32),
            shaped((2, width, chunk), bf16),
        ],
        scratch_shapes=[
            pltpu.VMEM((tokens, width), bf16),
            pltpu.VMEM((tokens, hidden), bf16),
            pltpu.VMEM((hidden, width), bf16),
            pltpu.VMEM((tokens, width), bf16),
            pltpu.VMEM((tokens, hidden), bf16),
            pltpu.VMEM((2, width, chunk), bf16),
            pltpu.SemaphoreType.DMA((14,)),
            pltpu.SemaphoreType.DMA((2,)),
        ],
        compiler_params=params(60 << 20),
        cost_estimate=cost(3 * tokens * width * hidden, 22 << 20),
        name="hidden_grad",
    )(grad, slope, wd, low)


def feed_back_kernel(
    fast, inv_ref, gain, grad_hbm, hidden_hbm, wu_hbm, wo_hbm, xhat_hbm, low_hbm, mixed_hbm, got_hbm,
    vec_out, branch_hbm, back_hbm, send_hbm, keep_hbm, *refs,
):
    outs, refs = refs[: 4 * fast], refs[4 * fast :]
    grad_ref, hidden_ref, wu_ref, wo_ref, xhat_ref, low_ref, mixed_ref, got_ref, *refs = refs
    branch_ref, back_ref, send_ref, keep_ref, acc_ref, part_ref, sems, *pieces = refs
    tokens, width = grad_ref.shape
    half, narrow, chunk, parts = tokens // 2, width // 2, part_ref.shape[1], 4
    copies = Copies(sems)
    copies.start("grad", grad_hbm, grad_ref)
    for j in range(parts):
        at = slice(j * chunk, (j + 1) * chunk)
        copies.start(("hidden", j), hidden_hbm.at[:, at], hidden_ref.at[:, at])
        copies.start(("wu", j), wu_hbm.at[:, at], wu_ref.at[:, at])
        if j == 0:
            copies.start("low", low_hbm, low_ref)
            copies.start("got", got_hbm, got_ref)
    copies.start("xhat", xhat_hbm, xhat_ref)
    copies.start("wo", wo_hbm, wo_ref)
    copies.start("mixed", mixed_hbm, mixed_ref)
    copies.wait("grad")
    acc_ref[...] = grad_ref[...].astype(f32)
    for j in range(parts):
        at = slice(j * chunk, (j + 1) * chunk)
        copies.wait(("hidden", j), ("wu", j))
        for part in range(2):
            rows = slice(part * half, (part + 1) * half)
            acc_ref[rows, :] += dot_rows(hidden_ref[rows, at], wu_ref[:, at])
        if j == 0:
            copies.wait("low", "got")
        if not fast:
            continue
        size = pieces[0].shape[2]
        first = pieces[0].shape[3] - chunk

        @pl.when(j // 2 == Place()[1])
        def _():
            part_ref[...] = dot_cols(low_ref[...], hidden_ref[:, at]) + got_ref[j % 2].astype(f32)
            if j % 2 == 0:
                cut_rows(part_ref, pieces[:2], slice(0, chunk), False, size)
            else:
                lanes = slice(chunk, chunk + first)
                cut_rows(part_ref.at[:, :first], pieces[:2], lanes, False, size)
                lanes = slice(narrow, narrow + chunk - first)
                cut_rows(part_ref.at[:, first:], pieces[2:], lanes, True, size)

    for i in range(4 * fast):
        copies.start(("piece", i), pieces[i], outs[i])
    copies.wait("xhat", "wo", "mixed")
    tallies = []
    for part in range(2):
        rows = slice(part * half, (part + 1) * half)
        grad = acc_ref[rows, :]
        scaled = xhat_ref[rows, :].astype(f32)
        grad_low = norm_back(grad, scaled, inv_ref[rows, :], line(gain)).astype(bf16)
        branch_ref[rows, :] = grad_low
        copies.start(("branch", part), branch_ref.at[rows, :], branch_hbm.at[rows, :])
        back_ref[rows, :] = dot_rows(grad_low, wo_ref[...]).astype(bf16)
        copies.start(("back", part), back_ref.at[rows, :], back_hbm.at[rows, :])
        tallies.append(
            (
                jnp.sum(grad * scaled, axis=0, keepdims=True),
                jnp.sum(grad, axis=0, keepdims=True),
                jnp.sum(grad_low.astype(f32), axis=0, keepdims=True),
            )
        )
    for i in range(3):
        vec_out[i : i + 1, :] = tallies[0][i] + tallies[1][i]
    for i, out in ((1, send_ref), (0, keep_ref)):
        at = pl.ds(pl.multiple_of(Place()[1 + 4 * i] * narrow, narrow), narrow)
        out[...] = dot_cols(mixed_ref[...], branch_ref[:, at]).astype(bf16)
        copies.start(("out", i), out, (keep_hbm, send_hbm)[i])
    copies.wait(*[("piece", i) for i in range(4 * fast)])
    copies.wait(*[(name, i) for name in ("branch", "back", "out") for i in range(2)])


def feed_back(grad, grad_hidden, wu, wo, xhat, inverse, gain, low, mixed, got, fast):
    tokens, width = grad.shape
    hidden = wu.shape[1]
    chunk = hidden // 4
    narrow = width // 2
    first = chunk + width // 3
    pieces = [(2, 4, width // 16, first)] * 2 + [(2, 4, width // 16, 2 * chunk - first + narrow)] * 2
    pieces = [(each, bf16) for each in pieces] if fast else []
    full, strip = ((tokens, width), bf16), ((width, narrow), bf16)
    vmem = pl.BlockSpec(memory_space=pltpu.VMEM)
    scratch = [
        full, ((tokens, hidden), bf16), ((width, hidden), bf16), ((width, width), bf16), full, full, full,
        ((2, width, chunk), bf16), full, full, strip, strip, ((tokens, width), f32), ((width, chunk), f32),
    ]
    return pl.pallas_call(
        partial(feed_back_kernel, int(fast)),
        in_specs=[vmem, vmem] + [hbm()] * 8,
        out_specs=[vmem] + [hbm()] * (4 + len(pieces)),
        out_shape=[
            shaped((8, width), f32), shaped(*full), shaped(*full), shaped(*strip), shaped(*strip)
        ]
        + [shaped(*each) for each in pieces],
        scratch_shapes=[pltpu.VMEM(*each) for each in scratch]
        + [pltpu.SemaphoreType.DMA((24,))]
        + [pltpu.VMEM(*each) for each in pieces],
        compiler_params=params(60 << 20),
        cost_estimate=cost(4 * tokens * width * hidden, 30 << 20),
        name="feed_back",
    )(inverse, gain, grad, grad_hidden, wu, wo, xhat, low, mixed, got)


def join_kernel(keep_ref, got_ref, *refs):
    outs, acc_ref = refs[2:4], refs[4]
    acc_ref[...] = keep_ref[...].astype(f32) + got_ref[...].astype(f32)
    cut_rows(acc_ref, outs, slice(None), True, outs[0].shape[2])


def join_out(keep, got, pieces):
    width, narrow = keep.shape
    piece = pl.BlockSpec((2, 4, width // 16, narrow), lambda j: (0, 0, 0, 0))
    return pl.pallas_call(
        join_kernel,
        grid=(1,),
        in_specs=[whole(keep.shape), whole(got.shape)]
        + [pl.BlockSpec(memory_space=pl.ANY)] * 2,
        out_specs=[piece] * 2,
        out_shape=[shaped(each.shape, bf16) for each in pieces],
        input_output_aliases={2 + i: i for i in range(2)},
        scratch_shapes=[pltpu.VMEM((width, narrow), f32)],
        compiler_params=params(8 << 20),
        cost_estimate=cost(0, 3 << 20),
        name="join_out",
    )(keep, got, *pieces)


def probs_kernel(group, lens_ref, q_ref, k_ref, lse_ref, *refs):
    out, mask_ref = refs[-2:]
    step = pl.program_id(0)
    rows, length, _ = mask_ref.shape

    @pl.when(step == 0)
    def _():
        fill_mask(lens_ref, mask_ref)

    lane = lax.broadcasted_iota(jnp.int32, (1, 128), 1)
    pairs = q_ref.shape[1] // 128
    for pair in range(pairs):
        lanes = slice(pair * 128, (pair + 1) * 128)
        for row in range(rows):
            at = slice(row * length, (row + 1) * length)
            q = q_ref[at, lanes] * bf16(64 ** (-0.5))
            k = k_ref[at, lanes]
            for head in range(2):
                own = jnp.where((lane < 64) == (head == 0), q, bf16(0))
                place = ((step + group) * pairs + pair) * 2 + head
                log_total = lse_ref[row, pl.ds(place, 1), :]
                scores = dot_rows(k, own) + mask_ref[row]
                out[0, (row * pairs + pair) * 2 + head] = jnp.exp(scores - log_total).astype(bf16)


def probs_of(lens, q, k, lse, group, count, before=None):
    tokens, width = q.shape
    rows = lens.shape[0]
    length = tokens // rows
    lanes = 256
    heads = rows * lanes // 64
    act = pl.BlockSpec((tokens, lanes), lambda j: (0, j + group))
    return pl.pallas_call(
        partial(probs_kernel, group),
        grid=(count,),
        in_specs=[smem(), act, act, whole(lse.shape)] + ([] if before is None else [hbm()]),
        out_specs=pl.BlockSpec((1, heads, length, length), lambda j: (j + group, 0, 0, 0)),
        out_shape=shaped((width // lanes, heads, length, length), bf16),
        input_output_aliases={} if before is None else {4: 0},
        scratch_shapes=[pltpu.VMEM((rows, length, length), f32)],
        compiler_params=params(60 << 20),
        cost_estimate=cost(count * 4 * heads * length * length * 256, count << 22),
        name="probs",
    )(lens, q, k, lse, *(() if before is None else (before,)))


def attend_back_kernel(
    q_ref, k_ref, v_ref, probs_ref, mixed_ref, grad_ref, x_ref,
    first_sums, second_sums, up_sums, out, vec_out, send_out, keep_out, own_out, other_out, sums_ref, pack_ref,
):
    step = pl.program_id(0)
    length = probs_ref.shape[2]
    rows = q_ref.shape[0] // length

    lane = lax.broadcasted_iota(jnp.int32, (1, 128), 1)
    scale = 64 ** (-0.5)
    pairs = q_ref.shape[1] // 128
    for pair in range(pairs):
        lanes = slice(pair * 128, (pair + 1) * 128)
        query_sums, value_sums = [], []
        for row in range(rows):
            tokens = slice(row * length, (row + 1) * length)
            q = q_ref[tokens, lanes] * bf16(scale)
            k = k_ref[tokens, lanes]
            v = v_ref[tokens, lanes]
            grad = grad_ref[tokens, lanes]
            high, low = split_low(grad.astype(f32) * mixed_ref[tokens, lanes].astype(f32))
            grad_v = grad_k = grad_q = 0.0
            for head in range(2):
                mine = (lane < 64) == (head == 0)
                ones = jnp.broadcast_to(jnp.where(mine, 1.0, 0.0), (8, 128)).astype(bf16)
                inner = (dot_rows(ones, high) + dot_rows(ones, low))[:1]
                own_q = jnp.where(mine, q, bf16(0))
                own_grad = jnp.where(mine, grad, bf16(0))
                probs = probs_ref[0, (row * pairs + pair) * 2 + head]
                grad_scores = (probs.astype(f32) * (dot_rows(v, own_grad) - inner)).astype(bf16)
                grad_v = grad_v + dot(probs, own_grad)
                grad_k = grad_k + dot(grad_scores, own_q)
                grad_q = grad_q + dot_cols(jnp.where(mine, k, bf16(0)), grad_scores)
            grad_q = (jnp.transpose(grad_q) * scale).astype(bf16)
            grad_v = grad_v.astype(bf16)
            out[0, tokens, lanes] = grad_q
            out[1, tokens, lanes] = grad_k.astype(bf16)
            out[2, tokens, lanes] = grad_v
            query_sums.append(jnp.sum(grad_q.astype(f32), axis=0, keepdims=True))
            value_sums.append(jnp.sum(grad_v.astype(f32), axis=0, keepdims=True))
        vec_out[0:1, lanes] = sum(query_sums)
        vec_out[1:2, lanes] = sum(value_sums)
        at = pl.ds(pl.multiple_of((step * pairs + pair) * 128, 128), 128)
        sums_ref[0:1, at] = sum(query_sums)
        sums_ref[1:2, at] = sum(value_sums)
    for core, target in ((Place()[5], send_out), (Place()[1], keep_out)):
        lanes = pl.ds(pl.multiple_of(core * 128, 128), 128)
        grads = jnp.concatenate([out[i, :, lanes] for i in range(3)], axis=1)
        target[...] = dot_cols(x_ref[...], grads).astype(bf16)

    @pl.when(step == pl.num_programs(0) - 1)
    def _():
        sums = [sums_ref[i : i + 1, :] for i in range(2)]
        sums += [first_sums[2:3, :], second_sums[2:3, :], first_sums[0:1, :], first_sums[1:2, :]]
        sums += [second_sums[0:1, :], second_sums[1:2, :]]
        width = x_ref.shape[1]
        share = width // 8
        pack_ref[...] = jnp.zeros(pack_ref.shape, f32)
        for n in range(12):
            for d in range(8):
                if n < 8:
                    piece = sums[n][:, d * share : (d + 1) * share]
                else:
                    piece = up_sums[:, (d * 4 + n - 8) * share : (d * 4 + n - 7) * share]
                row = (d * 2 + n // 3 % 2) * (width // 16) + n % 3
                pack_ref[n // 6, row : row + 1, :share] = piece
        own_out[...] = pack_ref[Place()[1]].astype(bf16)
        other_out[...] = pack_ref[Place()[5]].astype(bf16)


def attend_back(q, k, v, probs, mixed, grad, x, first_sums, second_sums, up_sums):
    tokens, width = q.shape
    group = 256
    act = pl.BlockSpec((tokens, group), lambda j: (0, j))
    scores = pl.BlockSpec((1,) + probs.shape[1:], lambda j: (j, 0, 0, 0))
    return pl.pallas_call(
        attend_back_kernel,
        grid=(width // group,),
        in_specs=[act, act, act, scores, act, act, whole(x.shape)]
        + [whole(each.shape) for each in (first_sums, second_sums, up_sums)],
        out_specs=[
            pl.BlockSpec((3, tokens, group), lambda j: (0, 0, j)),
            pl.BlockSpec((8, group), lambda j: (0, j)),
            pl.BlockSpec((width, 384), lambda j: (0, j)),
            pl.BlockSpec((width, 384), lambda j: (0, j)),
            whole((width, 128)),
            whole((width, 128)),
        ],
        out_shape=[
            shaped((3, tokens, width), bf16),
            shaped((8, width), f32),
            shaped((width, width // group * 384), bf16),
            shaped((width, width // group * 384), bf16),
            shaped((width, 128), bf16),
            shaped((width, 128), bf16),
        ],
        scratch_shapes=[
            pltpu.VMEM((8, width), f32),
            pltpu.VMEM((2, width, 128), f32),
        ],
        compiler_params=params(60 << 20),
        cost_estimate=cost(20 * tokens * probs.shape[2] * width, 30 << 20),
        name="attend_back",
    )(q, k, v, probs, mixed, grad, x, first_sums, second_sums, up_sums)


def input_kernel(branch_hbm, grads_hbm, wq_hbm, wk_hbm, wv_hbm, out_hbm, branch_ref, grads_ref, weights_ref, out_ref, sems):
    copies = Copies(sems)
    for m, weight in enumerate((wq_hbm, wk_hbm, wv_hbm)):
        copies.start(("w", m), weight, weights_ref.at[m])
        copies.start(("g", m), grads_hbm.at[m], grads_ref.at[m])
        if m == 0:
            copies.start("branch", branch_hbm, branch_ref)
    tokens = out_ref.shape[0]
    parts = 4
    for m in range(3):
        copies.wait(("w", m), ("g", m))
        if m == 0:
            copies.wait("branch")
        for part in range(parts):
            rows = slice(part * tokens // parts, (part + 1) * tokens // parts)
            before = branch_ref[rows, :].astype(f32) if m == 0 else out_ref[rows, :]
            out_ref[rows, :] = before + dot_rows(grads_ref[m, rows, :], weights_ref[m])
            if m == 2:
                copies.start(("out", part), out_ref.at[rows, :], out_hbm.at[rows, :])
    copies.wait(*[("out", part) for part in range(parts)])


def input_grad(branch, grads, wq, wk, wv):
    tokens, width = branch.shape
    return pl.pallas_call(
        input_kernel,
        in_specs=[hbm()] * 5,
        out_specs=hbm(),
        out_shape=shaped((tokens, width), f32),
        scratch_shapes=[
            pltpu.VMEM((tokens, width), bf16),
            pltpu.VMEM((3, tokens, width), bf16),
            pltpu.VMEM((3, width, width), bf16),
            pltpu.VMEM((tokens, width), f32),
            pltpu.SemaphoreType.DMA((11,)),
        ],
        compiler_params=params(60 << 20),
        cost_estimate=cost(6 * tokens * width * width, 13 << 20),
        name="input_grad",
    )(branch, grads, wq, wk, wv)


def down_kernel(keep_hbm, got_hbm, *refs):
    outs, refs = refs[:4], refs[4:]
    keep_ref, got_ref, acc_ref, sems, *pieces = refs
    parts, _, half, _ = got_ref.shape
    copies = Copies(sems)
    for z in range(parts):
        copies.start(("keep", z), keep_hbm.at[z], keep_ref.at[z])
        copies.start(("got", z), got_hbm.at[z], got_ref.at[z])
    strip = half // 4
    for z in range(parts):
        copies.wait(("keep", z), ("got", z))
        for y in range(2):
            acc_ref[...] = keep_ref[z, y].astype(f32) + got_ref[z, y].astype(f32)
            for rel in range(2):
                at = pl.multiple_of((Place()[2] ^ rel) * 2 * strip, 2 * strip)
                pieces[rel][y, z] = acc_ref[pl.ds(at, strip), :].astype(bf16)

                @pl.when(Place()[3] == y ^ rel)
                def _():
                    for x in range(2):
                        rows = slice((2 * x + 1) * strip, (2 * x + 2) * strip)
                        pieces[2 + rel][x, z] = acc_ref[rows, :].astype(bf16)

        for i in range(4):
            copies.start(("piece", i, z), pieces[i].at[:, z], outs[i].at[:, z])
    copies.wait(*[("piece", i, z) for i in range(4) for z in range(parts)])


def down_grad(keep, got):
    parts, _, half, share = got.shape
    piece = (2, parts, half // 4, share)
    return pl.pallas_call(
        down_kernel,
        in_specs=[hbm()] * 2,
        out_specs=[hbm()] * 4,
        out_shape=[shaped(piece, bf16)] * 4,
        scratch_shapes=[
            pltpu.VMEM(got.shape, bf16),
            pltpu.VMEM(got.shape, bf16),
            pltpu.VMEM((half, share), f32),
            pltpu.SemaphoreType.DMA((24,)),
        ]
        + [pltpu.VMEM(piece, bf16)] * 4,
        compiler_params=params(60 << 20),
        cost_estimate=cost(0, 7 << 20),
        name="down_keep",
    )(keep, got)


def cut_rows(acc_ref, outs, at, by_y, size):
    outer = acc_ref.shape[0] // 4 // size
    for rel, out in enumerate(outs):
        for z in range(outer):
            for i in range(2):
                y, x = (Place()[3] ^ rel, i) if by_y else (i, Place()[2] ^ rel)
                row = pl.multiple_of(((z * 2 + y) * 2 + x) * size, size)
                out[i, z, :, at] = acc_ref[pl.ds(row, size), :].astype(bf16)


def head_kernel(vec_ref, got_vec_ref, keep_hbm, got_hbm, *refs):
    outs, (keep_ref, got_ref, acc_ref, sems) = refs[:4], refs[4:]
    width, total = keep_ref.shape
    half, size = outs[0].shape[3], outs[0].shape[2]
    parts = width // 4 // size
    span = width // parts
    copies = Copies(sems)
    for z in range(parts):
        rows = slice(z * span, (z + 1) * span)
        copies.start(("keep", z), keep_hbm.at[rows, :], keep_ref.at[rows, :])
        copies.start(("got", z), got_hbm.at[rows, :], got_ref.at[rows, :])
    for z in range(parts):
        rows = slice(z * span, (z + 1) * span)
        acc_ref[:, total:] = vec_ref[rows, :].astype(f32) + got_vec_ref[rows, :].astype(f32)
        copies.wait(("keep", z), ("got", z))
        acc_ref[:, :total] = keep_ref[rows, :].astype(f32) + got_ref[rows, :].astype(f32)
        for rel in range(2):
            for i in range(2):
                at = pl.multiple_of((i * 2 + (Place()[2] ^ rel)) * size, size)
                outs[rel][i, z] = acc_ref[pl.ds(at, size), :half].astype(bf16)
                at = pl.multiple_of(((Place()[3] ^ rel) * 2 + i) * size, size)
                outs[2 + rel][i, z] = acc_ref[pl.ds(at, size), half:].astype(bf16)


def head_grad(keep, vectors, got_vectors, got):
    width, total = keep.shape
    piece_shape = (2, 4, width // 16, (total + 128) // 2)
    vmem = pl.BlockSpec(memory_space=pltpu.VMEM)
    return pl.pallas_call(
        head_kernel,
        in_specs=[vmem, vmem] + [hbm()] * 2,
        out_specs=[vmem] * 4,
        out_shape=[shaped(piece_shape, bf16)] * 4,
        scratch_shapes=[
            pltpu.VMEM(keep.shape, bf16),
            pltpu.VMEM(keep.shape, bf16),
            pltpu.VMEM((width // 4, total + 128), f32),
            pltpu.SemaphoreType.DMA((8,)),
        ],
        compiler_params=params(12 << 20),
        cost_estimate=cost(0, 6 << 20),
        name="head_keep",
    )(vectors, got_vectors, keep, got)


def mix_kernel(which, parts, *refs):
    ins, outs = refs[:-parts], refs[-parts:]
    for rel, out in enumerate(outs):
        at = Place()[which] ^ rel if parts > 1 else 0
        total = ins[0][at].astype(f32)
        for ref in ins[1:]:
            total = total + ref[at].astype(f32)
        out[...] = total.astype(bf16)


def mix(which, arrays):
    parts = arrays[0].shape[0]
    return pl.pallas_call(
        partial(mix_kernel, which, parts),
        in_specs=[pl.BlockSpec(memory_space=pltpu.VMEM)] * len(arrays),
        out_specs=[pl.BlockSpec(memory_space=pltpu.VMEM)] * parts,
        out_shape=[shaped(arrays[0].shape[1:], bf16)] * parts,
        compiler_params=params(8 << 20),
        cost_estimate=cost(0, 2 * arrays[0].size * (len(arrays) + 1)),
        name="mix",
    )(*arrays)


def first_exchange(parts):
    return [parts[0], swap(parts[1], "tower", 2), parts[2], swap(parts[3], "dp", 1)]


def second_exchange(parts):
    return [parts[0], swap(parts[1], "dp", 1), parts[2], swap(parts[3], "tower", 2)]


def cross_kernel(*refs):
    ins, outs = refs[:4], refs[4:]
    for i in range(2):
        mine, got = ins[2 * i : 2 * i + 2]
        for rel in range(2):
            at = Place()[3 - i] ^ rel
            outs[2 * i + rel][...] = (mine[at].astype(f32) + got[at].astype(f32)).astype(bf16)


def cross(parts):
    vmem = pl.BlockSpec(memory_space=pltpu.VMEM)
    return pl.pallas_call(
        cross_kernel,
        in_specs=[vmem] * 4,
        out_specs=[vmem] * 4,
        out_shape=[shaped(each.shape[1:], bf16) for each in parts],
        compiler_params=params(5 << 20),
        cost_estimate=cost(0, 6 << 20),
        name="cross",
    )(*parts)


def outer_kernel(axis, *refs):
    ins, outs = refs[:4], refs[4:]
    for rel, out in enumerate(outs):
        at = Place()[4] ^ rel
        sums = [ins[2 * i][at].astype(f32) + ins[2 * i + 1][at].astype(f32) for i in range(2)]
        out[...] = jnp.concatenate(sums, axis=axis).astype(bf16)


def cut_halves(axis, parts):
    vmem = pl.BlockSpec(memory_space=pltpu.VMEM)
    outer = parts[0].shape[0]
    shape = list(parts[0].shape[1:])
    shape[axis] += parts[2].shape[1 + axis]
    return pl.pallas_call(
        partial(outer_kernel, axis),
        in_specs=[vmem] * 4,
        out_specs=[vmem] * outer,
        out_shape=[shaped(tuple(shape), bf16)] * outer,
        compiler_params=params(8 << 20),
        cost_estimate=cost(0, 3 << 20),
        name="cut_halves",
    )(*parts)


def near_kernel(axis, *refs):
    ins, outs = refs[:4], refs[4:]
    for rel, out in enumerate(outs):
        for upper in range(out.shape[0]):
            at = upper * 2 + ((Place()[4] & 1) ^ rel)
            sums = [ins[2 * i][at].astype(f32) + ins[2 * i + 1][at].astype(f32) for i in range(2)]
            out[upper] = jnp.concatenate(sums, axis=axis).astype(bf16)


def cut_near(axis, parts):
    vmem = pl.BlockSpec(memory_space=pltpu.VMEM)
    shape = list(parts[0].shape[1:])
    shape[axis] += parts[2].shape[1 + axis]
    return pl.pallas_call(
        partial(near_kernel, axis),
        in_specs=[vmem] * 4,
        out_specs=[vmem] * 2,
        out_shape=[shaped((parts[0].shape[0] // 2, *shape), bf16)] * 2,
        compiler_params=params(8 << 20),
        cost_estimate=cost(0, 3 << 20),
        name="cut_near",
    )(*parts)


def near_exchange(parts):
    return [parts[0], swap(parts[1], "dp", 2)]


def far_exchange(parts):
    return [parts[0], swap(parts[1], "dp", 4)]


def exchange_outer(parts):
    return [parts[0]] + [swap(part, "dp", 2 * rel) for rel, part in enumerate(parts) if rel]


def join_outer(parts):
    return mix(4, [part[None] for part in parts])[0]


def spread_kernel(kind, *refs):
    blocks, outs = refs[:4], refs[4:]
    core, far = Place()[1], Place()[2]
    share = outs[0].shape[0]
    for i, block in enumerate(blocks):
        c, x = core ^ (i >> 1), far ^ (i & 1)
        value = block[...].astype(f32)
        size = value.shape[0]
        rows = pl.ds(pl.multiple_of(x * size, size), size)
        if kind == "down":
            at = pl.multiple_of((c * 2 + x) * size, size)
            refs[-1][pl.ds(at, size), :] = value
            continue
        half = outs[1].shape[1] // 2
        if kind == "up":
            total = outs[0].shape[1] // 2
            wide = pl.ds(pl.multiple_of(c * total, total), total)
            narrow = pl.ds(pl.multiple_of(c * half, half), half)
            first = total // 3 * 2
            outs[0][rows, wide] = jnp.concatenate([value[:, :first], value[:, first + half :]], axis=1)
            outs[1][rows, narrow] = value[:, first : first + half]
        else:
            groups = half // 128
            for j in range(groups):
                lanes = pl.ds(pl.multiple_of(j * 256 + c * 128, 128), 128)
                for m in range(3):
                    outs[m][rows, lanes] = value[:, (j * 3 + m) * 128 : (j * 3 + m + 1) * 128]
            refs[-1][c * 2 + x] = value[:16, 3 * half :]
    if kind == "down":
        outs[0][...] = jnp.transpose(refs[-1][...])
    if kind == "head":
        for n in range(8):
            outs[3 + n][...] = refs[-1][n // 3, n % 3 : n % 3 + 1, :share].reshape(-1)
        last = [refs[-1][n // 3, n % 3 : n % 3 + 1, :share] for n in range(8, 12)]
        outs[11][...] = jnp.concatenate(last, axis=1).reshape(-1)


def spread(kind, block, far, shapes):
    blocks = [block, far, swap(block, "tower", 1), swap(far, "tower", 1)]
    return pl.pallas_call(
        partial(spread_kernel, kind),
        in_specs=[pl.BlockSpec(memory_space=pltpu.VMEM)] * 4,
        out_specs=[pl.BlockSpec(memory_space=pltpu.VMEM)] * len(shapes),
        out_shape=[shaped(shape, f32) for shape in shapes],
        scratch_shapes=[pltpu.VMEM((4, 16, 128) if kind == "head" else shapes[0][::-1], f32)],
        compiler_params=params(8 << 20),
        cost_estimate=cost(0, 2 << 20),
        name="spread_" + kind,
    )(*blocks)


def shards(
    layer_input,
    seg_lengths,
    positives,
    query_weight,
    key_weight,
    value_weight,
    out_weight,
    up_weight,
    down_weight,
    query_bias,
    value_offset_bias,
    out_bias,
    up_bias,
    down_bias,
    first_gain,
    first_shift,
    second_gain,
    latter_norm_translation,
):
    row_count = layer_input.shape[1]
    row_len = layer_input.shape[2]
    width = layer_input.shape[3]
    slot_count = seg_lengths.shape[2]
    token_count = row_count * row_len
    dp_count = lax.axis_size("dp")
    flat_in = layer_input.reshape(token_count, width)
    lens = seg_lengths.reshape(row_count, slot_count)

    (
        q, k, v, mixed, lse, low, first_scaled, first_inverse,
        active, slope, second_scaled, second_inverse, pooled, unit,
    ) = forward(
        lens, positives, flat_in, query_weight, key_weight, value_weight, out_weight,
        query_bias, value_offset_bias, out_bias, first_gain, first_shift,
        up_weight, up_bias, down_weight, down_bias, second_gain, latter_norm_translation,
    )
    rows, probs = gather_all(
        unit,
        lambda: probs_of(lens, q, k, lse, 0, 1),
        lambda before: probs_of(lens, q, k, lse, 1, width // 256 - 1, before),
    )
    loss, grad_second, second_sums, down_half, down_keep = match(
        lens, rows, pooled, second_scaled, second_inverse, second_gain, active
    )
    loss = loss.reshape(())
    share = width // dp_count
    fast = dp_count == 8 and lax.axis_size("tower") == 4
    grad_hidden, up_sums, up_half = hidden_grad(grad_second, slope, down_weight, low)
    if fast:
        got = swap(down_half, "tower", 1)
        got, grad_hidden, up_half = lax.optimization_barrier((got, grad_hidden, up_half))
        down_parts = down_grad(down_keep, got)
        up_half = swap(up_half, "tower", 1)
        down_parts, grad_hidden, up_half = lax.optimization_barrier(
            (down_parts, grad_hidden, up_half)
        )
        down_parts = first_exchange(down_parts)
    first_sums, grad_branch, grad_mixed, out_half, out_keep, *up_parts = feed_back(
        grad_second, grad_hidden, up_weight, out_weight, first_scaled, first_inverse,
        first_gain, low, mixed, up_half, fast,
    )
    if fast:
        down_parts, out_half = lax.optimization_barrier((down_parts, out_half))
        out_half = swap(out_half, "tower", 1)
        down_parts = cross(down_parts)
        down_parts, out_half = lax.optimization_barrier((down_parts, out_half))
        up_parts[2:] = join_out(out_keep, out_half, up_parts[2:])
        up_parts, down_parts, grad_mixed = lax.optimization_barrier((up_parts, down_parts, grad_mixed))
        up_parts = first_exchange(up_parts)
        down_parts = second_exchange(down_parts)
    grads, head_sums, head_half, head_keep, vectors, other_vectors = attend_back(
        q, k, v, probs, mixed, grad_mixed, flat_in, first_sums, second_sums, up_sums
    )
    if fast:
        up_parts, down_parts, grads, head_half, other_vectors = lax.optimization_barrier(
            (up_parts, down_parts, grads, head_half, other_vectors)
        )
    if fast:
        got = swap(head_half, "tower", 1)
        got_vectors = swap(other_vectors, "tower", 1)
        down_parts = cut_near(0, down_parts)
        up_parts = cross(up_parts)
        up_parts, down_parts, got = lax.optimization_barrier((up_parts, down_parts, got))
        up_parts = second_exchange(up_parts)
        down_parts = near_exchange(down_parts)
        parts = head_grad(head_keep, vectors, got_vectors, got)
        up_parts, down_parts, parts, grads = lax.optimization_barrier(
            (up_parts, down_parts, parts, grads)
        )
        parts = first_exchange(parts)
        down_parts = far_exchange(mix(6, down_parts))
        up_parts = near_exchange(cut_near(1, up_parts))
        grad_input = input_grad(grad_branch, grads, query_weight, key_weight, value_weight)
        down_parts, up_parts, parts, grad_input = lax.optimization_barrier(
            (down_parts, up_parts, parts, grad_input)
        )
        parts = cross(parts)
        up_parts = mix(6, up_parts)
        down_part = join_outer(down_parts)
        down_part, up_parts, parts = lax.optimization_barrier((down_part, up_parts, parts))
        up_parts = far_exchange(up_parts)
        parts = second_exchange(parts)
        up_parts, parts = lax.optimization_barrier((up_parts, parts))
        parts = cut_halves(1, parts)
        up_parts, parts = lax.optimization_barrier((up_parts, parts))
        parts = exchange_outer(parts)
        up_part = join_outer(up_parts)
        down_far, up_far = swap(down_part, "tower", 2), swap(up_part, "tower", 2)
        up_far, down_far, parts = lax.optimization_barrier((up_far, down_far, parts))
        head_part = join_outer(parts)
        head_far = swap(head_part, "tower", 2)
        (total_down,) = spread("down", down_part, down_far, [(4 * share, width)])
        total_up, total_out = spread(
            "up", up_part, up_far, [(share, up_weight.shape[1]), (share, width)]
        )
        total_down, total_up, total_out, head_far = lax.optimization_barrier(
            (total_down, total_up, total_out, head_far)
        )
        total_query, total_key, total_value, *sums = spread(
            "head", head_part, head_far,
            [(share, width)] * 3 + [(share,)] * 8 + [(4 * share,)],
        )
    else:
        grad_input = input_grad(grad_branch, grads, query_weight, key_weight, value_weight)
        outer = dp_count // 2
        vectors = jnp.concatenate(
            [
                vec.reshape(dp_count, -1)
                for vec in (
                    head_sums[0],
                    head_sums[1],
                    first_sums[2],
                    second_sums[2],
                    first_sums[0],
                    first_sums[1],
                    second_sums[0],
                    second_sums[1],
                    up_sums,
                )
            ],
            axis=1,
        ).astype(bf16)

        def by_rows(grad):
            return grad.astype(bf16).reshape(outer, 2, share, 2, 2, width).transpose(3, 4, 1, 0, 2, 5)

        square = jnp.stack(
            [dot_cols(flat_in, grads[i]) for i in range(3)] + [dot_cols(mixed, grad_branch)], axis=1
        )
        vectors = vectors.reshape(outer, 2, 2, 2, -1).transpose(2, 3, 1, 0, 4)
        vectors = jnp.pad(vectors, ((0, 0),) * 4 + ((0, width - vectors.shape[-1]),))
        down = dot_cols(active, grad_second).astype(bf16)
        down = down.reshape(outer, 2, 2, 2, share, width).transpose(2, 3, 1, 0, 4, 5)
        total_down = sum_group(down).reshape(4 * share, width)
        total_up = sum_group(by_rows(dot_cols(low, grad_hidden))).reshape(4, share, width)
        total_up = total_up.transpose(1, 0, 2).reshape(share, 4 * width)
        last = jnp.concatenate([by_rows(square), vectors[:, :, :, :, None]], axis=4)
        last = sum_group(last).reshape(4, share + 1, width)
        total_query, total_key, total_value, total_out = [last[i, :share] for i in range(4)]
        short = last[:, share, : share * 3].reshape(-1)
        sums = [short[i * share : (i + 1) * share] for i in range(8)] + [short[8 * share :]]
    grad_input = grad_input.reshape(layer_input.shape)
    return (
        loss,
        grad_input,
        total_query,
        total_key,
        total_value,
        total_out,
        total_up,
        total_down,
        sums[0],
        sums[1],
        sums[2],
        sums[8],
        sums[3],
        *sums[4:8],
    )


def solution(mesh):
    in_specs = (P("tower", "dp", None, None), P("tower", "dp", None), P(None, "dp", None)) + (P(),) * 15
    out_specs = (P(), P("tower", "dp", None, None)) + (P("dp", None),) * 6 + (P("dp"),) * 9
    return jax.shard_map(shards, mesh=mesh, in_specs=in_specs, out_specs=out_specs, check_vma=False)
```
